32 devices in a mesh: section: 2 (over y), dp: 2 (over x), ctx: 8 (over z, core).
Axes of the slice: x: 2, y: 2, z: 4, core: 2. Of those that a mesh axis runs over, the one named last changes fastest.
Arguments:
- tokens: bfloat16 [2, 4, 1024, 768], P(None, 'dp', 'ctx'), may hold values from -6 to 6
- lengths: int32 [2, 4], P(None, 'dp'), may hold values from 32 to 1024, as said below
- norm_gains: float32 [2, 2, 768], P('section'), may hold values from 0.5 to 1.5
- norm_offsets: float32 [2, 2, 768], P('section'), may hold values from -1.5 to 1.5
- attn_query: bfloat16 [2, 768, 768], P('section'), may hold values from -0.21875 to 0.21875
- kv_proj: bfloat16 [768, 128], replicated, may hold values from -0.21875 to 0.21875
- attn_out: bfloat16 [2, 768, 768], P('section'), may hold values from -2 to 2
- ffn_in: bfloat16 [2, 768, 3072], P('section'), may hold values from -0.21875 to 0.21875
- ffn_out: bfloat16 [2, 3072, 768], P('section'), may hold values from -0.109375 to 0.109375
- cotangent: bfloat16 [2, 4, 1024, 768], P(None, 'dp', 'ctx'), may hold values from -6 to 6
Outputs:
- layer_outputs: bfloat16 [2, 2, 4, 1024, 768], P('section', None, 'dp', 'ctx')
- input_grads: float32 [2, 2, 4, 1024, 768], P('section', None, 'dp', 'ctx')
- grad_norms: float32 [2, 768, 4], P('section', ('dp', 'ctx'))
- grad_query: float32 [2, 768, 768], P('section', ('dp', 'ctx'))
- grad_kv: float32 [768, 128], P(('section', 'dp', 'ctx'))
- grad_out: float32 [2, 768, 768], P('section', ('dp', 'ctx'))
- grad_ffn_in: float32 [2, 768, 3072], P('section', ('dp', 'ctx'))
- grad_ffn_out: float32 [2, 3072, 768], P('section', ('dp', 'ctx'))
The draws below stay inside these ranges and needn't reach their ends.
Inputs may be any that keep to these rules, and one draw needn't show every extreme that they name: `lengths`: real tokens of each sequence, the rest padding; in each micro-batch one of the 2 sequences of every index of dp has all 1024.
All inputs are finite; a program needn't handle non-finite values.
Results may differ from the reference program's by a relative error of at most 0.018.
Values may be sent and summed in bfloat16 or wider, within the bound.
No kernel may reach another device: no remote copies, remote signals or barrier semaphores. Data moves between devices by JAX's collectives and lax.ppermute only.
A program may use at most 256 MiB of HBM per device.

```python
from functools import partial
import jax
import jax.numpy as jnp
from jax import lax

D = 768
HEADS = 12
HEAD_DIM = 64
FF = 3072
ROT = 16
MB = 2
SEQ_MB = 2
LENGTH = 1024
SEQS = 4


def draw_lengths(key, part):
    key = jax.random.fold_in(key, 11)
    key_shift, key_extra, key_pick = jax.random.split(key, 3)
    shifts = jax.random.randint(key_shift, (MB, SEQS), 0, 5).astype(jnp.int32)
    base_len = jnp.right_shift(jnp.full((MB, SEQS), LENGTH, jnp.int32), shifts)
    half_len = base_len // 2
    extra_len = jax.random.randint(key_extra, (MB, SEQS), 0, 1 << 20).astype(jnp.int32) % (half_len + 1)
    groups = SEQS // SEQ_MB
    chosen = jax.random.randint(key_pick, (MB, groups), 0, SEQ_MB).astype(jnp.int32)
    places = jnp.arange(SEQS, dtype=jnp.int32)
    picked = chosen[:, places // SEQ_MB] == (places % SEQ_MB)[None, :]
    return jnp.where(picked, LENGTH, half_len + extra_len).astype(jnp.int32)


def level_of(rng, dims, cuts, low, high):
    loudness = 1.0
    for position, blocks in cuts:
        steps = jax.random.uniform(jax.random.fold_in(jax.random.fold_in(rng, 6), position), (blocks,), jnp.float32, low / len(cuts), high / len(cuts))
        loudness = loudness * jnp.repeat(jnp.exp(steps), dims[position] // blocks).reshape((-1,) + (1,) * (len(dims) - 1 - position))
    return loudness


def centred(stream_key, dims, width, reach, pieces=(), kind=jnp.bfloat16):
    result = jax.random.normal(stream_key, dims, jnp.float32) * width
    if len(pieces) > 0:
        result = level_of(stream_key, dims, pieces, -0.22, 0.18) * result
    return jnp.clip(result, min=-reach, max=reach).astype(kind)


def setup_inputs(seed: int = 0) -> dict:
    splits = jax.random.split(jax.random.key(seed), 11)
    tokens = centred(splits[0], (MB, SEQS, LENGTH, D), 1.0, 6.0, ((1, 2), (2, 8)))
    lengths = draw_lengths(jax.random.fold_in(splits[10], 71), 0)
    norm_gains = jnp.clip(1.0 + 0.1 * jax.random.normal(splits[2], (2, 2, D), jnp.float32), 0.5, 1.5)
    norm_offsets = centred(splits[3], (2, 2, D), 0.3, 1.5, ((0, 2),), jnp.float32)
    attn_query = centred(splits[4], (2, D, D), D ** -0.5, 0.21875, ((0, 2),))
    kv_proj = centred(splits[5], (D, 2 * HEAD_DIM), D ** -0.5, 0.21875)
    attn_out = centred(splits[6], (2, D, D), 8 ** -0.5, 2.0, ((0, 2),))
    ffn_in = centred(splits[7], (2, D, FF), D ** -0.5, 0.21875, ((0, 2),))
    ffn_out = centred(splits[8], (2, FF, D), FF ** -0.5, 0.109375, ((0, 2),))
    cotangent = centred(splits[9], (MB, SEQS, LENGTH, D), 1.0, 6.0, ((1, 2), (2, 8)))
    return dict(tokens=tokens, lengths=lengths, norm_gains=norm_gains, norm_offsets=norm_offsets, attn_query=attn_query, kv_proj=kv_proj, attn_out=attn_out, ffn_in=ffn_in, ffn_out=ffn_out, cotangent=cotangent)


@jax.custom_vjp
def low(v):
    return lax.optimization_barrier(v.astype(jnp.bfloat16)).astype(jnp.float32)

@jax.custom_vjp
def low_back(v):
    return v

def low_keep(v):
    return (low(v), None)

def low_pass(kept, grad):
    return (grad,)

def back_keep(v):
    return (v, None)

def back_low(kept, grad):
    return (low(grad),)
low.defvjp(low_keep, low_pass)
low_back.defvjp(back_keep, back_low)

def layer_norm(values, scale_gain, offset):
    center = values - lax.optimization_barrier(jnp.mean(values, axis=-1, keepdims=True))
    spread = lax.optimization_barrier(jnp.mean(center * center, axis=-1, keepdims=True))
    return center * lax.rsqrt(spread + 1e-05) * scale_gain + offset

def rotary_tables(positions):
    half_rot = ROT // 2
    inverse = jnp.power(10000.0, -jnp.arange(half_rot, dtype=jnp.float32) * (2.0 / ROT))
    angles = positions.astype(jnp.float32)[:, None] * inverse[None, :]
    return (jnp.cos(angles)[:, None, :], jnp.sin(angles)[:, None, :])

def rotate(values, cosine, sine_table):
    half_rot = ROT // 2
    lower_half = values[..., :half_rot]
    upper_half = values[..., half_rot:ROT]
    return jnp.concatenate([lower_half * cosine - upper_half * sine_table, upper_half * cosine + lower_half * sine_table, values[..., ROT:]], axis=-1)

def block_apply(hidden, length, layer_weights, shared):
    norm_gain, offsets, w_query, w_out, w_in, w_back, w_keys = layer_weights
    cosine, sine_table = rotary_tables(jnp.arange(LENGTH))
    normed = low(layer_norm(hidden, norm_gain[0], offsets[0]))
    q_raw = low_back(jnp.dot(normed, w_query, precision=lax.Precision.HIGHEST))
    queries = low(rotate(q_raw.reshape(LENGTH, HEADS, HEAD_DIM), cosine, sine_table))
    if shared is None:
        kv_raw = low_back(jnp.dot(normed, w_keys, precision=lax.Precision.HIGHEST))
        key_part = rotate(kv_raw[:, None, :HEAD_DIM], cosine, sine_table)[:, 0]
        shared = low(jnp.concatenate([key_part, kv_raw[:, HEAD_DIM:]], axis=-1))
    scores = low_back(jnp.einsum('ihd,jd->hij', queries, shared[:, :HEAD_DIM], precision=lax.Precision.HIGHEST))
    places = jnp.arange(LENGTH)
    allowed = (places[None, :] <= places[:, None]) & (places[None, :] < length)
    logits = jnp.where(allowed[None], scores * HEAD_DIM ** (-0.5), -1000000000.0)
    weights_soft = low(jax.nn.softmax(logits, axis=-1))
    mixed_heads = jnp.einsum('hij,jd->ihd', weights_soft, shared[:, HEAD_DIM:], precision=lax.Precision.HIGHEST).reshape(LENGTH, D)
    mixed_heads = low(low_back(mixed_heads))
    attended = jnp.dot(mixed_heads, w_out, precision=lax.Precision.HIGHEST)
    second = low(layer_norm(hidden, norm_gain[1], offsets[1]))
    upper_proj = low_back(jnp.dot(second, w_in, precision=lax.Precision.HIGHEST))
    activated = low(jax.nn.gelu(upper_proj, approximate=False))
    return (hidden + attended + jnp.dot(activated, w_back, precision=lax.Precision.HIGHEST), shared)

def one_sequence(params, seq_item):
    tokens_row, shift_row, length = seq_item
    norm_gain, offsets, w_query, w_keys, w_out, w_in, w_back = params
    first_w = (norm_gain[0], offsets[0], w_query[0], w_out[0], w_in[0], w_back[0], w_keys)
    out_first, shared = block_apply(tokens_row, length, first_w, None)
    passed = low(low_back(out_first)) + shift_row
    second_w = (norm_gain[1], offsets[1], w_query[1], w_out[1], w_in[1], w_back[1], w_keys)
    out_second, ignored = block_apply(passed, length, second_w, shared)
    return (out_first, out_second)

def reference(tokens, lengths, norm_gains, norm_offsets, attn_query, kv_proj, attn_out, ffn_in, ffn_out, cotangent):
    seq_total = MB * SEQS
    inputs = tokens.astype(jnp.float32).reshape(seq_total, LENGTH, D)
    shifts = jnp.zeros_like(inputs)
    flat_lengths = lengths.reshape(seq_total)
    params = (norm_gains.astype(jnp.float32), norm_offsets.astype(jnp.float32), attn_query.astype(jnp.float32), kv_proj.astype(jnp.float32), attn_out.astype(jnp.float32), ffn_in.astype(jnp.float32), ffn_out.astype(jnp.float32))

    def forward(params, inputs, shifts):
        seq_step = jax.checkpoint(partial(one_sequence, params))
        return lax.map(seq_step, (inputs, shifts, flat_lengths))
    outputs, pullback = jax.vjp(forward, params, inputs, shifts)
    cot_flat = cotangent.astype(jnp.float32).reshape(seq_total, LENGTH, D)
    grad_params, grad_inputs, grad_shifts = pullback((jnp.zeros_like(outputs[0]), cot_flat))
    gains_grad, offsets_grad, query_grad, keys_grad, out_grad, in_grad, back_grad = grad_params
    layer_outputs = jnp.stack([outputs[0], outputs[1]]).reshape(2, MB, SEQS, LENGTH, D).astype(jnp.bfloat16)
    input_grads = jnp.stack([grad_inputs, grad_shifts]).reshape(2, MB, SEQS, LENGTH, D)
    grad_norms = jnp.stack([gains_grad[:, 0], offsets_grad[:, 0], gains_grad[:, 1], offsets_grad[:, 1]], axis=-1)
    return (layer_outputs, input_grads, grad_norms, query_grad, keys_grad, out_grad, in_grad, back_grad)
```

```python
from functools import partial

import jax
import jax.numpy as jnp
import numpy as np
from jax import lax
from jax.experimental import pallas as pl
from jax.experimental.pallas import tpu as pltpu
from jax.sharding import PartitionSpec as P

HEADS = 12
HEAD_DIM = 64
ROT = 16
PAIR = 2 * HEAD_DIM
PAIRS = HEADS // 2
LOG2E = 1.4426950408889634
SCALE = HEAD_DIM**-0.5
MASKED = -8e9
F32 = jnp.float32
BF16 = jnp.bfloat16
VMEM_LIMIT = 56 * 1024 * 1024

PASS_A = (0, 0)
PASS_B = (1, 0)
PASS_C = (1, -1)
PASS_D = (0, 1)


def dot(left, right):
    return jnp.dot(left, right, preferred_element_type=F32)


def dot_nt(left, right, **kwargs):
    return lax.dot_general(left, right, (((1,), (1,)), ((), ())), preferred_element_type=F32, **kwargs)


def dot_tn(left, right):
    return lax.dot_general(left, right, (((0,), (0,)), ((), ())), preferred_element_type=F32)


def whole(shape):
    zeros = (0,) * len(shape)
    return pl.BlockSpec(shape, lambda *_: zeros)


def call(body, grid, in_specs, out_specs, out_shape, scratch=(), flops=0, moved=0):
    return pl.pallas_call(
        body,
        grid_spec=pltpu.PrefetchScalarGridSpec(
            num_scalar_prefetch=1,
            grid=grid,
            in_specs=in_specs,
            out_specs=out_specs,
            scratch_shapes=list(scratch),
        ),
        out_shape=out_shape,
        compiler_params=pltpu.CompilerParams(vmem_limit_bytes=VMEM_LIMIT),
        cost_estimate=pl.CostEstimate(flops=flops, bytes_accessed=moved, transcendentals=0),
    )


def rotary_table(length):
    half = ROT // 2
    inverse = 10000.0 ** (-np.arange(half) * (2.0 / ROT))
    angles = np.arange(length)[:, None] * inverse[None, :]
    cosine, sine = np.cos(angles), np.sin(angles)
    table = np.zeros((length, 3, 2, HEAD_DIM), np.float32)
    table[:, 0] = 1.0
    table[:, 0, :, :half] = cosine[:, None]
    table[:, 0, :, half:ROT] = cosine[:, None]
    table[:, 1, :, :half] = -sine[:, None]
    table[:, 2, :, half:ROT] = sine[:, None]
    return table.reshape(length, 3 * PAIR)


def rotate(values, table, sign=1.0):
    around = pltpu.roll(values, PAIR - ROT // 2, 1) * table[:, PAIR : 2 * PAIR]
    around = around + pltpu.roll(values, ROT // 2, 1) * table[:, 2 * PAIR :]
    return values * table[:, :PAIR] + (around if sign > 0 else -around)


def rotate_keys(values, table, sign=1.0):
    lane = lax.broadcasted_iota(jnp.int32, values.shape, 1)
    return jnp.where(lane < HEAD_DIM, rotate(values, table, sign), values)


def standardize(values):
    center = values - jnp.mean(values, axis=-1, keepdims=True)
    scale = lax.rsqrt(jnp.mean(center * center, axis=-1, keepdims=True) + 1e-05)
    return center * scale, scale


def norm_back(grads, gain, normed, scale):
    inner = grads * gain
    lean = jnp.mean(inner, axis=-1, keepdims=True)
    along = jnp.mean(inner * normed, axis=-1, keepdims=True)
    return scale * (inner - lean - normed * along)


def gelu_parts(values):
    size = jnp.abs(values) * 0.7071067811865476
    base = 1.0 + 0.3275911 * size
    turn = pl.reciprocal(base, approx=True)
    turn = turn * (2.0 - base * turn)
    bell = jnp.exp2(values * values * (-0.5 * LOG2E))
    tail = turn * (
        0.127414796 + turn * (-0.142248368 + turn * (0.7107068705 + turn * (-0.7265760135 + turn * 0.5307027145)))
    )
    tail = tail * bell
    share = jnp.where(values >= 0.0, 1.0 - tail, tail)
    return values * share, share + values * (bell * 0.3989422804014327)


def keys_body(meta, tokens, gains, offsets, w_keys, table, shared):
    normed, _ = standardize(tokens[0].reshape(-1, tokens.shape[-1]).astype(F32))
    normed = (normed * gains[0, 0:1] + offsets[0, 0:1]).astype(BF16)
    raw = dot(normed, w_keys[...])
    span = table.shape[0]
    for seq in range(raw.shape[0] // span):
        shared[0, seq] = rotate_keys(raw[seq * span : (seq + 1) * span], table[...]).astype(BF16)


def make_keys(meta, tokens, gains, offsets, w_keys, table):
    batches, seqs, span, width = tokens.shape
    return call(
        keys_body,
        (batches,),
        [
            pl.BlockSpec((1, seqs, span, width), lambda b, meta: (b, 0, 0, 0)),
            whole(gains.shape),
            whole(offsets.shape),
            whole(w_keys.shape),
            pl.BlockSpec((span, 3 * PAIR), lambda b, meta: (meta[0], 0)),
        ],
        pl.BlockSpec((1, seqs, span, PAIR), lambda b, meta: (b, 0, 0, 0)),
        jax.ShapeDtypeStruct((batches, seqs, span, PAIR), BF16),
    )(meta, tokens, gains, offsets, w_keys, table)


def front_body(save, meta, hidden, gains, offsets, w_query, table, w_in, w_back, *rest):
    if save:
        queries, result, normed, second, active, slope, second_sc = rest
    else:
        queries, result, second_sc = rest
    step = pl.program_id(0)

    @pl.when(step == 0)
    def _():
        values = hidden[...].astype(F32)
        unit, _ = standardize(values)
        first = (unit * gains[0, 0:1] + offsets[0, 0:1]).astype(BF16)
        second_sc[...] = (unit * gains[0, 1:2] + offsets[0, 1:2]).astype(BF16)
        if save:
            normed[...] = first
            second[...] = second_sc[...]
        raw = dot(first, w_query[0])
        span = table.shape[0]
        for seq in range(raw.shape[0] // span):
            rows = pl.ds(seq * span, span)
            for pair in range(PAIRS):
                lanes = slice(pair * PAIR, (pair + 1) * PAIR)
                queries[rows, lanes] = rotate(raw[seq * span : (seq + 1) * span, lanes], table[...]).astype(BF16)
        result[...] = values

    upper = dot(second_sc[...], w_in[0])
    value, rate = gelu_parts(upper)
    value = value.astype(BF16)
    if save:
        active[...] = value
        slope[...] = rate.astype(BF16)
    result[...] += dot(value, w_back[0])


def front(save, meta, hidden, gains, offsets, w_query, table, w_in, w_back):
    rows, width = hidden.shape
    inner = w_in.shape[2]
    block = min(512, inner)
    span = rows // 2
    out_specs = [whole((rows, width)), whole((rows, width))]
    out_shape = [jax.ShapeDtypeStruct((rows, width), BF16), jax.ShapeDtypeStruct((rows, width), F32)]
    if save:
        out_specs += [whole((rows, width)), whole((rows, width))]
        out_specs += [pl.BlockSpec((rows, block), lambda j, meta: (0, j))] * 2
        out_shape += [jax.ShapeDtypeStruct((rows, width), BF16)] * 2
        out_shape += [jax.ShapeDtypeStruct((rows, inner), BF16)] * 2
    return call(
        partial(front_body, save),
        (inner // block,),
        [
            whole((rows, width)),
            whole(gains.shape),
            whole(offsets.shape),
            whole(w_query.shape),
            pl.BlockSpec((span, 3 * PAIR), lambda j, meta: (meta[0], 0)),
            pl.BlockSpec((1, width, block), lambda j, meta: (0, 0, j)),
            pl.BlockSpec((1, block, width), lambda j, meta: (0, j, 0)),
        ],
        out_specs,
        out_shape,
        [pltpu.VMEM((rows, width), BF16)],
        flops=2 * rows * width * (width + 2 * inner),
        moved=2 * width * (width + 2 * inner) + 4 * rows * inner,
    )(meta, hidden, gains, offsets, w_query, table, w_in, w_back)


def stack_pair(values, first_half):
    span = values.shape[0]
    lane = lax.broadcasted_iota(jnp.int32, (span, PAIR), 1)
    here = lane < HEAD_DIM if first_half else lane >= HEAD_DIM
    turned = pltpu.roll(values.astype(F32), HEAD_DIM, 1).astype(BF16)
    low, high = (values, turned) if first_half else (turned, values)
    zero = jnp.zeros_like(values)
    return jnp.concatenate([jnp.where(here, low, zero), jnp.where(here, high, zero)], axis=0)


def unstack_pair(values):
    span = values.shape[1] // 2
    return jnp.concatenate([values[:, :span], values[:, span:]], axis=0).T


def allowed_keys(meta, length, span, seq_length):
    key = lax.broadcasted_iota(jnp.int32, (length, 2 * span), 0)
    query = lax.broadcasted_iota(jnp.int32, (1, 2 * span), 1)
    query = jnp.where(query >= span, query - span, query) + meta[0] * span
    return key <= jnp.minimum(query, seq_length - 1)


def attend_body(which, meta, queries, shared, w_out, base, mixed, norms, result):
    seq = pl.program_id(0)
    batch = which[0] + which[1] * meta[2]
    span = queries.shape[0]
    pairs = shared[...].reshape(-1, PAIR)
    length = pairs.shape[0]
    turned = pairs.T
    row = lax.broadcasted_iota(jnp.int32, turned.shape, 0)
    turned = jnp.where(row < HEAD_DIM, jnp.ones_like(turned), turned)
    seq_length = meta[4 + 2 * batch + seq]
    allowed = allowed_keys(meta, length, span, seq_length)
    for pair in range(PAIRS):
        lanes = slice(pair * PAIR, (pair + 1) * PAIR)
        stacked = stack_pair(queries[:, lanes], True)
        scores = jnp.where(allowed, dot_nt(pairs, stacked), MASKED)
        top = jnp.max(scores, axis=0, keepdims=True)
        weights = jnp.exp2((scores - top) * (SCALE * LOG2E)).astype(BF16)
        summed = dot(turned, weights)
        total = summed[0:1]
        mixed[:, lanes] = unstack_pair(summed[HEAD_DIM:] * (1.0 / total)).astype(BF16)
        norms[0, :, pair * 2 * span : (pair + 1) * 2 * span] = top * (SCALE * LOG2E) + jnp.log2(total)
    result[...] = (base[...] + dot(mixed[...], w_out[0])).astype(BF16)


def attend(which, meta, queries, gathered, w_out, base):
    rows, width = queries.shape
    count, _, seqs, span, _ = gathered.shape
    return call(
        partial(attend_body, which),
        (seqs,),
        [
            pl.BlockSpec((span, width), lambda s, meta: (s, 0)),
            pl.BlockSpec((count, 1, 1, span, PAIR), lambda s, meta: (0, which[0] + which[1] * meta[2], s, 0, 0)),
            whole(w_out.shape),
            pl.BlockSpec((span, width), lambda s, meta: (s, 0)),
        ],
        [
            pl.BlockSpec((span, width), lambda s, meta: (s, 0)),
            pl.BlockSpec((1, 1, HEADS * span), lambda s, meta: (s, 0, 0)),
            pl.BlockSpec((span, width), lambda s, meta: (s, 0)),
        ],
        [
            jax.ShapeDtypeStruct((rows, width), BF16),
            jax.ShapeDtypeStruct((seqs, 1, HEADS * span), F32),
            jax.ShapeDtypeStruct((rows, width), BF16),
        ],
        flops=4 * rows * count * span * width + 2 * rows * width * width,
        moved=2 * width * width + 8 * rows * width,
    )(meta, queries, gathered, w_out, base)


def attend_back_body(
    which, meta, upstream, queries, mixed, norms, shared, w_out, w_query, table, d_raw, d_shared, d_normed, d_mixed_sc
):
    seq = pl.program_id(0)
    batch = which[0] + which[1] * meta[2]
    span = table.shape[0]

    @pl.when(seq == 0)
    def _():
        d_mixed_sc[...] = dot_nt(upstream[...], w_out[0]).astype(BF16)

    rows = pl.ds(pl.multiple_of(seq * span, span), span)
    pairs = shared[...].reshape(-1, PAIR)
    length = pairs.shape[0]
    turned = pairs.T
    allowed = allowed_keys(meta, length, span, meta[4 + 2 * batch + seq])
    head_of = lax.broadcasted_iota(jnp.int32, (8, PAIR), 1) // HEAD_DIM
    pick = (head_of == lax.broadcasted_iota(jnp.int32, (8, PAIR), 0)).astype(F32)
    total = jnp.zeros((length, PAIR), F32)
    for pair in range(PAIRS):
        lanes = slice(pair * PAIR, (pair + 1) * PAIR)
        d_mixed = d_mixed_sc[rows, lanes]
        lean = dot_nt(pick, d_mixed.astype(F32) * mixed[rows, lanes].astype(F32), precision=lax.Precision.HIGHEST)
        lean = jnp.concatenate([lean[0:1], lean[1:2]], axis=1)
        q_stack = stack_pair(queries[rows, lanes], True)
        d_stack = stack_pair(d_mixed, False)
        scores = dot_nt(pairs, q_stack)
        norm = norms[seq, :, pair * 2 * span : (pair + 1) * 2 * span]
        weights = jnp.where(allowed, jnp.exp2(scores * (SCALE * LOG2E) - norm), 0.0)
        d_weights = dot_nt(pairs, d_stack)
        d_scores = (weights * (d_weights - lean)).astype(BF16)
        total += dot(
            jnp.concatenate([d_scores, weights.astype(BF16)], axis=1),
            jnp.concatenate([(q_stack.astype(F32) * SCALE).astype(BF16), d_stack], axis=0),
        )
        d_query = unstack_pair(dot(turned, d_scores)[:HEAD_DIM]) * SCALE
        d_raw[rows, lanes] = rotate(d_query, table[...], -1.0).astype(BF16)
    d_shared[...] = total.astype(BF16).reshape(d_shared.shape)

    @pl.when(seq == pl.num_programs(0) - 1)
    def _():
        d_normed[...] = dot_nt(d_raw[...], w_query[0])


def attend_back(which, meta, upstream, queries, mixed, norms, gathered, w_out, w_query, table):
    rows, width = queries.shape
    count, _, seqs, span, _ = gathered.shape
    return call(
        partial(attend_back_body, which),
        (seqs,),
        [
            whole((rows, width)),
            whole((rows, width)),
            whole((rows, width)),
            whole(norms.shape),
            pl.BlockSpec((count, 1, 1, span, PAIR), lambda s, meta: (0, which[0] + which[1] * meta[2], s, 0, 0)),
            whole(w_out.shape),
            whole(w_query.shape),
            pl.BlockSpec((span, 3 * PAIR), lambda s, meta: (meta[0], 0)),
        ],
        [
            whole((rows, width)),
            pl.BlockSpec((count, 1, span, PAIR), lambda s, meta: (0, s, 0, 0)),
            whole((rows, width)),
        ],
        [
            jax.ShapeDtypeStruct((rows, width), BF16),
            jax.ShapeDtypeStruct((count, seqs, span, PAIR), BF16),
            jax.ShapeDtypeStruct((rows, width), F32),
        ],
        [pltpu.VMEM((rows, width), BF16)],
        flops=10 * rows * count * span * width + 4 * rows * width * width,
        moved=4 * width * width + 8 * rows * width,
    )(meta, upstream, queries, mixed, norms, gathered, w_out, w_query, table)


def feed_back_body(
    meta, upstream, slope, w_in, w_back, hidden, gains, d_normed, d_upper, d_hidden, d_low, d_norms, d_second
):
    step = pl.program_id(0)
    rate = (dot_nt(upstream[...], w_back[0]) * slope[...].astype(F32)).astype(BF16)
    d_upper[...] = rate
    part = dot_nt(rate, w_in[0])

    @pl.when(step == 0)
    def _():
        d_second[...] = part

    @pl.when(step > 0)
    def _():
        d_second[...] += part

    @pl.when(step == pl.num_programs(0) - 1)
    def _():
        unit, scale = standardize(hidden[...].astype(F32))
        one, two = d_normed[...], d_second[...]
        total = upstream[...].astype(F32) + norm_back(
            one * gains[0, 0:1] + two * gains[0, 1:2], 1.0, unit, scale
        )
        d_hidden[...] = total
        d_low[...] = total.astype(BF16)
        d_norms[0:1] = jnp.sum(one * unit, axis=0, keepdims=True)
        d_norms[1:2] = jnp.sum(one, axis=0, keepdims=True)
        d_norms[2:3] = jnp.sum(two * unit, axis=0, keepdims=True)
        d_norms[3:4] = jnp.sum(two, axis=0, keepdims=True)
        d_norms[4:8] = jnp.zeros((4, unit.shape[1]), F32)


def feed_back(meta, upstream, slope, w_in, w_back, hidden, gains, d_normed):
    rows, width = upstream.shape
    inner = w_in.shape[2]
    block = min(512, inner)
    return call(
        feed_back_body,
        (inner // block,),
        [
            whole((rows, width)),
            pl.BlockSpec((rows, block), lambda j, meta: (0, j)),
            pl.BlockSpec((1, width, block), lambda j, meta: (0, 0, j)),
            pl.BlockSpec((1, block, width), lambda j, meta: (0, j, 0)),
            whole((rows, width)),
            whole(gains.shape),
            whole((rows, width)),
        ],
        [
            pl.BlockSpec((rows, block), lambda j, meta: (0, j)),
            whole((rows, width)),
            whole((rows, width)),
            whole((8, width)),
        ],
        [
            jax.ShapeDtypeStruct((rows, inner), BF16),
            jax.ShapeDtypeStruct((rows, width), F32),
            jax.ShapeDtypeStruct((rows, width), BF16),
            jax.ShapeDtypeStruct((8, width), F32),
        ],
        [pltpu.VMEM((rows, width), F32)],
        flops=4 * rows * width * inner,
        moved=4 * width * inner + 4 * rows * inner + 12 * rows * width,
    )(meta, upstream, slope, w_in, w_back, hidden, gains, d_normed)


def store_halves(meta, block, keep, send, scratch):
    groups, _, part, lanes = scratch.shape
    scratch[...] = block.astype(BF16).reshape(groups, 2, part, lanes)
    core = meta[1]
    keep[...] = scratch[:, pl.ds(core, 1)].reshape(keep.shape)
    send[...] = scratch[:, pl.ds(1 - core, 1)].reshape(send.shape)


def weights_tall_body(meta, left_c, left_d, right_c, right_d, keep, send, scratch):
    block = dot_tn(left_c[...], right_c[...]) + dot_tn(left_d[...], right_d[...])
    store_halves(meta, block, keep, send, scratch)


def weights_tall(meta, shards, left_c, left_d, right_c, right_d):
    rows, tall = left_c.shape
    width = right_c.shape[1]
    part = tall // shards
    if part % 64:
        return weights_full(meta, shards, left_c, left_d, right_c, right_d)
    spec = pl.BlockSpec((1, part, width), lambda j, meta: (j, 0, 0))
    shape = jax.ShapeDtypeStruct((shards // 2, part, width), BF16)
    return call(
        weights_tall_body,
        (shards // 2,),
        [pl.BlockSpec((rows, 2 * part), lambda j, meta: (0, j))] * 2 + [whole((rows, width))] * 2,
        [spec, spec],
        [shape, shape],
        [pltpu.VMEM((1, 2, part, width), BF16)],
        flops=4 * rows * tall * width,
        moved=4 * rows * (tall + width) + 2 * tall * width,
    )(meta, left_c, left_d, right_c, right_d)


def weights_full_body(meta, left_c, left_d, right_c, right_d, full, turned_c, turned_d):
    @pl.when(pl.program_id(0) == 0)
    def _():
        turned_c[...] = left_c[...].T
        turned_d[...] = left_d[...].T

    block = dot(turned_c[...], right_c[...]) + dot(turned_d[...], right_d[...])
    full[...] = block.astype(BF16)


def weights_full(meta, shards, left_c, left_d, right_c, right_d):
    rows, tall = left_c.shape
    wide = right_c.shape[1]
    block = 256
    full = call(
        weights_full_body,
        (wide // block,),
        [whole((rows, tall))] * 2 + [pl.BlockSpec((rows, block), lambda j, meta: (0, j))] * 2,
        pl.BlockSpec((tall, block), lambda j, meta: (0, j)),
        jax.ShapeDtypeStruct((tall, wide), BF16),
        [pltpu.VMEM((tall, rows), BF16), pltpu.VMEM((tall, rows), BF16)],
        flops=4 * rows * tall * wide,
        moved=4 * rows * (tall + wide) + 2 * tall * wide,
    )(meta, left_c, left_d, right_c, right_d)
    return split_cores(full.reshape(shards, tall // shards, wide))


def weights_wide_body(meta, left_c, left_d, right_c, right_d, keep, send, scratch, turned_c, turned_d):
    @pl.when(pl.program_id(0) == 0)
    def _():
        turned_c[...] = left_c[...].T
        turned_d[...] = left_d[...].T

    block = dot(turned_c[...], right_c[...]) + dot(turned_d[...], right_d[...])
    store_halves(meta, block, keep, send, scratch)


def weights_wide(meta, shards, left_c, left_d, right_c, right_d):
    rows, tall = left_c.shape
    wide = right_c.shape[1]
    block = min(512, wide) if wide % 512 == 0 else 384
    part = tall // shards
    if part % 16:
        return weights_full(meta, shards, left_c, left_d, right_c, right_d)
    spec = pl.BlockSpec((shards // 2, part, block), lambda j, meta: (0, 0, j))
    shape = jax.ShapeDtypeStruct((shards // 2, part, wide), BF16)
    return call(
        weights_wide_body,
        (wide // block,),
        [whole((rows, tall))] * 2 + [pl.BlockSpec((rows, block), lambda j, meta: (0, j))] * 2,
        [spec, spec],
        [shape, shape],
        [
            pltpu.VMEM((shards // 2, 2, part, block), BF16),
            pltpu.VMEM((tall, rows), BF16),
            pltpu.VMEM((tall, rows), BF16),
        ],
        flops=4 * rows * tall * wide,
        moved=4 * rows * (tall + wide) + 2 * tall * wide,
    )(meta, left_c, left_d, right_c, right_d)


def tail_body(
    meta, own, other, hid_d, hid_c, nrm_d, nrm_c, dh_d, dh_c, sums_d, sums_c, gains, w_keys, table, grads, d_keys, d_norms
):
    section = meta[2]
    first = (section == 0).astype(F32)
    span = table.shape[0]
    seqs = own.shape[1]
    keys_sum = None
    norm_sum = sums_d[...] + sums_c[...]
    gain = gains[0, 0:1]
    for slot, (hidden, normed, d_hidden) in enumerate(((hid_d, nrm_d, dh_d), (hid_c, nrm_c, dh_c))):
        raw = []
        for seq in range(seqs):
            both = (own[slot, seq].astype(F32) + other[1 - slot, seq].astype(F32)) * first
            raw.append(rotate_keys(both, table[...], -1.0).astype(BF16))
        raw = jnp.concatenate(raw, axis=0)
        part = dot_tn(normed[...], raw)
        keys_sum = part if keys_sum is None else keys_sum + part
        d_normed = dot_nt(raw, w_keys[...])
        unit, scale = standardize(hidden[...].astype(F32))
        batch = section if slot == 0 else 1 - section
        grads[pl.ds(batch, 1)] = (d_hidden[...] + norm_back(d_normed, gain, unit, scale))[None]
        norm_sum += jnp.concatenate(
            [
                jnp.sum(d_normed * unit, axis=0, keepdims=True),
                jnp.sum(d_normed, axis=0, keepdims=True),
                jnp.zeros((6, unit.shape[1]), F32),
            ],
            axis=0,
        )
    d_keys[...] = keys_sum.astype(BF16)
    d_norms[...] = norm_sum


def tail(meta, *arrays):
    rows, width = arrays[2].shape
    span = arrays[0].shape[2]
    table = arrays[-1]
    return call(
        tail_body,
        (1,),
        [whole(array.shape) for array in arrays[:-1]]
        + [pl.BlockSpec((span, table.shape[1]), lambda j, meta: (meta[0], 0))],
        [whole((2, rows, width)), whole((width, PAIR)), whole((8, width))],
        [
            jax.ShapeDtypeStruct((2, rows, width), F32),
            jax.ShapeDtypeStruct((width, PAIR), BF16),
            jax.ShapeDtypeStruct((8, width), F32),
        ],
    )(meta, *arrays)


def swap(value, axis, bit):
    count = lax.axis_size(axis)
    return lax.ppermute(value, axis, [(source, source ^ bit) for source in range(count)])


def across(value, steps):
    pairs = [(0, 1)] if steps > 0 else [(1, 0)]
    return lax.ppermute(value, "section", pairs)


def halve(parts, axis, bit, place, received):
    mine = (lax.axis_index(axis) // bit) % 2
    if received is None:
        cut = [
            value.reshape(value.shape[:place] + (2, value.shape[place] // 2) + value.shape[place + 1 :])
            for value in parts
        ]
        if place == 1:
            pass
        other = sum(lax.dynamic_index_in_dim(value, 1 - mine, place, keepdims=False).astype(F32) for value in cut)
        keep = [lax.dynamic_index_in_dim(value, mine, place, keepdims=False) for value in cut]
        return keep + [swap(other.astype(BF16), axis, bit)]
    return parts + [received]


def finish_scatter(keep, send):
    groups, depth = lax.axis_size("dp"), lax.axis_size("ctx") // 2
    parts = [keep, swap(send, "ctx", 1)]
    bit = groups // 2
    while bit >= 1:
        parts = halve(parts, "dp", bit, 0, None)
        bit //= 2
    bit = 2
    while depth > 1:
        parts = [value.reshape((depth // 2, 2) + value.shape[1:]) for value in parts]
        mine = (lax.axis_index("ctx") // bit) % 2
        other = sum(lax.dynamic_index_in_dim(value, 1 - mine, 1, keepdims=False).astype(F32) for value in parts)
        parts = [lax.dynamic_index_in_dim(value, mine, 1, keepdims=False) for value in parts]
        parts.append(swap(other.astype(BF16), "ctx", bit))
        depth //= 2
        bit *= 2
    return sum(value.astype(F32) for value in parts).reshape(keep.shape[1:])


def split_cores(value):
    shards, part, lanes = value.shape
    cut = value.reshape(shards // 2, 2, part, lanes)
    core = lax.axis_index("ctx") % 2
    return (
        lax.dynamic_index_in_dim(cut, core, 1, keepdims=False),
        lax.dynamic_index_in_dim(cut, 1 - core, 1, keepdims=False),
    )


def scatter_keys(value):
    parts, depth, bit = [value], value.shape[0], 1
    while depth > 1:
        parts = [v.reshape((depth // 2, 2) + v.shape[1:]) for v in parts]
        mine = (lax.axis_index("ctx") // bit) % 2
        other = sum(lax.dynamic_index_in_dim(v, 1 - mine, 1, keepdims=False).astype(F32) for v in parts)
        parts = [lax.dynamic_index_in_dim(v, mine, 1, keepdims=False) for v in parts]
        parts.append(swap(other.astype(BF16), "ctx", bit))
        depth //= 2
        bit *= 2
    return sum(v.astype(F32) for v in parts).astype(BF16)[0]


def per_device(
    length, tokens, lengths, norm_gains, norm_offsets, w_query, w_keys, w_out, w_in, w_back, cotangent
):
    batches, seqs, span, width = tokens.shape
    rows = seqs * span
    shards = lax.axis_size("dp") * lax.axis_size("ctx")
    section = lax.axis_index("section")
    place = lax.axis_index("ctx")
    first = section == 0
    meta = jnp.concatenate(
        [jnp.stack([place, place % 2, section, section]).astype(jnp.int32), lengths.reshape(-1)]
    )
    table = jnp.asarray(rotary_table(length))

    own = make_keys(meta, tokens, norm_gains, norm_offsets, w_keys, table)
    shared = jnp.where(first, own, across(own, 1))
    gathered = lax.all_gather(shared, "ctx")

    def forward(which, hidden, save):
        queries, base, *kept = front(
            save, meta, hidden, norm_gains, norm_offsets, w_query, table, w_in, w_back
        )
        mixed, norms, result = attend(which, meta, queries, gathered, w_out, base)
        return result, (hidden, queries, mixed, norms, *kept)

    def backward(which, saved, upstream):
        hidden, queries, mixed, norms, normed, second, active, slope = saved
        d_raw, d_shared, d_normed = attend_back(
            which, meta, upstream, queries, mixed, norms, gathered, w_out, w_query, table
        )
        d_upper, d_hidden, d_low, d_norms = feed_back(
            meta, upstream, slope, w_in, w_back, hidden, norm_gains, d_normed
        )
        return d_low, d_hidden, d_norms, d_raw, d_upper, d_shared

    flat = tokens.reshape(batches, rows, width)
    cot = cotangent.reshape(batches, rows, width)
    out_a, _ = forward(PASS_A, flat[0], False)
    came_a = across(out_a, 1)
    out_b, _ = forward(PASS_B, flat[1], False)
    came_b = across(out_b, 1)
    out_c, saved_c = forward(PASS_C, jnp.where(first, flat[1], came_a), True)
    low_one, *_ = backward(PASS_C, saved_c, cot[0])
    back_d = across(low_one, -1)
    out_d, saved_d = forward(PASS_D, jnp.where(first, flat[0], came_b), True)
    up_d = jnp.where(first, back_d, cot[1])
    low_d, dh_d, sums_d, raw_d, upper_d, ds_d = backward(PASS_D, saved_d, up_d)
    back_c = across(low_d, -1)
    up_c = jnp.where(first, back_c, cot[0])

    hid_c, _, mixed_c, _, normed_c, second_c, active_c, _ = saved_c
    hid_d, _, mixed_d, _, normed_d, second_d, active_d, _ = saved_d
    grad_back = finish_scatter(*weights_tall(meta, shards, active_c, active_d, up_c, up_d))
    grad_out = finish_scatter(*weights_wide(meta, shards, mixed_c, mixed_d, up_c, up_d))
    low_c, dh_c, sums_c, raw_c, upper_c, ds_c = backward(PASS_C, saved_c, up_c)
    grad_in = finish_scatter(*weights_wide(meta, shards, second_c, second_d, upper_c, upper_d))
    grad_query = finish_scatter(*weights_wide(meta, shards, normed_c, normed_d, raw_c, raw_d))

    own_keys = scatter_keys(jnp.stack([ds_d, ds_c], axis=1))
    other_keys = across(own_keys, -1)
    input_grads, d_keys, d_norms = tail(
        meta, own_keys, other_keys, hid_d, hid_c, normed_d, normed_c, dh_d, dh_c, sums_d, sums_c, norm_gains, w_keys, table
    )
    sections = lax.axis_size("section")
    share = width // (sections * shards)
    d_keys = d_keys.reshape(sections, shards, share, PAIR).transpose(1, 0, 2, 3).reshape(shards, sections * share, PAIR)
    d_norms = d_norms.T.reshape(shards, width // shards, 8)
    d_norms = jnp.pad(d_norms, ((0, 0), (0, 0), (0, PAIR - 8))).astype(BF16)
    small = finish_scatter(*split_cores(jnp.concatenate([d_keys, d_norms], axis=-1)))
    grad_norms = small[:, PAIR : PAIR + 4]
    keys_both = small[:, :PAIR].reshape(sections, share, PAIR)
    grad_keys = jnp.where(first, keys_both[0], across(keys_both[1], 1))
    outs = jnp.where(first, jnp.stack([out_d, out_c]), jnp.stack([out_c, out_d]))
    return (
        outs.reshape((1,) + tokens.shape),
        input_grads.reshape((1,) + tokens.shape),
        grad_norms[None],
        grad_query[None],
        grad_keys,
        grad_out[None],
        grad_in[None],
        grad_back[None],
    )


def solution(mesh):
    def run(*arrays):
        length = arrays[0].shape[2]
        return jax.shard_map(
            partial(per_device, length),
            mesh=mesh,
            in_specs=(
                P(None, "dp", "ctx", None),
                P(None, "dp"),
                P("section", None, None),
                P("section", None, None),
                P("section", None, None),
                P(),
                P("section", None, None),
                P("section", None, None),
                P("section", None, None),
                P(None, "dp", "ctx", None),
            ),
            out_specs=(
                P("section", None, "dp", "ctx", None),
                P("section", None, "dp", "ctx", None),
                P("section", ("dp", "ctx"), None),
                P("section", ("dp", "ctx"), None),
                P(("section", "dp", "ctx"), None),
                P("section", ("dp", "ctx"), None),
                P("section", ("dp", "ctx"), None),
                P("section", ("dp", "ctx"), None),
            ),
            check_vma=False,
        )(*arrays)

    return run
```

```python
from functools import partial

import jax
import jax.numpy as jnp
import numpy as np
from jax import lax
from jax.experimental import pallas as pl
from jax.experimental.pallas import tpu as pltpu
from jax.sharding import PartitionSpec as P

HEADS = 12
HEAD_DIM = 64
ROT = 16
PAIR = 2 * HEAD_DIM
PAIRS = HEADS // 2
LOG2E = 1.4426950408889634
SCALE = HEAD_DIM**-0.5
MASKED = -1e30
F32 = jnp.float32
BF16 = jnp.bfloat16
VMEM_LIMIT = 60 * 1024 * 1024
FLOPS = 1_000_000

PASS_C = (1, -1)
PASS_D = (0, 1)


def dot(left, right):
    return jnp.dot(left, right, preferred_element_type=F32)


def dot_nt(left, right, **kwargs):
    return lax.dot_general(left, right, (((1,), (1,)), ((), ())), preferred_element_type=F32, **kwargs)


def dot_tn(left, right):
    return lax.dot_general(left, right, (((0,), (0,)), ((), ())), preferred_element_type=F32)


def whole(shape):
    zeros = (0,) * len(shape)
    return pl.BlockSpec(shape, lambda *_: zeros)


def call(body, grid, in_specs, out_specs, out_shape, scratch=()):
    return pl.pallas_call(
        body,
        grid_spec=pltpu.PrefetchScalarGridSpec(
            num_scalar_prefetch=1,
            grid=grid,
            in_specs=in_specs,
            out_specs=out_specs,
            scratch_shapes=list(scratch),
        ),
        out_shape=out_shape,
        compiler_params=pltpu.CompilerParams(vmem_limit_bytes=VMEM_LIMIT),
        cost_estimate=pl.CostEstimate(flops=FLOPS, bytes_accessed=0, transcendentals=0),
    )


IN_HBM = pl.BlockSpec(memory_space=pltpu.HBM)


def fetch(sems, *pairs):
    copies = [pltpu.make_async_copy(source, target, sems.at[n]) for n, (source, target) in enumerate(pairs)]
    for copy in copies:
        copy.start()
    return copies


def shape_of(rows, columns, dtype):
    return jax.ShapeDtypeStruct((rows, columns), dtype)


def rotary_table(length):
    half = ROT // 2
    inverse = 10000.0 ** (-np.arange(half) * (2.0 / ROT))
    angles = np.arange(length)[:, None] * inverse[None, :]
    cosine, sine = np.cos(angles), np.sin(angles)
    table = np.zeros((length, 3, 2, HEAD_DIM), np.float32)
    table[:, 0] = 1.0
    table[:, 0, :, :half] = cosine[:, None]
    table[:, 0, :, half:ROT] = cosine[:, None]
    table[:, 1, :, :half] = -sine[:, None]
    table[:, 2, :, half:ROT] = sine[:, None]
    return table.reshape(length, 3 * PAIR)


def rotate(values, table, sign=1.0):
    around = pltpu.roll(values, PAIR - ROT // 2, 1) * table[:, PAIR : 2 * PAIR]
    around = around + pltpu.roll(values, ROT // 2, 1) * table[:, 2 * PAIR :]
    return values * table[:, :PAIR] + (around if sign > 0 else -around)


def rotate_keys(values, table, sign=1.0):
    lane = lax.broadcasted_iota(jnp.int32, values.shape, 1)
    return jnp.where(lane < HEAD_DIM, rotate(values, table, sign), values)


def standardize(values):
    center = values - jnp.mean(values, axis=-1, keepdims=True)
    scale = lax.rsqrt(jnp.mean(center * center, axis=-1, keepdims=True) + 1e-05)
    return center * scale, scale


def norm_back(grads, gain, normed, scale):
    inner = grads * gain
    lean = jnp.mean(inner, axis=-1, keepdims=True)
    along = jnp.mean(inner * normed, axis=-1, keepdims=True)
    return scale * (inner - lean - normed * along)


def gelu_parts(values):
    size = jnp.abs(values) * 0.7071067811865476
    base = 1.0 + 0.3275911 * size
    turn = pl.reciprocal(base, approx=True)
    turn = turn * (2.0 - base * turn)
    bell = jnp.exp2(values * values * (-0.5 * LOG2E))
    tail = turn * (
        0.127414796 + turn * (-0.142248368 + turn * (0.7107068705 + turn * (-0.7265760135 + turn * 0.5307027145)))
    )
    tail = tail * bell
    share = jnp.where(values >= 0.0, 1.0 - tail, tail)
    return values * share, share + values * (bell * 0.3989422804014327)


def keys_body(tokens_h, gains_h, offsets_h, w_keys_h, table_h, shared, tokens, gains, offsets, w_keys, table, sems):
    span = table.shape[0]
    rows = pl.ds(pl.multiple_of(lax.axis_index("ctx") * span, span), span)
    copies = fetch(
        sems,
        (tokens_h, tokens),
        (gains_h, gains),
        (offsets_h, offsets),
        (w_keys_h, w_keys),
        (table_h.at[rows], table),
    )
    for copy in copies:
        copy.wait()
    batches, seqs, _, width = tokens.shape
    normed, _ = standardize(tokens[...].reshape(-1, width).astype(F32))
    normed = (normed * gains[0, 0:1] + offsets[0, 0:1]).astype(BF16)
    raw = dot(normed, w_keys[...])
    for batch in range(batches):
        for seq in range(seqs):
            start = (batch * seqs + seq) * span
            shared[batch, seq] = rotate_keys(raw[start : start + span], table[...]).astype(BF16)


def make_keys(tokens, gains, offsets, w_keys, table):
    batches, seqs, span, width = tokens.shape
    return pl.pallas_call(
        keys_body,
        in_specs=[IN_HBM] * 5,
        out_specs=pl.BlockSpec(memory_space=pltpu.VMEM),
        out_shape=jax.ShapeDtypeStruct((batches, seqs, span, PAIR), BF16),
        scratch_shapes=[
            pltpu.VMEM(tokens.shape, BF16),
            pltpu.VMEM(gains.shape, F32),
            pltpu.VMEM(offsets.shape, F32),
            pltpu.VMEM(w_keys.shape, BF16),
            pltpu.VMEM((span, table.shape[1]), F32),
            pltpu.SemaphoreType.DMA((5,)),
        ],
        compiler_params=pltpu.CompilerParams(vmem_limit_bytes=VMEM_LIMIT),
    )(tokens, gains, offsets, w_keys, table)


def make_queries(first, w_query, table, queries):
    raw = dot(first, w_query)
    span = table.shape[0]
    for start in range(0, raw.shape[0], span):
        for pair in range(PAIRS):
            lanes = slice(pair * PAIR, (pair + 1) * PAIR)
            queries[start : start + span, lanes] = rotate(raw[start : start + span, lanes], table[...]).astype(BF16)


def front_body(
    save, block, meta, hidden_h, gains_h, offsets_h, table_h, w_query_h, w_in_h, *rest
):
    if save:
        queries, normed, second, active, slope, hidden, gains, offsets, table, w_query, w_in, sems = rest
    else:
        w_back_h, queries, result, hidden, gains, offsets, table, w_query, w_in, w_back, sems = rest
    span = table.shape[0]
    inner = w_in.shape[1]
    rows = pl.ds(pl.multiple_of(meta[0] * span, span), span)
    pairs = [
        (hidden_h, hidden),
        (gains_h, gains),
        (offsets_h, offsets),
        (w_query_h.at[0], w_query),
        (table_h.at[rows], table),
    ]
    for start in range(0, inner, block):
        lanes = pl.ds(start, block)
        pairs.append((w_in_h.at[0, :, lanes], w_in.at[:, lanes]))
        if not save:
            pairs.append((w_back_h.at[0, lanes, :], w_back.at[lanes, :]))
    copies = fetch(sems, *pairs)
    for copy in copies[:3]:
        copy.wait()
    values = hidden[...].reshape(-1, hidden.shape[-1]).astype(F32)
    unit, _ = standardize(values)
    first = (unit * gains[0, 0:1] + offsets[0, 0:1]).astype(BF16)
    feed = (unit * gains[0, 1:2] + offsets[0, 1:2]).astype(BF16)
    if save:
        normed[...] = first
        second[...] = feed
    for copy in copies[3:5]:
        copy.wait()
    make_queries(first, w_query[...], table, queries)
    if not save:
        result[...] = values
    each = 1 if save else 2
    for step in range(inner // block):
        lanes = slice(step * block, (step + 1) * block)
        copies[5 + each * step].wait()
        value, rate = gelu_parts(dot(feed, w_in[:, lanes]))
        value = value.astype(BF16)
        if save:
            active[:, lanes] = value
            slope[:, lanes] = rate.astype(BF16)
        else:
            copies[6 + each * step].wait()
            result[...] += dot(value, w_back[lanes, :])


def front(save, meta, hidden, gains, offsets, table, w_query, w_in, w_back=None):
    width = hidden.shape[-1]
    rows = hidden.size // width
    span = rows // 2 if save else hidden.shape[-2]
    inner = w_in.shape[2]
    block = 768 if inner % 768 == 0 else inner
    operands = [hidden, gains, offsets, table, w_query, w_in] + ([] if save else [w_back])
    if save:
        outs = [(rows, width, BF16)] * 3 + [(rows, inner, BF16)] * 2
    else:
        outs = [(rows, width, BF16), (rows, width, F32)]
    scratch = [
        pltpu.VMEM(hidden.shape, BF16),
        pltpu.VMEM(gains.shape, F32),
        pltpu.VMEM(offsets.shape, F32),
        pltpu.VMEM((span, table.shape[1]), F32),
        pltpu.VMEM((width, width), BF16),
        pltpu.VMEM((width, inner), BF16),
    ]
    if not save:
        scratch.append(pltpu.VMEM((inner, width), BF16))
    scratch.append(pltpu.SemaphoreType.DMA((5 + (1 if save else 2) * (inner // block),)))
    return call(
        partial(front_body, save, block),
        (1,),
        [pl.BlockSpec(memory_space=pl.ANY) if save else IN_HBM] + [IN_HBM] * (len(operands) - 1),
        [whole(out[:2]) for out in outs],
        [shape_of(*out) for out in outs],
        scratch,
    )(meta, *operands)


def spread_pair(values, low):
    lane = lax.broadcasted_iota(jnp.int32, values.shape, 1)
    here = lane < HEAD_DIM if low else lane >= HEAD_DIM
    turned = pltpu.roll(values.astype(F32), HEAD_DIM, 1).astype(BF16)
    one, two = (values, turned) if low else (turned, values)
    zero = jnp.zeros_like(values)
    return jnp.where(here, one, zero), jnp.where(here, two, zero)


def mask_rows(meta, span, length, seq_length):
    key = lax.broadcasted_iota(jnp.int32, (span, length), 1)
    query = lax.broadcasted_iota(jnp.int32, (span, length), 0) + meta[0] * span
    return jnp.where(key <= jnp.minimum(query, seq_length - 1), 0.0, MASKED)


def value_sides(pairs):
    lane = lax.broadcasted_iota(jnp.int32, pairs.shape, 1)
    high = jnp.where(lane < HEAD_DIM, jnp.ones_like(pairs), pairs)
    return pltpu.roll(high.astype(F32), HEAD_DIM, 1).astype(BF16), high


def attend_body(batch, meta, queries, shared, w_out_h, base, result, mixed, stacked, mask, w_out, sems):
    seq = pl.program_id(0)
    span = queries.shape[0]

    @pl.when(seq == 0)
    def _():
        fetch(sems, (w_out_h.at[0], w_out))

    pairs = shared[...].reshape(-1, PAIR)
    length = pairs.shape[0]
    mask[...] = mask_rows(meta, span, length, meta[4 + 2 * batch + seq])
    sides = value_sides(pairs)
    lane = lax.broadcasted_iota(jnp.int32, (span, PAIR), 1)
    for pair in range(PAIRS):
        for side, value in enumerate(spread_pair(queries[:, pair * PAIR : (pair + 1) * PAIR], True)):
            stacked[(2 * pair + side) * span : (2 * pair + side + 1) * span] = value
    group = 4
    for start in range(0, HEADS, group):
        all_scores = dot_nt(stacked[start * span : (start + group) * span], pairs)
        halves = []
        for head in range(start, start + group):
            place = (head - start) * span
            scores = all_scores[place : place + span] + mask[...]
            top = jnp.max(scores, axis=1, keepdims=True)
            weights = jnp.exp2((scores - top) * (SCALE * LOG2E)).astype(BF16)
            summed = dot(weights, sides[head % 2])
            halves.append(summed * pltpu.roll(1.0 / summed, HEAD_DIM, 1))
            if head % 2:
                lanes = slice(head // 2 * PAIR, (head // 2 + 1) * PAIR)
                mixed[:, lanes] = jnp.where(lane < HEAD_DIM, halves[-2], halves[-1]).astype(BF16)

    @pl.when(seq == 0)
    def _():
        pltpu.make_async_copy(w_out_h.at[0], w_out, sems.at[0]).wait()

    result[...] = (base[...] + dot(mixed[...], w_out[...])).astype(BF16)


def attend(batch, meta, queries, gathered, w_out, base):
    width = queries.shape[1]
    count, _, seqs, span, _ = gathered.shape
    rows = seqs * span
    return call(
        partial(attend_body, batch),
        (seqs,),
        [
            pl.BlockSpec((span, width), lambda s, meta: (batch * seqs + s, 0)),
            pl.BlockSpec((count, 1, 1, span, PAIR), lambda s, meta: (0, batch, s, 0, 0)),
            IN_HBM,
            pl.BlockSpec((span, width), lambda s, meta: (batch * seqs + s, 0)),
        ],
        pl.BlockSpec((span, width), lambda s, meta: (s, 0)),
        jax.ShapeDtypeStruct((rows, width), BF16),
        [
            pltpu.VMEM((span, width), BF16),
            pltpu.VMEM((HEADS * span, PAIR), BF16),
            pltpu.VMEM((span, count * span), F32),
            pltpu.VMEM((width, width), BF16),
            pltpu.SemaphoreType.DMA((1,)),
        ],
    )(meta, queries, gathered, w_out, base)


def softmax_back(fresh, pairs, sides, mask, q_sides, d_sides, saved, first_head, weights_sc, d_scores_sc):
    span = q_sides[0].shape[0]
    count = len(q_sides)
    lane = lax.broadcasted_iota(jnp.int32, (span, PAIR), 1)
    products = dot_nt(jnp.concatenate(q_sides + d_sides, axis=0), pairs)
    for n in range(count):
        rows = slice(n * span, (n + 1) * span)
        here = lane == first_head + n
        scores = products[rows]
        d_weights = products[(count + n) * span : (count + n + 1) * span]
        if fresh:
            scores = scores + mask
            top = jnp.max(scores, axis=1, keepdims=True)
            weights = jnp.exp2((scores - top) * (SCALE * LOG2E))
            sums = jnp.sum(weights, axis=1, keepdims=True)
            weights = weights * (1.0 / sums)
            saved = jnp.where(here, top * (SCALE * LOG2E) + jnp.log2(sums), saved)
        else:
            norm = jnp.sum(jnp.where(here, saved, 0.0), axis=1, keepdims=True)
            weights = jnp.exp2(scores * (SCALE * LOG2E) + mask - norm)
        lean = jnp.sum(weights * d_weights, axis=1, keepdims=True)
        weights_sc[rows] = weights.astype(BF16)
        d_scores_sc[rows] = (weights * (d_weights - lean)).astype(BF16)
    return saved


GROUP = 4


def attend_back_part(fresh, seq_length, meta, rows, pairs, queries, d_mixed, table, norms, mixed, d_raw, mask_sc, weights_sc, d_scores_sc):
    span = table.shape[0]
    length = pairs.shape[0]
    lane = lax.broadcasted_iota(jnp.int32, (span, PAIR), 1)
    mask_sc[:, :length] = mask_rows(meta, span, length, seq_length)
    mask = mask_sc[:, :length]
    side = value_sides(pairs)[0] if fresh else None
    saved = jnp.zeros((span, PAIR), F32) if fresh else norms[rows]
    total = None
    for number, first_head in enumerate(range(0, HEADS, GROUP)):
        q_sides, d_sides = [], []
        for pair in range(first_head // 2, (first_head + GROUP) // 2):
            lanes = slice(pair * PAIR, (pair + 1) * PAIR)
            q_sides += spread_pair(queries[rows, lanes], True)
            d_sides += spread_pair(d_mixed[rows, lanes], False)
        slot = number % 2
        weights = weights_sc.at[slot, :, :length]
        d_scores = d_scores_sc.at[slot, :, :length]
        saved = softmax_back(fresh, pairs, side, mask, q_sides, d_sides, saved, first_head, weights, d_scores)
        weights, d_scores = weights[...], d_scores[...]
        d_query = dot(d_scores, pairs)
        out = dot(weights, side) if fresh else None
        scaled = [(value.astype(F32) * SCALE).astype(BF16) for value in q_sides]
        part = dot_tn(
            jnp.concatenate([d_scores, weights], axis=0), jnp.concatenate(scaled + d_sides, axis=0)
        )
        total = part if total is None else total + part
        for n in range(0, GROUP, 2):
            pair = (first_head + n) // 2
            lanes = slice(pair * PAIR, (pair + 1) * PAIR)

            def join(values):
                one = values[n * span : (n + 1) * span]
                two = values[(n + 1) * span : (n + 2) * span]
                return jnp.where(lane < HEAD_DIM, one, pltpu.roll(two, HEAD_DIM, 1))

            if fresh:
                mixed[rows, lanes] = join(out).astype(BF16)
            d_raw[rows, lanes] = rotate(join(d_query) * SCALE, table[...], -1.0).astype(BF16)
    if fresh:
        norms[rows] = saved
    return total


def feed_back_part(upstream, slope, w_in, w_back, d_upper, block, waits):
    inner = slope.shape[1]
    two = None
    for step in range(inner // block):
        lanes = slice(step * block, (step + 1) * block)
        waits(step)
        rate = (dot_nt(upstream, w_back[lanes, :]) * slope[:, lanes].astype(F32)).astype(BF16)
        d_upper[:, lanes] = rate
        part = dot_nt(rate, w_in[:, lanes])
        two = part if two is None else two + part
    return two


def chain_body(which, block, meta, upstream, hidden, queries, slope, shared, *rest):
    (gains_h, table_h, w_query_h, w_out_h, w_in_h, w_back_h) = rest[:6]
    (mixed, norms, d_raw, d_shared, d_upper, d_hidden, d_low, d_norms) = rest[6:14]
    (gains, table, w_query, w_out, w_in, w_back, d_mixed, mask_sc, weights_sc, d_scores_sc, sems) = rest[14:]
    span = table.shape[0]
    seqs = shared.shape[2]
    inner = slope.shape[1]
    batch = which[0] + which[1] * meta[2]
    place = pl.ds(pl.multiple_of(meta[0] * span, span), span)
    operands = [(w_out_h.at[0], w_out), (table_h.at[place], table), (gains_h, gains), (w_query_h.at[0], w_query)]
    for start in range(0, inner, block):
        lanes = pl.ds(start, block)
        operands.append((w_back_h.at[0, lanes, :], w_back.at[lanes, :]))
        operands.append((w_in_h.at[0, :, lanes], w_in.at[:, lanes]))
    copies = fetch(sems, *operands)
    copies[0].wait()
    d_mixed[...] = dot_nt(upstream[...], w_out[...]).astype(BF16)
    copies[1].wait()
    for seq in range(seqs):
        pairs = shared[:, 0, seq].reshape(-1, PAIR)
        rows = slice(seq * span, (seq + 1) * span)
        total = attend_back_part(
            True, meta[4 + 2 * batch + seq], meta, rows, pairs, queries, d_mixed, table, norms, mixed, d_raw,
            mask_sc, weights_sc, d_scores_sc
        )
        d_shared[:, seq] = total.astype(BF16).reshape(d_shared.shape[0], span, PAIR)

    def waits(step):
        copies[4 + 2 * step].wait()
        copies[5 + 2 * step].wait()

    two = feed_back_part(upstream[...], slope, w_in, w_back, d_upper, block, waits)
    copies[2].wait()
    copies[3].wait()
    one = dot_nt(d_raw[...], w_query[...])
    unit, scale = standardize(hidden[...].astype(F32))
    total = upstream[...].astype(F32) + norm_back(one * gains[0, 0:1] + two * gains[0, 1:2], 1.0, unit, scale)
    d_hidden[...] = total
    d_low[...] = total.astype(BF16)
    d_norms[...] = sum_rows(one * unit, one, two * unit, two)


def chain(which, meta, upstream, hidden, queries, slope, gathered, gains, table, w_query, w_out, w_in, w_back):
    rows, width = queries.shape
    count, _, seqs, span, _ = gathered.shape
    inner = slope.shape[1]
    length = count * span
    block = 768 if inner % 768 == 0 else inner
    flat = whole((rows, width))
    outs = [(rows, width, BF16), (rows, PAIR, F32), (rows, width, BF16), None, (rows, inner, BF16), (rows, width, F32), (rows, width, BF16), (8, width, F32)]
    shared_shape = (count, seqs, span, PAIR)
    return call(
        partial(chain_body, which, block),
        (1,),
        [flat, flat, flat, whole((rows, inner))]
        + [pl.BlockSpec((count, 1, seqs, span, PAIR), lambda j, meta: (0, which[0] + which[1] * meta[2], 0, 0, 0))]
        + [IN_HBM] * 6,
        [whole(shared_shape) if out is None else whole(out[:2]) for out in outs],
        [jax.ShapeDtypeStruct(shared_shape, BF16) if out is None else shape_of(*out) for out in outs],
        [
            pltpu.VMEM(gains.shape, F32),
            pltpu.VMEM((span, table.shape[1]), F32),
            pltpu.VMEM((width, width), BF16),
            pltpu.VMEM((width, width), BF16),
            pltpu.VMEM((width, inner), BF16),
            pltpu.VMEM((inner, width), BF16),
            pltpu.VMEM((rows, width), BF16),
            pltpu.VMEM((span, length), F32),
            pltpu.VMEM((2, GROUP * span, length), BF16),
            pltpu.VMEM((2, GROUP * span, length), BF16),
            pltpu.SemaphoreType.DMA((4 + 2 * (inner // block),)),
        ],
    )(meta, upstream, hidden, queries, slope, gathered, gains, table, w_query, w_out, w_in, w_back)


def attend_back_body(which, split, meta, upstream, queries, norms, shared, *rest):
    (up_d, raw_d, mixed_c, mixed_d, normed_c, normed_d, w_out_h, w_query_h, table_h) = rest[:9]
    (d_raw, d_shared, d_normed) = rest[9:12]
    halves = rest[12:14] if split else rest[12:13]
    (d_mixed, mask_sc, weights_sc, d_scores_sc, table, w_out, w_query, sems) = rest[12 + len(halves) :][:8]
    span = table.shape[0]
    batch = which[0] + which[1] * meta[2]
    place = pl.ds(pl.multiple_of(meta[0] * span, span), span)
    copies = fetch(sems, (w_out_h.at[0], w_out), (table_h.at[place], table), (w_query_h.at[0], w_query))
    copies[0].wait()
    d_mixed[...] = dot_nt(upstream[...], w_out[...]).astype(BF16)
    copies[1].wait()
    for seq in range(shared.shape[2]):
        pairs = shared[:, 0, seq].reshape(-1, PAIR)
        rows = slice(seq * span, (seq + 1) * span)
        total = attend_back_part(
            False, meta[4 + 2 * batch + seq], meta, rows, pairs, queries, d_mixed, table, norms, None, d_raw,
            mask_sc, weights_sc, d_scores_sc
        )
        d_shared[:, seq] = total.astype(BF16).reshape(d_shared.shape[0], span, PAIR)
    copies[2].wait()
    d_normed[...] = dot_nt(d_raw[...], w_query[...])
    both = jnp.concatenate([upstream[...], up_d[...]], axis=0)
    left = jnp.concatenate([mixed_c[...], mixed_d[...]], axis=0)
    outer = dot_tn(left, both).astype(BF16)
    both = jnp.concatenate([d_raw[...], raw_d[...]], axis=0)
    left = jnp.concatenate([normed_c[...], normed_d[...]], axis=0)
    query = dot_tn(left, both).astype(BF16)
    width = both.shape[1]
    if len(halves) == 1:
        halves[0][:, :width] = outer
        halves[0][:, width:] = query
        return
    keep, send, pair_sc = halves[0], halves[1], rest[-1]
    pair_sc[..., :width] = outer.reshape(pair_sc.shape[:3] + (width,))
    pair_sc[..., width:] = query.reshape(pair_sc.shape[:3] + (width,))
    keep[...] = pair_sc[:, pl.ds(meta[1], 1)].reshape(keep.shape)
    send[...] = pair_sc[:, pl.ds(1 - meta[1], 1)].reshape(send.shape)


def attend_back(
    which, shards, meta, upstream, queries, norms, gathered, up_d, raw_d, mixed_c, mixed_d, normed_c, normed_d, w_out, w_query, table
):
    rows, width = queries.shape
    count, _, seqs, span, _ = gathered.shape
    length = count * span
    shared_shape = (count, seqs, span, PAIR)
    part = width // shards
    split = part % 16 == 0
    if split:
        pairs = [(shards // 2, part, 2 * width)] * 2
    else:
        pairs = [(width, 2 * width)]
    outs = call(
        partial(attend_back_body, which, split),
        (1,),
        [whole((rows, width))] * 2
        + [whole(norms.shape)]
        + [pl.BlockSpec((count, 1, seqs, span, PAIR), lambda j, meta: (0, which[0] + which[1] * meta[2], 0, 0, 0))]
        + [whole((rows, width))] * 6
        + [IN_HBM] * 3,
        [whole((rows, width)), whole(shared_shape), whole((rows, width))] + [whole(shape) for shape in pairs],
        [
            shape_of(rows, width, BF16),
            jax.ShapeDtypeStruct(shared_shape, BF16),
            shape_of(rows, width, F32),
        ]
        + [jax.ShapeDtypeStruct(shape, BF16) for shape in pairs],
        [
            pltpu.VMEM((rows, width), BF16),
            pltpu.VMEM((span, length), F32),
            pltpu.VMEM((2, GROUP * span, length), BF16),
            pltpu.VMEM((2, GROUP * span, length), BF16),
            pltpu.VMEM((span, table.shape[1]), F32),
            pltpu.VMEM((width, width), BF16),
            pltpu.VMEM((width, width), BF16),
            pltpu.SemaphoreType.DMA((3,)),
        ]
        + ([pltpu.VMEM((shards // 2, 2, part, 2 * width), BF16)] if split else []),
    )(meta, upstream, queries, norms, gathered, up_d, raw_d, mixed_c, mixed_d, normed_c, normed_d, w_out, w_query, table)
    if split:
        return outs
    return (*outs[:3], *split_cores(outs[3].reshape(shards, part, 2 * width)))


def finish_body(block, meta, *rest):
    hidden, mixed, active = rest[0:2], rest[2:4], rest[4:6]
    w_out_h, w_back_h, result_c, result_d, w_out, w_back, sems = rest[6:]
    inner = w_back.shape[0]
    pairs = [(w_out_h.at[0], w_out)]
    for start in range(0, inner, block):
        pairs.append((w_back_h.at[0, pl.ds(start, block), :], w_back.at[pl.ds(start, block), :]))
    copies = fetch(sems, *pairs)
    rows = hidden[0].shape[0]

    def both(refs, lanes=slice(None)):
        return jnp.concatenate([refs[0][:, lanes], refs[1][:, lanes]], axis=0)

    copies[0].wait()
    total = both(hidden).astype(F32) + dot(both(mixed), w_out[...])
    for step in range(inner // block):
        lanes = slice(step * block, (step + 1) * block)
        copies[1 + step].wait()
        total += dot(both(active, lanes), w_back[lanes, :])
    result_c[...] = total[:rows].astype(BF16)
    result_d[...] = total[rows:].astype(BF16)


def finish(meta, hidden, mixed, active, w_out, w_back):
    rows, width = hidden[0].shape
    inner = active[0].shape[1]
    block = 768 if inner % 768 == 0 else inner
    return call(
        partial(finish_body, block),
        (1,),
        [whole((rows, width))] * 4 + [whole((rows, inner))] * 2 + [IN_HBM] * 2,
        [whole((rows, width))] * 2,
        [shape_of(rows, width, BF16)] * 2,
        [
            pltpu.VMEM((width, width), BF16),
            pltpu.VMEM((inner, width), BF16),
            pltpu.SemaphoreType.DMA((1 + inner // block,)),
        ],
    )(meta, *hidden, *mixed, *active, w_out, w_back)


def sum_rows(*values):
    sums = [jnp.sum(value, axis=0, keepdims=True) for value in values]
    return jnp.concatenate(sums + [jnp.zeros_like(sums[0])] * (8 - len(sums)), axis=0)


def feed_back_body(block, meta, upstream, slope, w_in_h, w_back_h, d_upper, d_second, w_in, w_back, sems):
    inner = slope.shape[1]
    operands = []
    for start in range(0, inner, block):
        lanes = pl.ds(start, block)
        operands.append((w_back_h.at[0, lanes, :], w_back.at[lanes, :]))
        operands.append((w_in_h.at[0, :, lanes], w_in.at[:, lanes]))
    copies = fetch(sems, *operands)

    def waits(step):
        copies[2 * step].wait()
        copies[2 * step + 1].wait()

    d_second[...] = feed_back_part(upstream[...], slope, w_in, w_back, d_upper, block, waits)


def feed_back(meta, upstream, slope, w_in, w_back):
    rows, width = upstream.shape
    inner = w_in.shape[2]
    block = 768 if inner % 768 == 0 else inner
    return call(
        partial(feed_back_body, block),
        (1,),
        [whole((rows, width)), whole((rows, inner))] + [IN_HBM] * 2,
        [whole((rows, inner)), whole((rows, width))],
        [shape_of(rows, inner, BF16), shape_of(rows, width, F32)],
        [
            pltpu.VMEM((width, inner), BF16),
            pltpu.VMEM((inner, width), BF16),
            pltpu.SemaphoreType.DMA((2 * (inner // block),)),
        ],
    )(meta, upstream, slope, w_in, w_back)


def store_halves(meta, block, keep, send, scratch):
    groups, _, part, lanes = scratch.shape
    scratch[...] = block.astype(BF16).reshape(groups, 2, part, lanes)
    core = meta[1]
    keep[...] = scratch[:, pl.ds(core, 1)].reshape(keep.shape)
    send[...] = scratch[:, pl.ds(1 - core, 1)].reshape(send.shape)


def late_feed_body(shards, block, meta, active_c, active_d, up_c, up_d, slope, *rest):
    w_in_h, w_back_h, keep, send, d_upper, d_second, w_in, w_back, scratch, sems = rest
    inner = w_in.shape[1]
    operands = []
    for start in range(0, inner, block):
        lanes = pl.ds(start, block)
        operands.append((w_back_h.at[0, lanes, :], w_back.at[lanes, :]))
        operands.append((w_in_h.at[0, :, lanes], w_in.at[:, lanes]))
    copies = fetch(sems, *operands)
    part = inner // shards
    both = jnp.concatenate([up_c[...], up_d[...]], axis=0)
    for group in range(shards // 2):
        lanes = slice(group * 2 * part, (group + 1) * 2 * part)
        left = jnp.concatenate([active_c[:, lanes], active_d[:, lanes]], axis=0)
        scratch[group] = dot_tn(left, both).astype(BF16).reshape(2, part, both.shape[1])
    core = meta[1]
    keep[...] = scratch[:, pl.ds(core, 1)].reshape(keep.shape)
    send[...] = scratch[:, pl.ds(1 - core, 1)].reshape(send.shape)

    def waits(step):
        copies[2 * step].wait()
        copies[2 * step + 1].wait()

    d_second[...] = feed_back_part(up_c[...], slope, w_in, w_back, d_upper, block, waits)


def late_feed(meta, shards, active_c, active_d, up_c, up_d, slope, w_in, w_back):
    rows, width = up_c.shape
    inner = w_in.shape[2]
    part = inner // shards
    if part % 64:
        halves = weights_full(meta, shards, active_c, active_d, up_c, up_d)
        return (*halves, *feed_back(meta, up_c, slope, w_in, w_back))
    block = 768 if inner % 768 == 0 else inner
    half = (shards // 2, part, width)
    return call(
        partial(late_feed_body, shards, block),
        (1,),
        [whole((rows, inner))] * 2 + [whole((rows, width))] * 2 + [whole((rows, inner))] + [IN_HBM] * 2,
        [whole(half), whole(half), whole((rows, inner)), whole((rows, width))],
        [jax.ShapeDtypeStruct(half, BF16)] * 2 + [shape_of(rows, inner, BF16), shape_of(rows, width, F32)],
        [
            pltpu.VMEM((width, inner), BF16),
            pltpu.VMEM((inner, width), BF16),
            pltpu.VMEM((shards // 2, 2, part, width), BF16),
            pltpu.SemaphoreType.DMA((2 * (inner // block),)),
        ],
    )(meta, active_c, active_d, up_c, up_d, slope, w_in, w_back)


def weights_full_body(meta, left_c, left_d, right_c, right_d, full, turned_c, turned_d):
    @pl.when(pl.program_id(0) == 0)
    def _():
        turned_c[...] = left_c[...].T
        turned_d[...] = left_d[...].T

    block = dot(turned_c[...], right_c[...]) + dot(turned_d[...], right_d[...])
    full[...] = block.astype(BF16)


def weights_full(meta, shards, left_c, left_d, right_c, right_d):
    rows, tall = left_c.shape
    wide = right_c.shape[1]
    block = 256
    full = call(
        weights_full_body,
        (wide // block,),
        [whole((rows, tall))] * 2 + [pl.BlockSpec((rows, block), lambda j, meta: (0, j))] * 2,
        pl.BlockSpec((tall, block), lambda j, meta: (0, j)),
        jax.ShapeDtypeStruct((tall, wide), BF16),
        [pltpu.VMEM((tall, rows), BF16), pltpu.VMEM((tall, rows), BF16)],
    )(meta, left_c, left_d, right_c, right_d)
    return split_cores(full.reshape(shards, tall // shards, wide))


def weights_wide_body(meta, left_c, left_d, right_c, right_d, keep, send, scratch, turned_c, turned_d):
    @pl.when(pl.program_id(0) == 0)
    def _():
        turned_c[...] = left_c[...].T
        turned_d[...] = left_d[...].T

    block = dot(turned_c[...], right_c[...]) + dot(turned_d[...], right_d[...])
    store_halves(meta, block, keep, send, scratch)


def weights_wide(meta, shards, left_c, left_d, right_c, right_d):
    rows, tall = left_c.shape
    wide = right_c.shape[1]
    block = min(512, wide) if wide % 512 == 0 else 384
    part = tall // shards
    if part % 16:
        return weights_full(meta, shards, left_c, left_d, right_c, right_d)
    spec = pl.BlockSpec((shards // 2, part, block), lambda j, meta: (0, 0, j))
    shape = jax.ShapeDtypeStruct((shards // 2, part, wide), BF16)
    return call(
        weights_wide_body,
        (wide // block,),
        [whole((rows, tall))] * 2 + [pl.BlockSpec((rows, block), lambda j, meta: (0, j))] * 2,
        [spec, spec],
        [shape, shape],
        [
            pltpu.VMEM((shards // 2, 2, part, block), BF16),
            pltpu.VMEM((tall, rows), BF16),
            pltpu.VMEM((tall, rows), BF16),
        ],
    )(meta, left_c, left_d, right_c, right_d)


def tail_body(
    meta, own_d, own_c, other, hid_d, hid_c, nrm_d, nrm_c, dh_d, sums_d, up_c, one_c, two_c,
    gains_h, w_keys_h, table_h, grads, *rest
):
    small, (gains, w_keys, table, sems) = rest[:2], rest[2:6]
    section = meta[2]
    first = (section == 0).astype(F32)
    span = table.shape[0]
    seqs = own_d.shape[0]
    rows = pl.ds(pl.multiple_of(meta[0] * span, span), span)
    copies = fetch(sems, (gains_h, gains), (w_keys_h, w_keys), (table_h.at[rows], table))
    for copy in copies:
        copy.wait()
    keys_sum = None
    norm_sum = sums_d[...]
    for slot, (own, hidden, normed) in enumerate(((own_d, hid_d, nrm_d), (own_c, hid_c, nrm_c))):
        raw = []
        for seq in range(seqs):
            both = (own[seq].astype(F32) + other[1 - slot, seq].astype(F32)) * first
            raw.append(rotate_keys(both, table[...], -1.0).astype(BF16))
        raw = jnp.concatenate(raw, axis=0)
        part = dot_tn(normed[...], raw)
        keys_sum = part if keys_sum is None else keys_sum + part
        one = dot_nt(raw, w_keys[...])
        unit, scale = standardize(hidden[...].astype(F32))
        if slot == 0:
            total = dh_d[...] + norm_back(one, gains[0, 0:1], unit, scale)
            norm_sum += sum_rows(one * unit, one)
        else:
            one, two = one + one_c[...], two_c[...]
            total = up_c[...].astype(F32) + norm_back(one * gains[0, 0:1] + two * gains[0, 1:2], 1.0, unit, scale)
            norm_sum += sum_rows(one * unit, one, two * unit, two)
        batch = section if slot == 0 else 1 - section
        grads[pl.ds(batch, 1)] = total[None]
    if len(rest) == 6:
        small[0][...] = keys_sum.astype(BF16)
        small[1][...] = norm_sum
        return
    gather = rest[6]
    groups, _, part, _ = gather.shape
    share = part // 2
    width = keys_sum.shape[0]
    turned = jnp.concatenate([norm_sum, jnp.zeros((PAIR - 8, width), F32)], axis=0).T
    for shard in range(2 * groups):
        place = gather.at[shard // 2, shard % 2]
        for half in range(2):
            start = half * width // 2 + shard * share
            place[half * share : (half + 1) * share, :PAIR] = keys_sum[start : start + share]
        place[:, PAIR:] = turned[shard * part : (shard + 1) * part]
    small[0][...] = gather[:, pl.ds(meta[1], 1)].reshape(small[0].shape).astype(BF16)
    small[1][...] = gather[:, pl.ds(1 - meta[1], 1)].reshape(small[1].shape).astype(BF16)


def small_parts(shards, sections, d_keys, d_norms):
    width = d_keys.shape[0]
    share = width // (sections * shards)
    d_keys = d_keys.reshape(sections, shards, share, PAIR).transpose(1, 0, 2, 3).reshape(shards, sections * share, PAIR)
    d_norms = d_norms.T.reshape(shards, width // shards, 8)
    d_norms = jnp.pad(d_norms, ((0, 0), (0, 0), (0, PAIR - 8))).astype(BF16)
    return split_cores(jnp.concatenate([d_keys, d_norms], axis=-1))


def tail(shards, sections, meta, *arrays):
    rows, width = arrays[3].shape
    span = arrays[0].shape[1]
    gains, w_keys, table = arrays[-3:]
    part = width // shards
    split = part % 16 == 0 and sections == 2
    if split:
        outs = [jax.ShapeDtypeStruct((shards // 2, part, 2 * PAIR), BF16)] * 2
    else:
        outs = [shape_of(width, PAIR, BF16), shape_of(8, width, F32)]
    grads, *small = call(
        tail_body,
        (1,),
        [whole(array.shape) for array in arrays[:-3]] + [IN_HBM] * 3,
        [whole((2, rows, width))] + [whole(out.shape) for out in outs],
        [jax.ShapeDtypeStruct((2, rows, width), F32)] + outs,
        [
            pltpu.VMEM(gains.shape, F32),
            pltpu.VMEM(w_keys.shape, BF16),
            pltpu.VMEM((span, table.shape[1]), F32),
            pltpu.SemaphoreType.DMA((3,)),
        ]
        + ([pltpu.VMEM((shards // 2, 2, part, 2 * PAIR), F32)] if split else []),
    )(meta, *arrays)
    return (grads, *small) if split else (grads, *small_parts(shards, sections, *small))


def swap(value, axis, bit):
    count = lax.axis_size(axis)
    return lax.ppermute(value, axis, [(source, source ^ bit) for source in range(count)])


def across(value, steps):
    pairs = [(0, 1)] if steps > 0 else [(1, 0)]
    return lax.ppermute(value, "section", pairs)


def after(value, *others):
    return lax.optimization_barrier((value, *others))[0]


def wide_sum(values):
    total = values[0].astype(F32)
    for value in values[1:]:
        total = total + value.astype(F32)
    return total


class Halving:
    def __init__(self, *parts):
        self.parts = list(parts)

    def prepare(self, axis, bit, low, *hold):
        cut = []
        for value in self.parts:
            places = value.shape[0]
            cut.append(value.reshape(((places // 2, 2) if low else (2, places // 2)) + value.shape[1:]))
        if hold:
            cut[0] = after(cut[0], *hold)
        place = 1 if low else 0
        mine = (lax.axis_index(axis) // bit) % 2
        other = wide_sum([lax.dynamic_index_in_dim(value, 1 - mine, place, keepdims=False) for value in cut])
        self.sent = other.astype(BF16)
        self.parts = [lax.dynamic_index_in_dim(value, mine, place, keepdims=False) for value in cut]
        self.way = (axis, bit)

    def launch(self, *hold):
        if hold:
            self.sent = after(self.sent, *hold)
        self.parts.append(swap(self.sent, *self.way))

    @property
    def received(self):
        return self.parts[-1]

    def bits(self, axis):
        count = lax.axis_size(axis)
        found = [1 << n for n in range(1 if axis == "ctx" else 0, count.bit_length() - 1)]
        return [(axis, bit, axis == "ctx") for bit in (found if axis == "ctx" else found[::-1])]

    def along(self, steps, hold=(), held=()):
        for step in steps:
            self.prepare(*step, *hold)
            self.launch(*held)
            hold, held = (), ()

    def result(self):
        return wide_sum([value.reshape(value.shape[1:]) for value in self.parts])


def split_cores(value):
    shards, part, lanes = value.shape
    cut = value.reshape(shards // 2, 2, part, lanes)
    core = lax.axis_index("ctx") % 2
    return (
        lax.dynamic_index_in_dim(cut, core, 1, keepdims=False),
        lax.dynamic_index_in_dim(cut, 1 - core, 1, keepdims=False),
    )


def per_device(
    length, tokens, lengths, norm_gains, norm_offsets, w_query, w_keys, w_out, w_in, w_back, cotangent
):
    batches, seqs, span, width = tokens.shape
    rows = seqs * span
    shards = lax.axis_size("dp") * lax.axis_size("ctx")
    section = lax.axis_index("section")
    place = lax.axis_index("ctx")
    first = section == 0
    table = jnp.asarray(rotary_table(length))

    own = make_keys(tokens, norm_gains, norm_offsets, w_keys, table)
    gathered = lax.all_gather(own, "ctx")
    meta = jnp.concatenate(
        [jnp.stack([place, place % 2, section, section]).astype(jnp.int32), lengths.reshape(-1)]
    )

    queries, base = front(False, meta, tokens, norm_gains, norm_offsets, table, w_query, w_in, w_back)
    came_a = across(attend(0, meta, queries, gathered, w_out, base), 1)
    came_b = across(attend(1, meta, queries, gathered, w_out, base), 1)
    gathered = lax.all_gather(jnp.where(first, own, across(own, 1)), "ctx")

    flat = tokens.reshape(batches, rows, width)
    cot = cotangent.reshape(batches, rows, width)

    def front_of(hidden):
        return front(True, meta, hidden, norm_gains, norm_offsets, table, w_query, w_in)

    def chain_of(which, upstream, hidden, queries, slope):
        return chain(
            which, meta, upstream, hidden, queries, slope, gathered, norm_gains, table, w_query, w_out, w_in, w_back
        )

    hid_c = jnp.where(first, flat[1], came_a)
    queries_c, normed_c, second_c, active_c, slope_c = front_of(hid_c)
    mixed_c, norms_c, _, ds_one, _, _, low_one, _ = chain_of(PASS_C, cot[0], hid_c, queries_c, slope_c)
    back_d = across(low_one, -1)
    hid_d = jnp.where(first, flat[0], came_b)
    queries_d, normed_d, second_d, active_d, slope_d = front_of(hid_d)
    up_d = jnp.where(first, back_d, cot[1])
    mixed_d, _, raw_d, ds_d, upper_d, dh_d, low_d, sums_d = chain_of(PASS_D, up_d, hid_d, queries_d, slope_d)
    back_c = across(low_d, -1)

    early = lax.psum_scatter(jnp.stack([ds_d, ds_one], axis=1), "ctx", scatter_dimension=0)
    up_c = jnp.where(first, back_c, cot[0])
    keep, send, upper_c, two_c = late_feed(meta, shards, active_c, active_d, up_c, up_d, slope_c, w_in, w_back)
    back = Halving(keep, swap(send, "ctx", 1))
    groups, depth = back.bits("dp"), back.bits("ctx")
    keep, send = weights_wide(meta, shards, second_c, second_d, upper_c, upper_d)
    inner = Halving(keep, swap(send, "ctx", 1))
    back.prepare(*groups[0], keep)
    back.launch()
    inner.prepare(*depth[0], back.sent)
    inner.launch()
    _, ds_c, one_c, keep, send = attend_back(
        PASS_C, shards, meta, after(up_c, inner.sent), queries_c, norms_c, gathered, up_d, raw_d, mixed_c, mixed_d,
        normed_c, normed_d, w_out, w_query, table
    )
    late = Halving(ds_c)
    late.prepare("ctx", 1, True)
    late.launch()
    pair = Halving(keep, swap(send, "ctx", 1))
    back.along(groups[1:])
    back.prepare(*depth[0], one_c)
    inner.prepare(*depth[1], one_c)
    late.prepare(*depth[0], back.sent, inner.sent)
    late.launch()
    pair.prepare(*groups[0], late.sent)
    pair.launch()
    late.along(depth[1:], hold=(pair.sent,))
    back.launch(late.sent)
    inner.launch(late.sent)
    early, _ = lax.optimization_barrier((early, late.sent))
    other_keys = across(early, -1)
    sections = lax.axis_size("section")
    late = after(late.result().astype(BF16), inner.sent, back.sent)
    input_grads, keep, send = tail(
        shards, sections, meta, early[0], late, other_keys, hid_d, hid_c, normed_d, normed_c, dh_d, sums_d, up_c, one_c, two_c,
        norm_gains, w_keys, table
    )
    small = Halving(keep, swap(send, "ctx", 1))
    out_c, out_d = finish(
        meta, (hid_c, after(hid_d, keep)), (mixed_c, mixed_d), (active_c, active_d), w_out, w_back
    )
    pair.along(groups[1:])
    back.prepare(*depth[1], out_c)
    inner.prepare(*(depth[2:] + groups)[0], out_c)
    pair.prepare(*depth[0], out_c)
    small.along(groups, hold=(back.sent, inner.sent, pair.sent))
    inner.launch(small.sent)
    small.prepare(*depth[0])
    small.launch()
    back.launch(small.sent)
    pair.launch(back.sent)
    small.along(depth[1:])
    back.along(depth[2:])
    pair.along(depth[1:])
    inner.along((depth[2:] + groups)[1:])
    small = small.result()
    pair = pair.result()
    share = width // (sections * shards)
    grad_norms = small[:, PAIR : PAIR + 4]
    outs = jnp.where(first, jnp.stack([out_d, out_c]), jnp.stack([out_c, out_d]))
    keys_both = small[:, :PAIR].reshape(sections, share, PAIR)
    grad_keys = jnp.where(first, keys_both[0], across(keys_both[1], 1))
    return (
        outs.reshape((1,) + tokens.shape),
        input_grads.reshape((1,) + tokens.shape),
        grad_norms[None],
        pair[None, :, width:],
        grad_keys,
        pair[None, :, :width],
        inner.result()[None],
        back.result()[None],
    )


def solution(mesh):
    def run(*arrays):
        length = arrays[0].shape[2]
        return jax.shard_map(
            partial(per_device, length),
            mesh=mesh,
            in_specs=(
                P(None, "dp", "ctx", None),
                P(None, "dp"),
                P("section", None, None),
                P("section", None, None),
                P("section", None, None),
                P(),
                P("section", None, None),
                P("section", None, None),
                P("section", None, None),
                P(None, "dp", "ctx", None),
            ),
            out_specs=(
                P("section", None, "dp", "ctx", None),
                P("section", None, "dp", "ctx", None),
                P("section", ("dp", "ctx"), None),
                P("section", ("dp", "ctx"), None),
                P(("section", "dp", "ctx"), None),
                P("section", ("dp", "ctx"), None),
                P("section", ("dp", "ctx"), None),
                P("section", ("dp", "ctx"), None),
            ),
            check_vma=False,
        )(*arrays)

    return run
```

```python
from functools import partial

import jax
import jax.numpy as jnp
import numpy as np
from jax import lax
from jax.experimental import pallas as pl
from jax.experimental.pallas import tpu as pltpu
from jax.sharding import PartitionSpec as P

HEADS = 12
HEAD_DIM = 64
ROT = 16
PAIR = 2 * HEAD_DIM
PAIRS = HEADS // 2
LOG2E = 1.4426950408889634
SCALE = HEAD_DIM**-0.5
MASKED = -1e30
F32 = jnp.float32
BF16 = jnp.bfloat16
VMEM_LIMIT = 60 * 1024 * 1024
FLOPS = 1_000_000

PASS_C = (1, -1)
PASS_D = (0, 1)


def dot(left, right):
    return jnp.dot(left, right, preferred_element_type=F32)


def dot_nt(left, right, **kwargs):
    return lax.dot_general(left, right, (((1,), (1,)), ((), ())), preferred_element_type=F32, **kwargs)


def dot_tn(left, right):
    return lax.dot_general(left, right, (((0,), (0,)), ((), ())), preferred_element_type=F32)


def whole(shape):
    zeros = (0,) * len(shape)
    return pl.BlockSpec(shape, lambda *_: zeros)


def call(body, grid, in_specs, out_specs, out_shape, scratch=(), behind=()):
    count = len(in_specs)

    def run(meta, *refs):
        body(meta, *refs[:count], *refs[count + len(behind) :])

    in_specs = list(in_specs) + [IN_HBM] * len(behind)
    made = pl.pallas_call(
        run,
        grid_spec=pltpu.PrefetchScalarGridSpec(
            num_scalar_prefetch=1,
            grid=grid,
            in_specs=in_specs,
            out_specs=out_specs,
            scratch_shapes=list(scratch),
        ),
        out_shape=out_shape,
        compiler_params=pltpu.CompilerParams(vmem_limit_bytes=VMEM_LIMIT),
        cost_estimate=pl.CostEstimate(flops=FLOPS, bytes_accessed=0, transcendentals=0),
    )
    return lambda *operands: made(*operands, *behind)


IN_HBM = pl.BlockSpec(memory_space=pltpu.HBM)


def fetch(sems, *pairs):
    copies = [pltpu.make_async_copy(source, target, sems.at[n]) for n, (source, target) in enumerate(pairs)]
    for copy in copies:
        copy.start()
    return copies


def shape_of(rows, columns, dtype):
    return jax.ShapeDtypeStruct((rows, columns), dtype)


def rotary_table(length):
    half = ROT // 2
    inverse = 10000.0 ** (-np.arange(half) * (2.0 / ROT))
    angles = np.arange(length)[:, None] * inverse[None, :]
    cosine, sine = np.cos(angles), np.sin(angles)
    table = np.zeros((length, 3, 2, HEAD_DIM), np.float32)
    table[:, 0] = 1.0
    table[:, 0, :, :half] = cosine[:, None]
    table[:, 0, :, half:ROT] = cosine[:, None]
    table[:, 1, :, :half] = -sine[:, None]
    table[:, 2, :, half:ROT] = sine[:, None]
    return table.reshape(length, 3 * PAIR)


def rotate(values, table, sign=1.0):
    around = pltpu.roll(values, PAIR - ROT // 2, 1) * table[:, PAIR : 2 * PAIR]
    around = around + pltpu.roll(values, ROT // 2, 1) * table[:, 2 * PAIR :]
    return values * table[:, :PAIR] + (around if sign > 0 else -around)


def rotate_keys(values, table, sign=1.0):
    lane = lax.broadcasted_iota(jnp.int32, values.shape, 1)
    return jnp.where(lane < HEAD_DIM, rotate(values, table, sign), values)


def standardize(values):
    center = values - jnp.mean(values, axis=-1, keepdims=True)
    scale = lax.rsqrt(jnp.mean(center * center, axis=-1, keepdims=True) + 1e-05)
    return center * scale, scale


def norm_back(grads, gain, normed, scale):
    inner = grads * gain
    lean = jnp.mean(inner, axis=-1, keepdims=True)
    along = jnp.mean(inner * normed, axis=-1, keepdims=True)
    return scale * (inner - lean - normed * along)


def gelu_parts(values):
    size = jnp.abs(values) * 0.7071067811865476
    base = 1.0 + 0.3275911 * size
    turn = pl.reciprocal(base, approx=True)
    turn = turn * (2.0 - base * turn)
    bell = jnp.exp2(values * values * (-0.5 * LOG2E))
    tail = turn * (
        0.127414796 + turn * (-0.142248368 + turn * (0.7107068705 + turn * (-0.7265760135 + turn * 0.5307027145)))
    )
    tail = tail * bell
    share = jnp.where(values >= 0.0, 1.0 - tail, tail)
    return values * share, share + values * (bell * 0.3989422804014327)


def keys_body(tokens_h, gains_h, offsets_h, w_keys_h, table_h, shared, tokens, gains, offsets, w_keys, table, sems):
    span = table.shape[0]
    rows = pl.ds(pl.multiple_of(lax.axis_index("ctx") * span, span), span)
    copies = fetch(
        sems,
        (tokens_h, tokens),
        (gains_h, gains),
        (offsets_h, offsets),
        (w_keys_h, w_keys),
        (table_h.at[rows], table),
    )
    for copy in copies:
        copy.wait()
    batches, seqs, _, width = tokens.shape
    normed, _ = standardize(tokens[...].reshape(-1, width).astype(F32))
    normed = (normed * gains[0, 0:1] + offsets[0, 0:1]).astype(BF16)
    raw = dot(normed, w_keys[...])
    for batch in range(batches):
        for seq in range(seqs):
            start = (batch * seqs + seq) * span
            shared[batch, seq] = rotate_keys(raw[start : start + span], table[...]).astype(BF16)


def make_keys(tokens, gains, offsets, w_keys, table):
    batches, seqs, span, width = tokens.shape
    return pl.pallas_call(
        keys_body,
        in_specs=[IN_HBM] * 5,
        out_specs=pl.BlockSpec(memory_space=pltpu.VMEM),
        out_shape=jax.ShapeDtypeStruct((batches, seqs, span, PAIR), BF16),
        scratch_shapes=[
            pltpu.VMEM(tokens.shape, BF16),
            pltpu.VMEM(gains.shape, F32),
            pltpu.VMEM(offsets.shape, F32),
            pltpu.VMEM(w_keys.shape, BF16),
            pltpu.VMEM((span, table.shape[1]), F32),
            pltpu.SemaphoreType.DMA((5,)),
        ],
        compiler_params=pltpu.CompilerParams(vmem_limit_bytes=VMEM_LIMIT),
    )(tokens, gains, offsets, w_keys, table)


def make_queries(first, w_query, table, queries):
    raw = dot(first, w_query)
    span = table.shape[0]
    for start in range(0, raw.shape[0], span):
        for pair in range(PAIRS):
            lanes = slice(pair * PAIR, (pair + 1) * PAIR)
            queries[start : start + span, lanes] = rotate(raw[start : start + span, lanes], table[...]).astype(BF16)


def front_part(hidden, gains, offsets, table, w_query, w_in, queries, normed, second, waits):
    values = hidden.astype(F32)
    waits(0)
    unit, _ = standardize(values)
    first = (unit * gains[0, 0:1] + offsets[0, 0:1]).astype(BF16)
    feed = (unit * gains[0, 1:2] + offsets[0, 1:2]).astype(BF16)
    if normed is not None:
        normed[...] = first
        second[...] = feed
    waits(1)
    make_queries(first, w_query[...], table, queries)
    return values, feed


def pick(meta, mine, other):
    return jnp.where(meta[2] == 0, mine[...], other[...])


def front_body(save, block, meta, hidden_h, gains_h, offsets_h, table_h, w_query_h, w_in_h, *rest):
    if save:
        came_h, chosen, queries, normed, second, active, slope, *rest = rest
        hidden, gains, offsets, table, w_query, w_in, sems, came = rest
    else:
        w_back_h, queries, result, hidden, gains, offsets, table, w_query, w_in, w_back, sems = rest
        normed = second = None
    span = table.shape[0]
    inner = w_in.shape[1]

    def run():
        rows = pl.ds(pl.multiple_of(meta[0] * span, span), span)
        pairs = [
            (hidden_h, hidden),
            (gains_h, gains),
            (offsets_h, offsets),
            (w_query_h.at[0], w_query),
            (table_h.at[rows], table),
        ]
        for start in range(0, inner, block):
            lanes = pl.ds(start, block)
            pairs.append((w_in_h.at[0, :, lanes], w_in.at[:, lanes]))
            if not save:
                pairs.append((w_back_h.at[0, lanes, :], w_back.at[lanes, :]))
        if save:
            pairs.append((came_h, came))
        copies = fetch(sems, *pairs)

        def waits(stage):
            for copy in copies[1:3] if stage == 0 else copies[3:5]:
                copy.wait()

        copies[0].wait()
        flat = hidden[...].reshape(-1, hidden.shape[-1])
        if save:
            copies[-1].wait()
            flat = jnp.where(meta[2] == 0, flat, came[...])
            chosen[...] = flat
        values, feed = front_part(flat, gains, offsets, table, w_query, w_in, queries, normed, second, waits)
        if not save:
            result[...] = values
        each = 1 if save else 2
        for step in range(inner // block):
            lanes = slice(step * block, (step + 1) * block)
            copies[5 + each * step].wait()
            value, rate = gelu_parts(dot(feed, w_in[:, lanes]))
            value = value.astype(BF16)
            if save:
                active[:, lanes] = value
                slope[:, lanes] = rate.astype(BF16)
            else:
                copies[6 + each * step].wait()
                result[...] += dot(value, w_back[lanes, :])

    if save:
        run()
    else:
        pl.when(meta[2] == 0)(run)


def front(meta, hidden, gains, offsets, table, w_query, w_in, w_back=None, came=None):
    save = came is not None
    shape = hidden.shape
    width = shape[-1]
    rows = int(np.prod(shape[:-1]))
    span = rows // 2 if save else shape[-2]
    inner = w_in.shape[2]
    block = 768 if inner % 768 == 0 else inner
    operands = [hidden, gains, offsets, table, w_query, w_in, came if save else w_back]
    if save:
        outs = [(rows, width, BF16)] * 4 + [(rows, inner, BF16)] * 2
    else:
        outs = [(rows, width, BF16), (rows, width, F32)]
    scratch = [
        pltpu.VMEM(shape, BF16),
        pltpu.VMEM(gains.shape, F32),
        pltpu.VMEM(offsets.shape, F32),
        pltpu.VMEM((span, table.shape[1]), F32),
        pltpu.VMEM((width, width), BF16),
        pltpu.VMEM((width, inner), BF16),
    ]
    if not save:
        scratch.append(pltpu.VMEM((inner, width), BF16))
    scratch.append(pltpu.SemaphoreType.DMA((6 + (1 if save else 2) * (inner // block),)))
    if save:
        scratch.append(pltpu.VMEM(shape, BF16))
    return call(
        partial(front_body, save, block),
        (1,),
        [IN_HBM] * len(operands),
        [whole(out[:2]) for out in outs],
        [shape_of(*out) for out in outs],
        scratch,
    )(meta, *operands)


def spread_pair(values, low):
    lane = lax.broadcasted_iota(jnp.int32, values.shape, 1)
    here = lane < HEAD_DIM if low else lane >= HEAD_DIM
    turned = pltpu.roll(values.astype(F32), HEAD_DIM, 1).astype(BF16)
    one, two = (values, turned) if low else (turned, values)
    zero = jnp.zeros_like(values)
    return jnp.where(here, one, zero), jnp.where(here, two, zero)


def mask_rows(meta, span, length, seq_length, first_key=0):
    key = lax.broadcasted_iota(jnp.int32, (span, length), 1) + first_key
    query = lax.broadcasted_iota(jnp.int32, (span, length), 0) + meta[0] * span
    return jnp.where(key <= jnp.minimum(query, seq_length - 1), 0.0, MASKED)


GROUP = 4
QUARTERS = 4


def by_quarters(meta, span, length, seq_length, run):
    quarter = length // QUARTERS
    needed = jnp.minimum((meta[0] + 1) * span, seq_length)
    count = lax.div(needed + quarter - 1, quarter)
    for number in range(1, QUARTERS + 1):
        pl.when(count == number)(partial(run, number * quarter))


def value_sides(pairs):
    lane = lax.broadcasted_iota(jnp.int32, pairs.shape, 1)
    high = jnp.where(lane < HEAD_DIM, jnp.ones_like(pairs), pairs)
    return pltpu.roll(high.astype(F32), HEAD_DIM, 1).astype(BF16), high


def attend_rows(pairs, mask, stacked, mixed):
    span = mixed.shape[0]
    side = value_sides(pairs)[0]
    lane = lax.broadcasted_iota(jnp.int32, (span, PAIR), 1)
    for start in range(0, HEADS, GROUP):
        all_scores = dot_nt(stacked[start * span : (start + GROUP) * span], pairs)
        weights = []
        for head in range(start, start + GROUP):
            place = (head - start) * span
            scores = all_scores[place : place + span] + mask
            top = jnp.max(scores, axis=1, keepdims=True)
            weights.append(jnp.exp2((scores - top) * (SCALE * LOG2E)).astype(BF16))
        summed = dot(jnp.concatenate(weights, axis=0), side)
        summed = summed * pltpu.roll(1.0 / summed, HEAD_DIM, 1)
        for head in range(0, GROUP, 2):
            one = summed[head * span : (head + 1) * span]
            two = pltpu.roll(summed[(head + 1) * span : (head + 2) * span], HEAD_DIM, 1)
            lanes = slice((start + head) // 2 * PAIR, ((start + head) // 2 + 1) * PAIR)
            mixed[:, lanes] = jnp.where(lane < HEAD_DIM, one, two).astype(BF16)


def attend_body(batch, meta, queries, shared, w_out_h, base, result, mixed, stacked, mask, w_out, sems):
    seq = pl.program_id(0)
    span = queries.shape[0]
    length = mask.shape[1]
    seq_length = meta[4 + 2 * batch + seq]

    def run():
        @pl.when(seq == 0)
        def _():
            fetch(sems, (w_out_h.at[0], w_out))

        for pair in range(PAIRS):
            for side, value in enumerate(spread_pair(queries[:, pair * PAIR : (pair + 1) * PAIR], True)):
                stacked[(2 * pair + side) * span : (2 * pair + side + 1) * span] = value
        def some(keys):
            mask[:, :keys] = mask_rows(meta, span, keys, seq_length)
            pairs = shared[: keys // span, 0, 0].reshape(keys, PAIR)
            attend_rows(pairs, mask[:, :keys], stacked, mixed)

        by_quarters(meta, span, length, seq_length, some)

        @pl.when(seq == 0)
        def _():
            pltpu.make_async_copy(w_out_h.at[0], w_out, sems.at[0]).wait()

        result[...] = (base[...] + dot(mixed[...], w_out[...])).astype(BF16)

    pl.when(meta[2] == 0)(run)


def attend(batch, meta, queries, gathered, w_out, base):
    width = queries.shape[1]
    count, _, seqs, span, _ = gathered.shape
    rows = seqs * span
    length = count * span
    return call(
        partial(attend_body, batch),
        (seqs,),
        [
            pl.BlockSpec((span, width), lambda s, meta: (batch * seqs + s, 0)),
            pl.BlockSpec((count, 1, 1, span, PAIR), lambda s, meta: (0, batch, s, 0, 0)),
            IN_HBM,
            pl.BlockSpec((span, width), lambda s, meta: (batch * seqs + s, 0)),
        ],
        pl.BlockSpec((span, width), lambda s, meta: (s, 0)),
        jax.ShapeDtypeStruct((rows, width), BF16),
        [
            pltpu.VMEM((span, width), BF16),
            pltpu.VMEM((HEADS * span, PAIR), BF16),
            pltpu.VMEM((span, length), F32),
            pltpu.VMEM((width, width), BF16),
            pltpu.SemaphoreType.DMA((1,)),
        ],
    )(meta, queries, gathered, w_out, base)


def softmax_back(fresh, pairs, sides, mask, q_sides, d_sides, saved, first_head, weights_sc, d_scores_sc):
    span = q_sides[0].shape[0]
    count = len(q_sides)
    lane = lax.broadcasted_iota(jnp.int32, (span, PAIR), 1)
    products = dot_nt(jnp.concatenate(q_sides + d_sides, axis=0), pairs)
    for n in range(count):
        rows = slice(n * span, (n + 1) * span)
        here = lane == first_head + n
        scores = products[rows]
        d_weights = products[(count + n) * span : (count + n + 1) * span]
        if fresh:
            scores = scores + mask
            top = jnp.max(scores, axis=1, keepdims=True)
            weights = jnp.exp2((scores - top) * (SCALE * LOG2E))
            sums = jnp.sum(weights, axis=1, keepdims=True)
            weights = weights * (1.0 / sums)
            saved = jnp.where(here, top * (SCALE * LOG2E) + jnp.log2(sums), saved)
        else:
            norm = jnp.sum(jnp.where(here, saved, 0.0), axis=1, keepdims=True)
            weights = jnp.exp2(scores * (SCALE * LOG2E) + mask - norm)
        lean = jnp.sum(weights * d_weights, axis=1, keepdims=True)
        weights_sc[rows] = weights.astype(BF16)
        d_scores_sc[rows] = (weights * (d_weights - lean)).astype(BF16)
    return saved


def attend_back_part(fresh, seq_length, meta, rows, pairs, queries, d_mixed, table, norms, mixed, d_raw, mask_sc, weights_sc, d_scores_sc, total):
    span = table.shape[0]
    length = pairs.shape[0]
    lane = lax.broadcasted_iota(jnp.int32, (span, PAIR), 1)
    mask_sc[:, :length] = mask_rows(meta, span, length, seq_length)
    mask = mask_sc[:, :length]
    side = value_sides(pairs)[0] if fresh else None
    saved = jnp.zeros((span, PAIR), F32) if fresh else norms[rows]
    for number, first_head in enumerate(range(0, HEADS, GROUP)):
        q_sides, d_sides = [], []
        for pair in range(first_head // 2, (first_head + GROUP) // 2):
            lanes = slice(pair * PAIR, (pair + 1) * PAIR)
            q_sides += spread_pair(queries[rows, lanes], True)
            d_sides += spread_pair(d_mixed[rows, lanes], False)
        slot = number % 2
        weights = weights_sc.at[slot, :, :length]
        d_scores = d_scores_sc.at[slot, :, :length]
        saved = softmax_back(fresh, pairs, side, mask, q_sides, d_sides, saved, first_head, weights, d_scores)
        weights, d_scores = weights[...], d_scores[...]
        d_query = dot(d_scores, pairs)
        out = dot(weights, side) if fresh else None
        scaled = [(value.astype(F32) * SCALE).astype(BF16) for value in q_sides]
        part = dot_tn(
            jnp.concatenate([d_scores, weights], axis=0), jnp.concatenate(scaled + d_sides, axis=0)
        )
        if number == 0:
            total[:length] = part
        else:
            total[:length] += part
        for n in range(0, GROUP, 2):
            pair = (first_head + n) // 2
            lanes = slice(pair * PAIR, (pair + 1) * PAIR)

            def join(values):
                one = values[n * span : (n + 1) * span]
                two = values[(n + 1) * span : (n + 2) * span]
                return jnp.where(lane < HEAD_DIM, one, pltpu.roll(two, HEAD_DIM, 1))

            if fresh:
                mixed[rows, lanes] = join(out).astype(BF16)
            d_raw[rows, lanes] = rotate(join(d_query) * SCALE, table[...], -1.0).astype(BF16)
    if fresh:
        norms[rows] = saved


def attend_back_all(fresh, batch, meta, shared, d_shared, span, total, run):
    count, seqs = d_shared.shape[:2]
    length = count * span

    @pl.loop(0, seqs)
    def _(seq):
        rows = pl.ds(pl.multiple_of(seq * span, span), span)
        seq_length = meta[4 + 2 * batch + seq]

        def some(keys):
            pairs = shared[: keys // span, 0, pl.ds(seq, 1)].reshape(keys, PAIR)
            run(seq_length, rows, pairs)
            if keys < length:
                total[keys:] = jnp.zeros((length - keys, PAIR), F32)

        by_quarters(meta, span, length, seq_length, some)
        d_shared[:, pl.ds(seq, 1)] = total[...].astype(BF16).reshape(count, 1, span, PAIR)


def feed_back_part(upstream, slope, w_in, w_back, d_upper, block, waits):
    inner = slope.shape[1]
    two = None
    for step in range(inner // block):
        lanes = slice(step * block, (step + 1) * block)
        waits(step)
        rate = (dot_nt(upstream, w_back[lanes, :]) * slope[:, lanes].astype(F32)).astype(BF16)
        d_upper[:, lanes] = rate
        part = dot_nt(rate, w_in[:, lanes])
        two = part if two is None else two + part
    return two


def chain_body(front, which, block, meta, up, hid, *rest):
    if front:
        came, shared, offsets_h, *rest = rest
    else:
        back, queries, slope, shared, *rest = rest
    gains_h, table_h, w_query_h, w_out_h, w_in_h, w_back_h, *rest = rest
    if front:
        hidden, queries, normed, second, active, slope, *rest = rest
        hidden[...] = pick(meta, hid, came)
        upstream = up
    else:
        upstream, *rest = rest
        upstream[...] = pick(meta, back, up)
        hidden = hid
    mixed, norms, d_raw, d_shared, d_upper, d_hidden, d_low, d_norms, *rest = rest
    gains, table, w_query, w_out, w_in, w_back, d_mixed, mask_sc, weights_sc, d_scores_sc, total_sc, sems, *rest = rest
    span = table.shape[0]
    inner = slope.shape[1]
    steps = inner // block
    batch = which[0] + which[1] * meta[2]
    place = pl.ds(pl.multiple_of(meta[0] * span, span), span)
    operands = [(gains_h, gains), (w_query_h.at[0], w_query), (table_h.at[place], table), (w_out_h.at[0], w_out)]
    for start in range(0, inner, block):
        lanes = pl.ds(start, block)
        operands.append((w_in_h.at[0, :, lanes], w_in.at[:, lanes]))
    for start in range(0, inner, block):
        lanes = pl.ds(start, block)
        operands.append((w_back_h.at[0, lanes, :], w_back.at[lanes, :]))
    if front:
        offsets = rest[0]
        operands.append((offsets_h, offsets))
    copies = fetch(sems, *operands)
    if front:

        def waits(stage):
            for copy in (copies[0], copies[-1]) if stage == 0 else copies[1:3]:
                copy.wait()

        _, feed = front_part(hidden[...], gains, offsets, table, w_query, w_in, queries, normed, second, waits)
        for step in range(steps):
            lanes = slice(step * block, (step + 1) * block)
            copies[4 + step].wait()
            value, rate = gelu_parts(dot(feed, w_in[:, lanes]))
            active[:, lanes] = value.astype(BF16)
            slope[:, lanes] = rate.astype(BF16)
    else:
        copies[2].wait()
    copies[3].wait()
    d_mixed[...] = dot_nt(upstream[...], w_out[...]).astype(BF16)

    def run(seq_length, rows, pairs):
        attend_back_part(
            True, seq_length, meta, rows, pairs, queries, d_mixed, table, norms, mixed, d_raw,
            mask_sc, weights_sc, d_scores_sc, total_sc
        )

    attend_back_all(True, batch, meta, shared, d_shared, span, total_sc, run)

    def more_waits(step):
        if not front:
            copies[4 + step].wait()
        copies[4 + steps + step].wait()

    two = feed_back_part(upstream[...], slope, w_in, w_back, d_upper, block, more_waits)
    if not front:
        for copy in copies[:2]:
            copy.wait()
    one = dot_nt(d_raw[...], w_query[...])
    unit, scale = standardize(hidden[...].astype(F32))
    total = upstream[...].astype(F32) + norm_back(one * gains[0, 0:1] + two * gains[0, 1:2], 1.0, unit, scale)
    d_hidden[...] = total
    d_low[...] = total.astype(BF16)
    d_norms[...] = sum_rows(one * unit, one, two * unit, two)


def chain(which, meta, upstream, hidden, more, gathered, gains, offsets, table, w_query, w_out, w_in, w_back):
    rows, width = hidden.shape
    count, _, seqs, span, _ = gathered.shape
    inner = w_in.shape[2]
    length = count * span
    block = 768 if inner % 768 == 0 else inner
    front = len(more) == 1
    flat = whole((rows, width))
    shared_shape = (count, seqs, span, PAIR)
    shared_spec = pl.BlockSpec((count, 1, seqs, span, PAIR), lambda j, meta: (0, which[0] + which[1] * meta[2], 0, 0, 0))
    outs = [(rows, width, BF16)] * 4 + [(rows, inner, BF16)] * 2 if front else [(rows, width, BF16)]
    outs += [(rows, width, BF16), (rows, PAIR, F32), (rows, width, BF16), None, (rows, inner, BF16), (rows, width, F32), (rows, width, BF16), (8, width, F32)]
    if front:
        operands, specs = [upstream, hidden, *more, gathered, offsets], [flat, flat, flat, shared_spec, IN_HBM]
    else:
        operands = [upstream, hidden, *more, gathered]
        specs = [flat, flat, flat, flat, whole((rows, inner)), shared_spec]
    return call(
        partial(chain_body, front, which, block),
        (1,),
        specs + [IN_HBM] * 6,
        [whole(shared_shape) if out is None else whole(out[:2]) for out in outs],
        [jax.ShapeDtypeStruct(shared_shape, BF16) if out is None else shape_of(*out) for out in outs],
        [
            pltpu.VMEM(gains.shape, F32),
            pltpu.VMEM((span, table.shape[1]), F32),
            pltpu.VMEM((width, width), BF16),
            pltpu.VMEM((width, width), BF16),
            pltpu.VMEM((width, inner), BF16),
            pltpu.VMEM((inner, width), BF16),
            pltpu.VMEM((rows, width), BF16),
            pltpu.VMEM((span, length), F32),
            pltpu.VMEM((2, GROUP * span, length), BF16),
            pltpu.VMEM((2, GROUP * span, length), BF16),
            pltpu.VMEM((length, PAIR), F32),
            pltpu.SemaphoreType.DMA((5 + 2 * (inner // block),)),
        ]
        + ([pltpu.VMEM(offsets.shape, F32)] if front else []),
    )(meta, *operands, gains, table, w_query, w_out, w_in, w_back)


def attend_back_body(which, split, meta, upstream, queries, norms, shared, *rest):
    (up_d, raw_d, mixed_c, mixed_d, normed_c, normed_d, w_out_h, w_query_h, table_h) = rest[:9]
    (d_raw, d_shared, d_normed) = rest[9:12]
    halves = rest[12:14] if split else rest[12:13]
    (d_mixed, mask_sc, weights_sc, d_scores_sc, total_sc, table, w_out, w_query, sems) = rest[12 + len(halves) :][:9]
    span = table.shape[0]
    batch = which[0] + which[1] * meta[2]
    place = pl.ds(pl.multiple_of(meta[0] * span, span), span)
    copies = fetch(sems, (w_out_h.at[0], w_out), (table_h.at[place], table), (w_query_h.at[0], w_query))
    copies[0].wait()
    d_mixed[...] = dot_nt(upstream[...], w_out[...]).astype(BF16)
    copies[1].wait()

    def run(seq_length, rows, pairs):
        attend_back_part(
            False, seq_length, meta, rows, pairs, queries, d_mixed, table, norms, None, d_raw,
            mask_sc, weights_sc, d_scores_sc, total_sc
        )

    attend_back_all(False, batch, meta, shared, d_shared, span, total_sc, run)
    copies[2].wait()
    d_normed[...] = dot_nt(d_raw[...], w_query[...])
    both = jnp.concatenate([upstream[...], up_d[...]], axis=0)
    left = jnp.concatenate([mixed_c[...], mixed_d[...]], axis=0)
    outer = dot_tn(left, both).astype(BF16)
    both = jnp.concatenate([d_raw[...], raw_d[...]], axis=0)
    left = jnp.concatenate([normed_c[...], normed_d[...]], axis=0)
    query = dot_tn(left, both).astype(BF16)
    width = both.shape[1]
    if len(halves) == 1:
        halves[0][:, :width] = outer
        halves[0][:, width:] = query
        return
    keep, send, pair_sc = halves[0], halves[1], rest[-1]
    pair_sc[..., :width] = outer.reshape(pair_sc.shape[:3] + (width,))
    pair_sc[..., width:] = query.reshape(pair_sc.shape[:3] + (width,))
    keep[...] = pair_sc[:, pl.ds(meta[1], 1)].reshape(keep.shape)
    send[...] = pair_sc[:, pl.ds(1 - meta[1], 1)].reshape(send.shape)


def attend_back(
    which, shards, meta, upstream, queries, norms, gathered, up_d, raw_d, mixed_c, mixed_d, normed_c, normed_d, w_out, w_query, table,
    behind=()
):
    rows, width = queries.shape
    count, _, seqs, span, _ = gathered.shape
    length = count * span
    shared_shape = (count, seqs, span, PAIR)
    part = width // shards
    split = part % 16 == 0
    if split:
        pairs = [(shards // 2, part, 2 * width)] * 2
    else:
        pairs = [(width, 2 * width)]
    outs = call(
        partial(attend_back_body, which, split),
        (1,),
        [whole((rows, width))] * 2
        + [whole(norms.shape)]
        + [pl.BlockSpec((count, 1, seqs, span, PAIR), lambda j, meta: (0, which[0] + which[1] * meta[2], 0, 0, 0))]
        + [whole((rows, width))] * 6
        + [IN_HBM] * 3,
        [whole((rows, width)), whole(shared_shape), whole((rows, width))] + [whole(shape) for shape in pairs],
        [
            shape_of(rows, width, BF16),
            jax.ShapeDtypeStruct(shared_shape, BF16),
            shape_of(rows, width, F32),
        ]
        + [jax.ShapeDtypeStruct(shape, BF16) for shape in pairs],
        [
            pltpu.VMEM((rows, width), BF16),
            pltpu.VMEM((span, length), F32),
            pltpu.VMEM((2, GROUP * span, length), BF16),
            pltpu.VMEM((2, GROUP * span, length), BF16),
            pltpu.VMEM((length, PAIR), F32),
            pltpu.VMEM((span, table.shape[1]), F32),
            pltpu.VMEM((width, width), BF16),
            pltpu.VMEM((width, width), BF16),
            pltpu.SemaphoreType.DMA((3,)),
        ]
        + ([pltpu.VMEM((shards // 2, 2, part, 2 * width), BF16)] if split else []),
        behind=behind,
    )(meta, upstream, queries, norms, gathered, up_d, raw_d, mixed_c, mixed_d, normed_c, normed_d, w_out, w_query, table)
    if split:
        return outs
    return (*outs[:3], *split_cores(outs[3].reshape(shards, part, 2 * width)))


def finish_body(block, meta, *rest):
    hidden, mixed, active = rest[0:2], rest[2:4], rest[4:6]
    w_out_h, w_back_h, outs, w_out, w_back, sems = rest[6:]
    inner = w_back.shape[0]
    pairs = [(w_out_h.at[0], w_out)]
    for start in range(0, inner, block):
        pairs.append((w_back_h.at[0, pl.ds(start, block), :], w_back.at[pl.ds(start, block), :]))
    copies = fetch(sems, *pairs)
    rows = hidden[0].shape[0]

    def both(refs, lanes=slice(None)):
        return jnp.concatenate([refs[0][:, lanes], refs[1][:, lanes]], axis=0)

    copies[0].wait()
    total = both(hidden).astype(F32) + dot(both(mixed), w_out[...])
    for step in range(inner // block):
        lanes = slice(step * block, (step + 1) * block)
        copies[1 + step].wait()
        total += dot(both(active, lanes), w_back[lanes, :])
    section = meta[2]
    outs[pl.ds(1 - section, 1)] = total[:rows].astype(BF16)[None]
    outs[pl.ds(section, 1)] = total[rows:].astype(BF16)[None]


def finish(meta, hidden, mixed, active, w_out, w_back, behind=()):
    rows, width = hidden[0].shape
    inner = active[0].shape[1]
    block = 768 if inner % 768 == 0 else inner
    return call(
        partial(finish_body, block),
        (1,),
        [whole((rows, width))] * 4 + [whole((rows, inner))] * 2 + [IN_HBM] * 2,
        whole((2, rows, width)),
        jax.ShapeDtypeStruct((2, rows, width), BF16),
        [
            pltpu.VMEM((width, width), BF16),
            pltpu.VMEM((inner, width), BF16),
            pltpu.SemaphoreType.DMA((1 + inner // block,)),
        ],
        behind=behind,
    )(meta, *hidden, *mixed, *active, w_out, w_back)


def sum_rows(*values):
    sums = [jnp.sum(value, axis=0, keepdims=True) for value in values]
    return jnp.concatenate(sums + [jnp.zeros_like(sums[0])] * (8 - len(sums)), axis=0)


def feed_back_body(block, meta, upstream, slope, w_in_h, w_back_h, d_upper, d_second, w_in, w_back, sems):
    inner = slope.shape[1]
    operands = []
    for start in range(0, inner, block):
        lanes = pl.ds(start, block)
        operands.append((w_back_h.at[0, lanes, :], w_back.at[lanes, :]))
        operands.append((w_in_h.at[0, :, lanes], w_in.at[:, lanes]))
    copies = fetch(sems, *operands)

    def waits(step):
        copies[2 * step].wait()
        copies[2 * step + 1].wait()

    d_second[...] = feed_back_part(upstream[...], slope, w_in, w_back, d_upper, block, waits)


def feed_back(meta, upstream, slope, w_in, w_back):
    rows, width = upstream.shape
    inner = w_in.shape[2]
    block = 768 if inner % 768 == 0 else inner
    return call(
        partial(feed_back_body, block),
        (1,),
        [whole((rows, width)), whole((rows, inner))] + [IN_HBM] * 2,
        [whole((rows, inner)), whole((rows, width))],
        [shape_of(rows, inner, BF16), shape_of(rows, width, F32)],
        [
            pltpu.VMEM((width, inner), BF16),
            pltpu.VMEM((inner, width), BF16),
            pltpu.SemaphoreType.DMA((2 * (inner // block),)),
        ],
    )(meta, upstream, slope, w_in, w_back)


def store_halves(meta, block, keep, send, scratch):
    groups, _, part, lanes = scratch.shape
    scratch[...] = block.astype(BF16).reshape(groups, 2, part, lanes)
    core = meta[1]
    keep[...] = scratch[:, pl.ds(core, 1)].reshape(keep.shape)
    send[...] = scratch[:, pl.ds(1 - core, 1)].reshape(send.shape)


def late_feed_body(shards, block, meta, active_c, active_d, up, back, up_d, slope, *rest):
    w_in_h, w_back_h, keep, send, d_upper, d_second, up_c, w_in, w_back, scratch, sems = rest
    up_c[...] = pick(meta, back, up)
    inner = w_in.shape[1]
    operands = []
    for start in range(0, inner, block):
        lanes = pl.ds(start, block)
        operands.append((w_back_h.at[0, lanes, :], w_back.at[lanes, :]))
        operands.append((w_in_h.at[0, :, lanes], w_in.at[:, lanes]))
    copies = fetch(sems, *operands)
    part = inner // shards
    both = jnp.concatenate([up_c[...], up_d[...]], axis=0)
    for group in range(shards // 2):
        lanes = slice(group * 2 * part, (group + 1) * 2 * part)
        left = jnp.concatenate([active_c[:, lanes], active_d[:, lanes]], axis=0)
        scratch[group] = dot_tn(left, both).astype(BF16).reshape(2, part, both.shape[1])
    core = meta[1]
    keep[...] = scratch[:, pl.ds(core, 1)].reshape(keep.shape)
    send[...] = scratch[:, pl.ds(1 - core, 1)].reshape(send.shape)

    def waits(step):
        copies[2 * step].wait()
        copies[2 * step + 1].wait()

    d_second[...] = feed_back_part(up_c[...], slope, w_in, w_back, d_upper, block, waits)


def late_feed(meta, shards, active_c, active_d, up, back, up_d, slope, w_in, w_back, behind=()):
    rows, width = up.shape
    inner = w_in.shape[2]
    part = inner // shards
    if part % 64:
        up_c = jnp.where(meta[2] == 0, back, up)
        halves = weights_full(meta, shards, active_c, active_d, up_c, up_d)
        return (*halves, *feed_back(meta, up_c, slope, w_in, w_back), up_c)
    block = 768 if inner % 768 == 0 else inner
    half = (shards // 2, part, width)
    return call(
        partial(late_feed_body, shards, block),
        (1,),
        [whole((rows, inner))] * 2 + [whole((rows, width))] * 3 + [whole((rows, inner))] + [IN_HBM] * 2,
        [whole(half), whole(half), whole((rows, inner)), whole((rows, width)), whole((rows, width))],
        [jax.ShapeDtypeStruct(half, BF16)] * 2 + [shape_of(rows, inner, BF16), shape_of(rows, width, F32), shape_of(rows, width, BF16)],
        [
            pltpu.VMEM((width, inner), BF16),
            pltpu.VMEM((inner, width), BF16),
            pltpu.VMEM((shards // 2, 2, part, width), BF16),
            pltpu.SemaphoreType.DMA((2 * (inner // block),)),
        ],
        behind=behind,
    )(meta, active_c, active_d, up, back, up_d, slope, w_in, w_back)


def weights_full_body(meta, left_c, left_d, right_c, right_d, full, turned_c, turned_d):
    @pl.when(pl.program_id(0) == 0)
    def _():
        turned_c[...] = left_c[...].T
        turned_d[...] = left_d[...].T

    block = dot(turned_c[...], right_c[...]) + dot(turned_d[...], right_d[...])
    full[...] = block.astype(BF16)


def weights_full(meta, shards, left_c, left_d, right_c, right_d):
    rows, tall = left_c.shape
    wide = right_c.shape[1]
    block = 256
    full = call(
        weights_full_body,
        (wide // block,),
        [whole((rows, tall))] * 2 + [pl.BlockSpec((rows, block), lambda j, meta: (0, j))] * 2,
        pl.BlockSpec((tall, block), lambda j, meta: (0, j)),
        jax.ShapeDtypeStruct((tall, wide), BF16),
        [pltpu.VMEM((tall, rows), BF16), pltpu.VMEM((tall, rows), BF16)],
    )(meta, left_c, left_d, right_c, right_d)
    return split_cores(full.reshape(shards, tall // shards, wide))


def weights_wide_body(meta, left_c, left_d, right_c, right_d, keep, send, scratch, turned_c, turned_d):
    @pl.when(pl.program_id(0) == 0)
    def _():
        turned_c[...] = left_c[...].T
        turned_d[...] = left_d[...].T

    block = dot(turned_c[...], right_c[...]) + dot(turned_d[...], right_d[...])
    store_halves(meta, block, keep, send, scratch)


def weights_wide(meta, shards, left_c, left_d, right_c, right_d):
    rows, tall = left_c.shape
    wide = right_c.shape[1]
    block = min(512, wide) if wide % 512 == 0 else 384
    part = tall // shards
    if part % 16:
        return weights_full(meta, shards, left_c, left_d, right_c, right_d)
    spec = pl.BlockSpec((shards // 2, part, block), lambda j, meta: (0, 0, j))
    shape = jax.ShapeDtypeStruct((shards // 2, part, wide), BF16)
    return call(
        weights_wide_body,
        (wide // block,),
        [whole((rows, tall))] * 2 + [pl.BlockSpec((rows, block), lambda j, meta: (0, j))] * 2,
        [spec, spec],
        [shape, shape],
        [
            pltpu.VMEM((shards // 2, 2, part, block), BF16),
            pltpu.VMEM((tall, rows), BF16),
            pltpu.VMEM((tall, rows), BF16),
        ],
    )(meta, left_c, left_d, right_c, right_d)


def tail_body(
    meta, own_d, own_c, other, hid_d, hid_c, nrm_d, nrm_c, dh_d, sums_d, up_c, one_c, two_c,
    gains_h, w_keys_h, table_h, grads, *rest
):
    small, (gains, w_keys, table, sems) = rest[:2], rest[2:6]
    section = meta[2]
    first = (section == 0).astype(F32)
    span = table.shape[0]
    seqs = own_d.shape[0]
    rows = pl.ds(pl.multiple_of(meta[0] * span, span), span)
    copies = fetch(sems, (gains_h, gains), (w_keys_h, w_keys), (table_h.at[rows], table))
    for copy in copies:
        copy.wait()
    keys_sum = None
    norm_sum = sums_d[...]
    for slot, (own, hidden, normed) in enumerate(((own_d, hid_d, nrm_d), (own_c, hid_c, nrm_c))):
        raw = []
        for seq in range(seqs):
            both = (own[seq].astype(F32) + other[1 - slot, seq].astype(F32)) * first
            raw.append(rotate_keys(both, table[...], -1.0).astype(BF16))
        raw = jnp.concatenate(raw, axis=0)
        part = dot_tn(normed[...], raw)
        keys_sum = part if keys_sum is None else keys_sum + part
        one = dot_nt(raw, w_keys[...])
        unit, scale = standardize(hidden[...].astype(F32))
        if slot == 0:
            total = dh_d[...] + norm_back(one, gains[0, 0:1], unit, scale)
            norm_sum += sum_rows(one * unit, one)
        else:
            one, two = one + one_c[...], two_c[...]
            total = up_c[...].astype(F32) + norm_back(one * gains[0, 0:1] + two * gains[0, 1:2], 1.0, unit, scale)
            norm_sum += sum_rows(one * unit, one, two * unit, two)
        batch = section if slot == 0 else 1 - section
        grads[pl.ds(batch, 1)] = total[None]
    if len(rest) == 6:
        small[0][...] = keys_sum.astype(BF16)
        small[1][...] = norm_sum
        return
    gather = rest[6]
    groups, _, part, _ = gather.shape
    share = part // 2
    width = keys_sum.shape[0]
    turned = jnp.concatenate([norm_sum, jnp.zeros((PAIR - 8, width), F32)], axis=0).T
    for shard in range(2 * groups):
        place = gather.at[shard // 2, shard % 2]
        for half in range(2):
            start = half * width // 2 + shard * share
            place[half * share : (half + 1) * share, :PAIR] = keys_sum[start : start + share]
        place[:, PAIR:] = turned[shard * part : (shard + 1) * part]
    small[0][...] = gather[:, pl.ds(meta[1], 1)].reshape(small[0].shape).astype(BF16)
    small[1][...] = gather[:, pl.ds(1 - meta[1], 1)].reshape(small[1].shape).astype(BF16)


def small_parts(shards, sections, d_keys, d_norms):
    width = d_keys.shape[0]
    share = width // (sections * shards)
    d_keys = d_keys.reshape(sections, shards, share, PAIR).transpose(1, 0, 2, 3).reshape(shards, sections * share, PAIR)
    d_norms = d_norms.T.reshape(shards, width // shards, 8)
    d_norms = jnp.pad(d_norms, ((0, 0), (0, 0), (0, PAIR - 8))).astype(BF16)
    return split_cores(jnp.concatenate([d_keys, d_norms], axis=-1))


def tail(shards, sections, meta, *arrays, behind=()):
    rows, width = arrays[3].shape
    span = arrays[0].shape[1]
    gains, w_keys, table = arrays[-3:]
    part = width // shards
    split = part % 16 == 0 and sections == 2
    if split:
        outs = [jax.ShapeDtypeStruct((shards // 2, part, 2 * PAIR), BF16)] * 2
    else:
        outs = [shape_of(width, PAIR, BF16), shape_of(8, width, F32)]
    grads, *small = call(
        tail_body,
        (1,),
        [whole(array.shape) for array in arrays[:-3]] + [IN_HBM] * 3,
        [whole((2, rows, width))] + [whole(out.shape) for out in outs],
        [jax.ShapeDtypeStruct((2, rows, width), F32)] + outs,
        [
            pltpu.VMEM(gains.shape, F32),
            pltpu.VMEM(w_keys.shape, BF16),
            pltpu.VMEM((span, table.shape[1]), F32),
            pltpu.SemaphoreType.DMA((3,)),
        ]
        + ([pltpu.VMEM((shards // 2, 2, part, 2 * PAIR), F32)] if split else []),
        behind=behind,
    )(meta, *arrays)
    return (grads, *small) if split else (grads, *small_parts(shards, sections, *small))


def swap(value, axis, bit):
    count = lax.axis_size(axis)
    return lax.ppermute(value, axis, [(source, source ^ bit) for source in range(count)])


def across(value, steps):
    pairs = [(0, 1)] if steps > 0 else [(1, 0)]
    return lax.ppermute(value, "section", pairs)


def after(value, *others):
    return lax.optimization_barrier((value, *others))[0]


def wide_sum(values):
    total = values[0].astype(F32)
    for value in values[1:]:
        total = total + value.astype(F32)
    return total


class Halving:
    def __init__(self, *parts):
        self.parts = list(parts)

    def prepare(self, axis, bit, low, *hold):
        cut = []
        for value in self.parts:
            places = value.shape[0]
            cut.append(value.reshape(((places // 2, 2) if low else (2, places // 2)) + value.shape[1:]))
        if hold:
            cut[0] = after(cut[0], *hold)
        place = 1 if low else 0
        mine = (lax.axis_index(axis) // bit) % 2
        other = wide_sum([lax.dynamic_index_in_dim(value, 1 - mine, place, keepdims=False) for value in cut])
        self.sent = other.astype(BF16)
        self.parts = [lax.dynamic_index_in_dim(value, mine, place, keepdims=False) for value in cut]
        self.way = (axis, bit)

    def launch(self, *hold):
        if hold:
            self.sent = after(self.sent, *hold)
        self.parts.append(swap(self.sent, *self.way))

    @property
    def received(self):
        return self.parts[-1]

    def bits(self, axis):
        count = lax.axis_size(axis)
        found = [1 << n for n in range(1 if axis == "ctx" else 0, count.bit_length() - 1)]
        return [(axis, bit, axis == "ctx") for bit in (found if axis == "ctx" else found[::-1])]

    def along(self, steps, hold=(), held=()):
        for step in steps:
            self.prepare(*step, *hold)
            self.launch(*held)
            hold, held = (), ()

    def result(self):
        return wide_sum([value.reshape(value.shape[1:]) for value in self.parts])


def split_cores(value):
    shards, part, lanes = value.shape
    cut = value.reshape(shards // 2, 2, part, lanes)
    core = lax.axis_index("ctx") % 2
    return (
        lax.dynamic_index_in_dim(cut, core, 1, keepdims=False),
        lax.dynamic_index_in_dim(cut, 1 - core, 1, keepdims=False),
    )


def per_device(
    length, tokens, lengths, norm_gains, norm_offsets, w_query, w_keys, w_out, w_in, w_back, cotangent
):
    batches, seqs, span, width = tokens.shape
    rows = seqs * span
    shards = lax.axis_size("dp") * lax.axis_size("ctx")
    section = lax.axis_index("section")
    place = lax.axis_index("ctx")
    first = section == 0
    table = jnp.asarray(rotary_table(length))

    own = make_keys(tokens, norm_gains, norm_offsets, w_keys, table)
    gathered = lax.all_gather(own, "ctx")
    meta = jnp.concatenate(
        [jnp.stack([place, place % 2, section, section]).astype(jnp.int32), lengths.reshape(-1)]
    )
    queries, base = front(meta, tokens, norm_gains, norm_offsets, table, w_query, w_in, w_back)
    came_a = across(attend(0, meta, queries, gathered, w_out, base), 1)
    came_b = across(attend(1, meta, queries, gathered, w_out, base), 1)
    gathered = lax.all_gather(jnp.where(first, own, across(own, 1)), "ctx")

    flat = tokens.reshape(batches, rows, width)
    cot = cotangent.reshape(batches, rows, width)

    def chain_of(which, upstream, hidden, *more):
        return chain(
            which, meta, upstream, hidden, more, gathered, norm_gains, norm_offsets, table, w_query, w_out, w_in, w_back
        )

    hid_c, queries_c, normed_c, second_c, active_c, slope_c, mixed_c, norms_c, _, ds_one, _, _, low_one, _ = chain_of(
        PASS_C, cot[0], flat[1], came_a
    )
    back_d = across(low_one, -1)
    early_c = lax.psum_scatter(ds_one, "ctx", scatter_dimension=0)
    hid_d, queries_d, normed_d, second_d, active_d, slope_d = front(
        meta, flat[0], norm_gains, norm_offsets, table, w_query, w_in, came=came_b
    )
    up_d, mixed_d, _, raw_d, ds_d, upper_d, dh_d, low_d, sums_d = chain_of(
        PASS_D, cot[1], hid_d, back_d, queries_d, slope_d
    )
    back_c = across(low_d, -1)
    early_d = Halving(after(ds_d, low_d))
    early_d.prepare("ctx", 1, True)
    early_d.launch()
    early_d.along(early_d.bits("ctx"))

    keep, send, upper_c, two_c, up_c = late_feed(
        meta, shards, active_c, active_d, cot[0], back_c, up_d, slope_c, w_in, w_back, behind=(early_c, early_d.sent)
    )
    early_d = early_d.result().astype(BF16)
    back = Halving(keep, swap(send, "ctx", 1))
    groups, depth = back.bits("dp"), back.bits("ctx")
    keep, send = weights_wide(meta, shards, second_c, second_d, upper_c, upper_d)
    inner = Halving(keep, swap(send, "ctx", 1))
    back.prepare(*groups[0], keep)
    back.launch()
    inner.prepare(*depth[0], back.sent)
    inner.launch()
    _, ds_c, one_c, keep, send = attend_back(
        PASS_C, shards, meta, up_c, queries_c, norms_c, gathered, up_d, raw_d, mixed_c, mixed_d,
        normed_c, normed_d, w_out, w_query, table, behind=(back.sent, inner.sent)
    )
    late = Halving(ds_c)
    late.prepare("ctx", 1, True)
    late.launch()
    pair = Halving(keep, swap(send, "ctx", 1))
    back.along(groups[1:])
    back.prepare(*depth[0], one_c)
    inner.prepare(*depth[1], one_c)
    late.prepare(*depth[0], back.sent, inner.sent)
    late.launch()
    pair.prepare(*groups[0], late.sent)
    pair.launch()
    late.along(depth[1:], hold=(pair.sent,))
    back.launch(late.sent)
    inner.launch(late.sent)
    other_keys = across(jnp.stack([early_d, early_c]), -1)
    sections = lax.axis_size("section")
    late = late.result().astype(BF16)
    input_grads, keep, send = tail(
        shards, sections, meta, early_d, late, other_keys, hid_d, hid_c, normed_d, normed_c, dh_d, sums_d, up_c, one_c, two_c,
        norm_gains, w_keys, table, behind=(back.sent, inner.sent, pair.sent)
    )
    small = Halving(keep, swap(send, "ctx", 1))
    outs = finish(
        meta, (hid_c, hid_d), (mixed_c, mixed_d), (active_c, active_d), w_out, w_back, behind=(keep,)
    )
    pair.along(groups[1:])
    back.prepare(*depth[1], outs)
    inner.prepare(*(depth[2:] + groups)[0], outs)
    pair.prepare(*depth[0], outs)
    back.launch()
    inner.launch(back.sent)
    pair.launch(inner.sent)
    small.along(groups, hold=(back.sent, inner.sent, pair.sent))
    pair.along(depth[1:], hold=(small.sent,))
    back.along(depth[2:])
    inner.along((depth[2:] + groups)[1:])
    small.along(depth[:1], hold=(pair.sent,))
    grad_back = after(back.result(), small.sent)
    grad_in = after(inner.result(), grad_back)
    small.along(depth[1:], hold=(grad_in,))
    small = small.result()
    pair = pair.result()
    share = width // (sections * shards)
    grad_norms = small[:, PAIR : PAIR + 4]
    keys_both = small[:, :PAIR].reshape(sections, share, PAIR)
    grad_keys = jnp.where(first, keys_both[0], across(keys_both[1], 1))
    return (
        outs.reshape((1,) + tokens.shape),
        input_grads.reshape((1,) + tokens.shape),
        grad_norms[None],
        pair[None, :, width:],
        grad_keys,
        pair[None, :, :width],
        grad_in[None],
        grad_back[None],
    )


def solution(mesh):
    def run(*arrays):
        length = arrays[0].shape[2]
        return jax.shard_map(
            partial(per_device, length),
            mesh=mesh,
            in_specs=(
                P(None, "dp", "ctx", None),
                P(None, "dp"),
                P("section", None, None),
                P("section", None, None),
                P("section", None, None),
                P(),
                P("section", None, None),
                P("section", None, None),
                P("section", None, None),
                P(None, "dp", "ctx", None),
            ),
            out_specs=(
                P("section", None, "dp", "ctx", None),
                P("section", None, "dp", "ctx", None),
                P("section", ("dp", "ctx"), None),
                P("section", ("dp", "ctx"), None),
                P(("section", "dp", "ctx"), None),
                P("section", ("dp", "ctx"), None),
                P("section", ("dp", "ctx"), None),
                P("section", ("dp", "ctx"), None),
            ),
            check_vma=False,
        )(*arrays)

    return run
```

```python
from functools import partial

import jax
import jax.numpy as jnp
import numpy as np
from jax import lax
from jax.experimental import pallas as pl
from jax.experimental.pallas import tpu as pltpu
from jax.sharding import PartitionSpec as P

HEADS = 12
HEAD_DIM = 64
ROT = 16
PAIR = 2 * HEAD_DIM
PAIRS = HEADS // 2
LOG2E = 1.4426950408889634
SCALE = HEAD_DIM**-0.5
MASKED = -1e30
F32 = jnp.float32
BF16 = jnp.bfloat16
VMEM_LIMIT = 60 * 1024 * 1024
FLOPS = 1_000_000

PASS_C = (1, -1)
PASS_D = (0, 1)


def dot(left, right):
    return jnp.dot(left, right, preferred_element_type=F32)


def dot_nt(left, right, **kwargs):
    return lax.dot_general(left, right, (((1,), (1,)), ((), ())), preferred_element_type=F32, **kwargs)


def dot_tn(left, right):
    return lax.dot_general(left, right, (((0,), (0,)), ((), ())), preferred_element_type=F32)


def whole(shape):
    zeros = (0,) * len(shape)
    return pl.BlockSpec(shape, lambda *_: zeros)


def call(body, grid, in_specs, out_specs, out_shape, scratch=(), behind=(), pushed=()):
    count, hidden = len(in_specs), len(behind)
    in_specs = list(in_specs) + [IN_HBM] * hidden
    scratch = list(scratch)
    if pushed:
        out_specs = [IN_HBM if n in pushed else spec for n, spec in enumerate(out_specs)]
        scratch += [pltpu.VMEM(out_shape[n].shape, out_shape[n].dtype) for n in pushed]
        scratch.append(pltpu.SemaphoreType.DMA((len(pushed),)))

    def run(meta, *refs):
        ins, refs = refs[:count], refs[count + hidden :]
        if not pushed:
            body(meta, *ins, *refs)
            return
        outs, own = list(refs[: len(out_shape)]), refs[len(out_shape) :]
        own, places, sems = own[: -1 - len(pushed)], own[-1 - len(pushed) : -1], own[-1]
        copies = {}
        for place, (number, local) in enumerate(zip(pushed, places)):
            copies[id(local)] = pltpu.make_async_copy(local, outs[number], sems.at[place])
            outs[number] = local
        waiting = []

        def push(*locals_):
            for local in locals_:
                copies[id(local)].start()
                waiting.append(copies[id(local)])

        body(meta, *ins, *outs, *own, push=push)
        for copy in waiting:
            copy.wait()

    made = pl.pallas_call(
        run,
        grid_spec=pltpu.PrefetchScalarGridSpec(
            num_scalar_prefetch=1,
            grid=grid,
            in_specs=in_specs,
            out_specs=out_specs,
            scratch_shapes=scratch,
        ),
        out_shape=out_shape,
        compiler_params=pltpu.CompilerParams(vmem_limit_bytes=VMEM_LIMIT),
        cost_estimate=pl.CostEstimate(flops=FLOPS, bytes_accessed=0, transcendentals=0),
    )
    return lambda *operands: made(*operands, *behind)


IN_HBM = pl.BlockSpec(memory_space=pltpu.HBM)


def fetch(sems, *pairs):
    copies = [pltpu.make_async_copy(source, target, sems.at[n]) for n, (source, target) in enumerate(pairs)]
    for copy in copies:
        copy.start()
    return copies


def shape_of(rows, columns, dtype):
    return jax.ShapeDtypeStruct((rows, columns), dtype)


def rotary_table(length):
    half = ROT // 2
    inverse = 10000.0 ** (-np.arange(half) * (2.0 / ROT))
    angles = np.arange(length)[:, None] * inverse[None, :]
    cosine, sine = np.cos(angles), np.sin(angles)
    table = np.zeros((length, 3, 2, HEAD_DIM), np.float32)
    table[:, 0] = 1.0
    table[:, 0, :, :half] = cosine[:, None]
    table[:, 0, :, half:ROT] = cosine[:, None]
    table[:, 1, :, :half] = -sine[:, None]
    table[:, 2, :, half:ROT] = sine[:, None]
    return table.reshape(length, 3 * PAIR)


def rotate(values, table, sign=1.0):
    around = pltpu.roll(values, PAIR - ROT // 2, 1) * table[:, PAIR : 2 * PAIR]
    around = around + pltpu.roll(values, ROT // 2, 1) * table[:, 2 * PAIR :]
    return values * table[:, :PAIR] + (around if sign > 0 else -around)


def rotate_keys(values, table, sign=1.0):
    lane = lax.broadcasted_iota(jnp.int32, values.shape, 1)
    return jnp.where(lane < HEAD_DIM, rotate(values, table, sign), values)


def standardize(values):
    center = values - jnp.mean(values, axis=-1, keepdims=True)
    scale = lax.rsqrt(jnp.mean(center * center, axis=-1, keepdims=True) + 1e-05)
    return center * scale, scale


def norm_back(grads, gain, normed, scale):
    inner = grads * gain
    lean = jnp.mean(inner, axis=-1, keepdims=True)
    along = jnp.mean(inner * normed, axis=-1, keepdims=True)
    return scale * (inner - lean - normed * along)


def gelu_parts(values):
    size = jnp.abs(values) * 0.7071067811865476
    base = 1.0 + 0.3275911 * size
    turn = pl.reciprocal(base, approx=True)
    turn = turn * (2.0 - base * turn)
    bell = jnp.exp2(values * values * (-0.5 * LOG2E))
    tail = turn * (
        0.127414796 + turn * (-0.142248368 + turn * (0.7107068705 + turn * (-0.7265760135 + turn * 0.5307027145)))
    )
    tail = tail * bell
    share = jnp.where(values >= 0.0, 1.0 - tail, tail)
    return values * share, share + values * (bell * 0.3989422804014327)


def keys_body(tokens_h, gains_h, offsets_h, w_keys_h, table_h, shared, tokens, gains, offsets, w_keys, table, sems):
    span = table.shape[0]
    rows = pl.ds(pl.multiple_of(lax.axis_index("ctx") * span, span), span)
    copies = fetch(
        sems,
        (tokens_h, tokens),
        (gains_h, gains),
        (offsets_h, offsets),
        (w_keys_h, w_keys),
        (table_h.at[rows], table),
    )
    for copy in copies:
        copy.wait()
    batches, seqs, _, width = tokens.shape
    normed, _ = standardize(tokens[...].reshape(-1, width).astype(F32))
    normed = (normed * gains[0, 0:1] + offsets[0, 0:1]).astype(BF16)
    raw = dot(normed, w_keys[...])
    for batch in range(batches):
        for seq in range(seqs):
            start = (batch * seqs + seq) * span
            shared[batch, seq] = rotate_keys(raw[start : start + span], table[...]).astype(BF16)


def make_keys(tokens, gains, offsets, w_keys, table):
    batches, seqs, span, width = tokens.shape
    return pl.pallas_call(
        keys_body,
        in_specs=[IN_HBM] * 5,
        out_specs=pl.BlockSpec(memory_space=pltpu.VMEM),
        out_shape=jax.ShapeDtypeStruct((batches, seqs, span, PAIR), BF16),
        scratch_shapes=[
            pltpu.VMEM(tokens.shape, BF16),
            pltpu.VMEM(gains.shape, F32),
            pltpu.VMEM(offsets.shape, F32),
            pltpu.VMEM(w_keys.shape, BF16),
            pltpu.VMEM((span, table.shape[1]), F32),
            pltpu.SemaphoreType.DMA((5,)),
        ],
        compiler_params=pltpu.CompilerParams(vmem_limit_bytes=VMEM_LIMIT),
    )(tokens, gains, offsets, w_keys, table)


def choose_body(meta, mine, other, out):
    out[...] = pick(meta, mine, other)


def choose(meta, mine, other, behind):
    return call(
        choose_body, (1,), [whole(mine.shape)] * 2, whole(mine.shape), jax.ShapeDtypeStruct(mine.shape, mine.dtype), behind=behind
    )(meta, mine, other)


def make_queries(first, w_query, table, queries):
    raw = dot(first, w_query)
    span = table.shape[0]
    for start in range(0, raw.shape[0], span):
        for pair in range(PAIRS):
            lanes = slice(pair * PAIR, (pair + 1) * PAIR)
            queries[start : start + span, lanes] = rotate(raw[start : start + span, lanes], table[...]).astype(BF16)


def front_part(hidden, gains, offsets, table, w_query, w_in, queries, normed, second, waits):
    values = hidden.astype(F32)
    waits(0)
    unit, _ = standardize(values)
    first = (unit * gains[0, 0:1] + offsets[0, 0:1]).astype(BF16)
    feed = (unit * gains[0, 1:2] + offsets[0, 1:2]).astype(BF16)
    if normed is not None:
        normed[...] = first
        second[...] = feed
    waits(1)
    make_queries(first, w_query[...], table, queries)
    return values, feed


def pick(meta, mine, other):
    return jnp.where(meta[2] == 0, mine[...], other[...])


def front_body(save, block, meta, hidden_h, gains_h, offsets_h, table_h, w_query_h, w_in_h, *rest):
    if save:
        came_h, chosen, queries, normed, second, active, slope, *rest = rest
        hidden, gains, offsets, table, w_query, w_in, sems, came = rest
    else:
        w_back_h, queries, result, hidden, gains, offsets, table, w_query, w_in, w_back, sems = rest
        normed = second = None
    span = table.shape[0]
    inner = w_in.shape[1]

    def run():
        rows = pl.ds(pl.multiple_of(meta[0] * span, span), span)
        pairs = [
            (hidden_h, hidden),
            (gains_h, gains),
            (offsets_h, offsets),
            (w_query_h.at[0], w_query),
            (table_h.at[rows], table),
        ]
        for start in range(0, inner, block):
            lanes = pl.ds(start, block)
            pairs.append((w_in_h.at[0, :, lanes], w_in.at[:, lanes]))
            if not save:
                pairs.append((w_back_h.at[0, lanes, :], w_back.at[lanes, :]))
        if save:
            pairs.append((came_h, came))
        copies = fetch(sems, *pairs)

        def waits(stage):
            for copy in copies[1:3] if stage == 0 else copies[3:5]:
                copy.wait()

        copies[0].wait()
        flat = hidden[...].reshape(-1, hidden.shape[-1])
        if save:
            copies[-1].wait()
            flat = jnp.where(meta[2] == 0, flat, came[...])
            chosen[...] = flat
        values, feed = front_part(flat, gains, offsets, table, w_query, w_in, queries, normed, second, waits)
        if not save:
            result[...] = values
        each = 1 if save else 2
        for step in range(inner // block):
            lanes = slice(step * block, (step + 1) * block)
            copies[5 + each * step].wait()
            value, rate = gelu_parts(dot(feed, w_in[:, lanes]))
            value = value.astype(BF16)
            if save:
                active[:, lanes] = value
                slope[:, lanes] = rate.astype(BF16)
            else:
                copies[6 + each * step].wait()
                result[...] += dot(value, w_back[lanes, :])

    if save:
        run()
    else:
        pl.when(meta[2] == 0)(run)


def front(meta, hidden, gains, offsets, table, w_query, w_in, w_back=None, came=None):
    save = came is not None
    shape = hidden.shape
    width = shape[-1]
    rows = int(np.prod(shape[:-1]))
    span = rows // 2 if save else shape[-2]
    inner = w_in.shape[2]
    block = 768 if inner % 768 == 0 else inner
    operands = [hidden, gains, offsets, table, w_query, w_in, came if save else w_back]
    if save:
        outs = [(rows, width, BF16)] * 4 + [(rows, inner, BF16)] * 2
    else:
        outs = [(rows, width, BF16), (rows, width, F32)]
    scratch = [
        pltpu.VMEM(shape, BF16),
        pltpu.VMEM(gains.shape, F32),
        pltpu.VMEM(offsets.shape, F32),
        pltpu.VMEM((span, table.shape[1]), F32),
        pltpu.VMEM((width, width), BF16),
        pltpu.VMEM((width, inner), BF16),
    ]
    if not save:
        scratch.append(pltpu.VMEM((inner, width), BF16))
    scratch.append(pltpu.SemaphoreType.DMA((6 + (1 if save else 2) * (inner // block),)))
    if save:
        scratch.append(pltpu.VMEM(shape, BF16))
    return call(
        partial(front_body, save, block),
        (1,),
        [IN_HBM] * len(operands),
        [whole(out[:2]) for out in outs],
        [shape_of(*out) for out in outs],
        scratch,
    )(meta, *operands)


def spread_pair(values, low):
    lane = lax.broadcasted_iota(jnp.int32, values.shape, 1)
    here = lane < HEAD_DIM if low else lane >= HEAD_DIM
    turned = pltpu.roll(values.astype(F32), HEAD_DIM, 1).astype(BF16)
    one, two = (values, turned) if low else (turned, values)
    zero = jnp.zeros_like(values)
    return jnp.where(here, one, zero), jnp.where(here, two, zero)


def mask_rows(meta, span, length, seq_length, first_key=0):
    key = lax.broadcasted_iota(jnp.int32, (span, length), 1) + first_key
    query = lax.broadcasted_iota(jnp.int32, (span, length), 0) + meta[0] * span
    return jnp.where(key <= jnp.minimum(query, seq_length - 1), 0.0, MASKED)


GROUP = 4
QUARTERS = 4


def by_quarters(meta, span, length, seq_length, run):
    quarter = length // QUARTERS
    needed = jnp.minimum((meta[0] + 1) * span, seq_length)
    count = lax.div(needed + quarter - 1, quarter)
    for number in range(1, QUARTERS + 1):
        pl.when(count == number)(partial(run, number * quarter))


def value_sides(pairs):
    lane = lax.broadcasted_iota(jnp.int32, pairs.shape, 1)
    high = jnp.where(lane < HEAD_DIM, jnp.ones_like(pairs), pairs)
    return pltpu.roll(high.astype(F32), HEAD_DIM, 1).astype(BF16), high


def attend_rows(pairs, mask, stacked, mixed):
    span = mixed.shape[0]
    side = value_sides(pairs)[0]
    lane = lax.broadcasted_iota(jnp.int32, (span, PAIR), 1)
    for start in range(0, HEADS, GROUP):
        all_scores = dot_nt(stacked[start * span : (start + GROUP) * span], pairs)
        weights = []
        for head in range(start, start + GROUP):
            place = (head - start) * span
            scores = all_scores[place : place + span] + mask
            top = jnp.max(scores, axis=1, keepdims=True)
            weights.append(jnp.exp2((scores - top) * (SCALE * LOG2E)).astype(BF16))
        summed = dot(jnp.concatenate(weights, axis=0), side)
        summed = summed * pltpu.roll(1.0 / summed, HEAD_DIM, 1)
        for head in range(0, GROUP, 2):
            one = summed[head * span : (head + 1) * span]
            two = pltpu.roll(summed[(head + 1) * span : (head + 2) * span], HEAD_DIM, 1)
            lanes = slice((start + head) // 2 * PAIR, ((start + head) // 2 + 1) * PAIR)
            mixed[:, lanes] = jnp.where(lane < HEAD_DIM, one, two).astype(BF16)


def attend_body(batch, meta, queries, shared, w_out_h, base, result, mixed, stacked, mask, w_out, sems):
    seq = pl.program_id(0)
    span = queries.shape[0]
    length = mask.shape[1]
    seq_length = meta[4 + 2 * batch + seq]

    def run():
        @pl.when(seq == 0)
        def _():
            fetch(sems, (w_out_h.at[0], w_out))

        for pair in range(PAIRS):
            for side, value in enumerate(spread_pair(queries[:, pair * PAIR : (pair + 1) * PAIR], True)):
                stacked[(2 * pair + side) * span : (2 * pair + side + 1) * span] = value
        def some(keys):
            mask[:, :keys] = mask_rows(meta, span, keys, seq_length)
            pairs = shared[: keys // span, 0, 0].reshape(keys, PAIR)
            attend_rows(pairs, mask[:, :keys], stacked, mixed)

        by_quarters(meta, span, length, seq_length, some)

        @pl.when(seq == 0)
        def _():
            pltpu.make_async_copy(w_out_h.at[0], w_out, sems.at[0]).wait()

        result[...] = (base[...] + dot(mixed[...], w_out[...])).astype(BF16)

    pl.when(meta[2] == 0)(run)


def attend(batch, meta, queries, gathered, w_out, base):
    width = queries.shape[1]
    count, _, seqs, span, _ = gathered.shape
    rows = seqs * span
    length = count * span
    return call(
        partial(attend_body, batch),
        (seqs,),
        [
            pl.BlockSpec((span, width), lambda s, meta: (batch * seqs + s, 0)),
            pl.BlockSpec((count, 1, 1, span, PAIR), lambda s, meta: (0, batch, s, 0, 0)),
            IN_HBM,
            pl.BlockSpec((span, width), lambda s, meta: (batch * seqs + s, 0)),
        ],
        pl.BlockSpec((span, width), lambda s, meta: (s, 0)),
        jax.ShapeDtypeStruct((rows, width), BF16),
        [
            pltpu.VMEM((span, width), BF16),
            pltpu.VMEM((HEADS * span, PAIR), BF16),
            pltpu.VMEM((span, length), F32),
            pltpu.VMEM((width, width), BF16),
            pltpu.SemaphoreType.DMA((1,)),
        ],
    )(meta, queries, gathered, w_out, base)


def softmax_back(fresh, pairs, sides, mask, q_sides, d_sides, saved, first_head, weights_sc, d_scores_sc):
    span = q_sides[0].shape[0]
    count = len(q_sides)
    lane = lax.broadcasted_iota(jnp.int32, (span, PAIR), 1)
    products = dot_nt(jnp.concatenate(q_sides + d_sides, axis=0), pairs)
    for n in range(count):
        rows = slice(n * span, (n + 1) * span)
        here = lane == first_head + n
        scores = products[rows]
        d_weights = products[(count + n) * span : (count + n + 1) * span]
        if fresh:
            scores = scores + mask
            top = jnp.max(scores, axis=1, keepdims=True)
            weights = jnp.exp2((scores - top) * (SCALE * LOG2E))
            sums = jnp.sum(weights, axis=1, keepdims=True)
            weights = weights * (1.0 / sums)
            saved = jnp.where(here, top * (SCALE * LOG2E) + jnp.log2(sums), saved)
        else:
            norm = jnp.sum(jnp.where(here, saved, 0.0), axis=1, keepdims=True)
            weights = jnp.exp2(scores * (SCALE * LOG2E) + mask - norm)
        lean = jnp.sum(weights * d_weights, axis=1, keepdims=True)
        weights_sc[rows] = weights.astype(BF16)
        d_scores_sc[rows] = (weights * (d_weights - lean)).astype(BF16)
    return saved


def attend_back_part(fresh, seq_length, meta, rows, pairs, queries, d_mixed, table, norms, mixed, d_raw, mask_sc, weights_sc, d_scores_sc, total):
    span = table.shape[0]
    length = pairs.shape[0]
    lane = lax.broadcasted_iota(jnp.int32, (span, PAIR), 1)
    mask_sc[:, :length] = mask_rows(meta, span, length, seq_length)
    mask = mask_sc[:, :length]
    side = value_sides(pairs)[0] if fresh else None
    saved = jnp.zeros((span, PAIR), F32) if fresh else norms[rows]
    for number, first_head in enumerate(range(0, HEADS, GROUP)):
        q_sides, d_sides = [], []
        for pair in range(first_head // 2, (first_head + GROUP) // 2):
            lanes = slice(pair * PAIR, (pair + 1) * PAIR)
            q_sides += spread_pair(queries[rows, lanes], True)
            d_sides += spread_pair(d_mixed[rows, lanes], False)
        slot = number % 2
        weights = weights_sc.at[slot, :, :length]
        d_scores = d_scores_sc.at[slot, :, :length]
        saved = softmax_back(fresh, pairs, side, mask, q_sides, d_sides, saved, first_head, weights, d_scores)
        weights, d_scores = weights[...], d_scores[...]
        d_query = dot(d_scores, pairs)
        out = dot(weights, side) if fresh else None
        scaled = [(value.astype(F32) * SCALE).astype(BF16) for value in q_sides]
        part = dot_tn(
            jnp.concatenate([d_scores, weights], axis=0), jnp.concatenate(scaled + d_sides, axis=0)
        )
        if number == 0:
            total[:length] = part
        else:
            total[:length] += part
        for n in range(0, GROUP, 2):
            pair = (first_head + n) // 2
            lanes = slice(pair * PAIR, (pair + 1) * PAIR)

            def join(values):
                one = values[n * span : (n + 1) * span]
                two = values[(n + 1) * span : (n + 2) * span]
                return jnp.where(lane < HEAD_DIM, one, pltpu.roll(two, HEAD_DIM, 1))

            if fresh:
                mixed[rows, lanes] = join(out).astype(BF16)
            d_raw[rows, lanes] = rotate(join(d_query) * SCALE, table[...], -1.0).astype(BF16)
    if fresh:
        norms[rows] = saved


def attend_back_all(fresh, batch, meta, shared, d_shared, span, total, run):
    count, seqs = d_shared.shape[:2]
    length = count * span

    @pl.loop(0, seqs)
    def _(seq):
        rows = pl.ds(pl.multiple_of(seq * span, span), span)
        seq_length = meta[4 + 2 * batch + seq]

        def some(keys):
            pairs = shared[: keys // span, 0, pl.ds(seq, 1)].reshape(keys, PAIR)
            run(seq_length, rows, pairs)
            if keys < length:
                total[keys:] = jnp.zeros((length - keys, PAIR), F32)

        by_quarters(meta, span, length, seq_length, some)
        d_shared[:, pl.ds(seq, 1)] = total[...].astype(BF16).reshape(count, 1, span, PAIR)


def feed_back_part(upstream, slope, w_in, w_back, d_upper, block, waits):
    inner = slope.shape[1]
    two = None
    for step in range(inner // block):
        lanes = slice(step * block, (step + 1) * block)
        waits(step)
        rate = (dot_nt(upstream, w_back[lanes, :]) * slope[:, lanes].astype(F32)).astype(BF16)
        d_upper[:, lanes] = rate
        part = dot_nt(rate, w_in[:, lanes])
        two = part if two is None else two + part
    return two


def chain_body(front, which, block, meta, up, hid, *rest, push):
    if front:
        came, shared, offsets_h, *rest = rest
    else:
        back, queries, slope, first_keys, shared, *rest = rest
    gains_h, table_h, w_query_h, w_out_h, w_in_h, w_back_h, *rest = rest
    if front:
        hidden, queries, normed, second, active, slope, *rest = rest
        hidden[...] = pick(meta, hid, came)
        push(hidden)
        upstream = up
    else:
        upstream, *rest = rest
        upstream[...] = pick(meta, back, up)
        push(upstream)
        hidden = hid
    mixed, norms, d_shared, d_low, *rest = rest
    if not front:
        d_raw, d_upper, d_hidden, d_norms, keys_keep, keys_send, *rest = rest
    gains, table, w_query, w_out, w_in, w_back, d_mixed, mask_sc, weights_sc, d_scores_sc, total_sc, sems, *rest = rest
    if front:
        offsets, d_raw, d_upper = rest
    span = table.shape[0]
    inner = slope.shape[1]
    steps = inner // block
    batch = which[0] + which[1] * meta[2]
    place = pl.ds(pl.multiple_of(meta[0] * span, span), span)
    operands = [(gains_h, gains), (w_query_h.at[0], w_query), (table_h.at[place], table), (w_out_h.at[0], w_out)]
    for start in range(0, inner, block):
        lanes = pl.ds(start, block)
        operands.append((w_in_h.at[0, :, lanes], w_in.at[:, lanes]))
    for start in range(0, inner, block):
        lanes = pl.ds(start, block)
        operands.append((w_back_h.at[0, lanes, :], w_back.at[lanes, :]))
    if front:
        operands.append((offsets_h, offsets))
    copies = fetch(sems, *operands)
    if front:

        def waits(stage):
            for copy in (copies[0], copies[-1]) if stage == 0 else copies[1:3]:
                copy.wait()

        _, feed = front_part(hidden[...], gains, offsets, table, w_query, w_in, queries, normed, second, waits)
        for step in range(steps):
            lanes = slice(step * block, (step + 1) * block)
            copies[4 + step].wait()
            value, rate = gelu_parts(dot(feed, w_in[:, lanes]))
            active[:, lanes] = value.astype(BF16)
            slope[:, lanes] = rate.astype(BF16)
        push(queries, normed, second, active, slope)
    else:
        copies[2].wait()
    copies[3].wait()
    d_mixed[...] = dot_nt(upstream[...], w_out[...]).astype(BF16)

    def run(seq_length, rows, pairs):
        attend_back_part(
            True, seq_length, meta, rows, pairs, queries, d_mixed, table, norms, mixed, d_raw,
            mask_sc, weights_sc, d_scores_sc, total_sc
        )

    attend_back_all(True, batch, meta, shared, d_shared, span, total_sc, run)
    push(mixed, norms, d_shared)
    if not front:
        push(d_raw)
        for out, core in ((keys_keep, meta[1]), (keys_send, 1 - meta[1])):
            for pair in range(out.shape[0]):
                for slot, keys in enumerate((first_keys, d_shared)):
                    out[pair, slot] = keys[pl.ds(2 * pair + core, 1)].reshape(out.shape[2:])
        push(keys_keep, keys_send)

    def more_waits(step):
        if not front:
            copies[4 + step].wait()
        copies[4 + steps + step].wait()

    two = feed_back_part(upstream[...], slope, w_in, w_back, d_upper, block, more_waits)
    if not front:
        push(d_upper)
        for copy in copies[:2]:
            copy.wait()
    one = dot_nt(d_raw[...], w_query[...])
    unit, scale = standardize(hidden[...].astype(F32))
    total = upstream[...].astype(F32) + norm_back(one * gains[0, 0:1] + two * gains[0, 1:2], 1.0, unit, scale)
    d_low[...] = total.astype(BF16)
    push(d_low)
    if not front:
        d_hidden[...] = total
        push(d_hidden)
        d_norms[...] = sum_rows(one * unit, one, two * unit, two)
        push(d_norms)


def chain(which, meta, upstream, hidden, more, gathered, gains, offsets, table, w_query, w_out, w_in, w_back):
    rows, width = hidden.shape
    count, _, seqs, span, _ = gathered.shape
    inner = w_in.shape[2]
    length = count * span
    block = inner // 2
    front = len(more) == 1
    flat = whole((rows, width))
    shared_shape = (count, seqs, span, PAIR)
    shared_spec = pl.BlockSpec((count, 1, seqs, span, PAIR), lambda j, meta: (0, which[0] + which[1] * meta[2], 0, 0, 0))
    outs = [(rows, width, BF16)] * 4 + [(rows, inner, BF16)] * 2 if front else [(rows, width, BF16)]
    outs += [(rows, width, BF16), (rows, PAIR, F32), None, (rows, width, BF16)]
    if not front:
        outs += [(rows, width, BF16), (rows, inner, BF16), (rows, width, F32), (8, width, F32)]
        outs += [(count // 2, 2, seqs, span, PAIR, BF16)] * 2
    if front:
        operands, specs = [upstream, hidden, *more, gathered, offsets], [flat, flat, flat, shared_spec, IN_HBM]
    else:
        operands = [upstream, hidden, *more, gathered]
        specs = [flat, flat, flat, flat, whole((rows, inner)), whole(shared_shape), shared_spec]
    return call(
        partial(chain_body, front, which, block),
        (1,),
        specs + [IN_HBM] * 6,
        [whole(shared_shape) if out is None else whole(out[:-1]) for out in outs],
        [jax.ShapeDtypeStruct(shared_shape, BF16) if out is None else jax.ShapeDtypeStruct(out[:-1], out[-1]) for out in outs],
        [
            pltpu.VMEM(gains.shape, F32),
            pltpu.VMEM((span, table.shape[1]), F32),
            pltpu.VMEM((width, width), BF16),
            pltpu.VMEM((width, width), BF16),
            pltpu.VMEM((width, inner), BF16),
            pltpu.VMEM((inner, width), BF16),
            pltpu.VMEM((rows, width), BF16),
            pltpu.VMEM((span, length), F32),
            pltpu.VMEM((2, GROUP * span, length), BF16),
            pltpu.VMEM((2, GROUP * span, length), BF16),
            pltpu.VMEM((length, PAIR), F32),
            pltpu.SemaphoreType.DMA((5 + 2 * (inner // block),)),
        ]
        + ([pltpu.VMEM(offsets.shape, F32), pltpu.VMEM((rows, width), BF16), pltpu.VMEM((rows, inner), BF16)] if front else []),
        pushed=tuple(range(len(outs))),
    )(meta, *operands, gains, table, w_query, w_out, w_in, w_back)


def attend_back_body(which, split, meta, upstream, queries, norms, shared, *rest, push):
    (first_own, *rest) = rest
    (up_d, raw_d, mixed_c, mixed_d, normed_c, normed_d, w_out_h, w_query_h, table_h) = rest[:9]
    (key_keep, key_send, d_normed) = rest[9:12]
    halves = rest[12:14] if split else rest[12:13]
    (d_raw, d_mixed, mask_sc, weights_sc, d_scores_sc, total_sc, d_shared, table, w_out, w_query, sems) = rest[12 + len(halves) :][:11]
    span = table.shape[0]
    batch = which[0] + which[1] * meta[2]
    place = pl.ds(pl.multiple_of(meta[0] * span, span), span)
    copies = fetch(sems, (w_out_h.at[0], w_out), (table_h.at[place], table), (w_query_h.at[0], w_query))
    copies[0].wait()
    d_mixed[...] = dot_nt(upstream[...], w_out[...]).astype(BF16)
    copies[1].wait()

    def run(seq_length, rows, pairs):
        attend_back_part(
            False, seq_length, meta, rows, pairs, queries, d_mixed, table, norms, None, d_raw,
            mask_sc, weights_sc, d_scores_sc, total_sc
        )

    attend_back_all(False, batch, meta, shared, d_shared, span, total_sc, run)
    for out, core in ((key_keep, meta[1]), (key_send, 1 - meta[1])):
        for pair in range(out.shape[0]):
            for slot, keys in enumerate((first_own, d_shared)):
                part = keys[pl.ds(2 * pair + core, 1)].reshape(out.shape[2:])
                out[pair, slot] = part
    push(key_keep, key_send)
    copies[2].wait()
    d_normed[...] = dot_nt(d_raw[...], w_query[...])
    push(d_normed)
    both = jnp.concatenate([upstream[...], up_d[...]], axis=0)
    left = jnp.concatenate([mixed_c[...], mixed_d[...]], axis=0)
    outer = dot_tn(left, both).astype(BF16)
    both = jnp.concatenate([d_raw[...], raw_d[...]], axis=0)
    left = jnp.concatenate([normed_c[...], normed_d[...]], axis=0)
    query = dot_tn(left, both).astype(BF16)
    width = both.shape[1]
    if len(halves) == 1:
        halves[0][:, :width] = outer
        halves[0][:, width:] = query
        push(halves[0])
        return
    keep, send, pair_sc = halves[0], halves[1], rest[-1]
    pair_sc[..., :width] = outer.reshape(pair_sc.shape[:3] + (width,))
    pair_sc[..., width:] = query.reshape(pair_sc.shape[:3] + (width,))
    keep[...] = pair_sc[:, pl.ds(meta[1], 1)].reshape(keep.shape)
    send[...] = pair_sc[:, pl.ds(1 - meta[1], 1)].reshape(send.shape)
    push(keep, send)


def attend_back(
    which, shards, meta, upstream, queries, norms, gathered, first_own, up_d, raw_d, mixed_c, mixed_d, normed_c, normed_d, w_out, w_query, table,
    behind=()
):
    rows, width = queries.shape
    count, _, seqs, span, _ = gathered.shape
    length = count * span
    shared_shape = (count, seqs, span, PAIR)
    key_half = (count // 2, 2, seqs, span, PAIR)
    part = width // shards
    split = part % 16 == 0
    if split:
        pairs = [(shards // 2, part, 2 * width)] * 2
    else:
        pairs = [(width, 2 * width)]
    outs = call(
        partial(attend_back_body, which, split),
        (1,),
        [whole((rows, width))] * 2
        + [whole(norms.shape)]
        + [pl.BlockSpec((count, 1, seqs, span, PAIR), lambda j, meta: (0, which[0] + which[1] * meta[2], 0, 0, 0))]
        + [whole(shared_shape)]
        + [whole((rows, width))] * 6
        + [IN_HBM] * 3,
        [whole(key_half)] * 2 + [whole((rows, width))] + [whole(shape) for shape in pairs],
        [
            jax.ShapeDtypeStruct(key_half, BF16),
            jax.ShapeDtypeStruct(key_half, BF16),
            shape_of(rows, width, F32),
        ]
        + [jax.ShapeDtypeStruct(shape, BF16) for shape in pairs],
        [
            pltpu.VMEM((rows, width), BF16),
            pltpu.VMEM((rows, width), BF16),
            pltpu.VMEM((span, length), F32),
            pltpu.VMEM((2, GROUP * span, length), BF16),
            pltpu.VMEM((2, GROUP * span, length), BF16),
            pltpu.VMEM((length, PAIR), F32),
            pltpu.VMEM(shared_shape, BF16),
            pltpu.VMEM((span, table.shape[1]), F32),
            pltpu.VMEM((width, width), BF16),
            pltpu.VMEM((width, width), BF16),
            pltpu.SemaphoreType.DMA((3,)),
        ]
        + ([pltpu.VMEM((shards // 2, 2, part, 2 * width), BF16)] if split else []),
        behind=behind,
        pushed=tuple(range(3 + len(pairs))),
    )(meta, upstream, queries, norms, gathered, first_own, up_d, raw_d, mixed_c, mixed_d, normed_c, normed_d, w_out, w_query, table)
    if split:
        return outs
    return (*outs[:3], *split_cores(outs[3].reshape(shards, part, 2 * width)))


def finish_body(block, meta, *rest):
    hidden, mixed, active = rest[0:2], rest[2:4], rest[4:6]
    w_out_h, w_back_h, outs, w_out, w_back, sems = rest[6:]
    inner = w_back.shape[0]
    pairs = [(w_out_h.at[0], w_out)]
    for start in range(0, inner, block):
        pairs.append((w_back_h.at[0, pl.ds(start, block), :], w_back.at[pl.ds(start, block), :]))
    copies = fetch(sems, *pairs)
    rows = hidden[0].shape[0]

    def both(refs, lanes=slice(None)):
        return jnp.concatenate([refs[0][:, lanes], refs[1][:, lanes]], axis=0)

    copies[0].wait()
    total = both(hidden).astype(F32) + dot(both(mixed), w_out[...])
    for step in range(inner // block):
        lanes = slice(step * block, (step + 1) * block)
        copies[1 + step].wait()
        total += dot(both(active, lanes), w_back[lanes, :])
    section = meta[2]
    outs[pl.ds(1 - section, 1)] = total[:rows].astype(BF16)[None]
    outs[pl.ds(section, 1)] = total[rows:].astype(BF16)[None]


def finish(meta, hidden, mixed, active, w_out, w_back, behind=()):
    rows, width = hidden[0].shape
    inner = active[0].shape[1]
    block = 768 if inner % 768 == 0 else inner
    return call(
        partial(finish_body, block),
        (1,),
        [whole((rows, width))] * 4 + [whole((rows, inner))] * 2 + [IN_HBM] * 2,
        whole((2, rows, width)),
        jax.ShapeDtypeStruct((2, rows, width), BF16),
        [
            pltpu.VMEM((width, width), BF16),
            pltpu.VMEM((inner, width), BF16),
            pltpu.SemaphoreType.DMA((1 + inner // block,)),
        ],
        behind=behind,
    )(meta, *hidden, *mixed, *active, w_out, w_back)


def sum_rows(*values):
    sums = [jnp.sum(value, axis=0, keepdims=True) for value in values]
    return jnp.concatenate(sums + [jnp.zeros_like(sums[0])] * (8 - len(sums)), axis=0)


def feed_back_body(block, meta, upstream, slope, w_in_h, w_back_h, d_upper, d_second, w_in, w_back, sems):
    inner = slope.shape[1]
    operands = []
    for start in range(0, inner, block):
        lanes = pl.ds(start, block)
        operands.append((w_back_h.at[0, lanes, :], w_back.at[lanes, :]))
        operands.append((w_in_h.at[0, :, lanes], w_in.at[:, lanes]))
    copies = fetch(sems, *operands)

    def waits(step):
        copies[2 * step].wait()
        copies[2 * step + 1].wait()

    d_second[...] = feed_back_part(upstream[...], slope, w_in, w_back, d_upper, block, waits)


def feed_back(meta, upstream, slope, w_in, w_back):
    rows, width = upstream.shape
    inner = w_in.shape[2]
    block = 768 if inner % 768 == 0 else inner
    return call(
        partial(feed_back_body, block),
        (1,),
        [whole((rows, width)), whole((rows, inner))] + [IN_HBM] * 2,
        [whole((rows, inner)), whole((rows, width))],
        [shape_of(rows, inner, BF16), shape_of(rows, width, F32)],
        [
            pltpu.VMEM((width, inner), BF16),
            pltpu.VMEM((inner, width), BF16),
            pltpu.SemaphoreType.DMA((2 * (inner // block),)),
        ],
    )(meta, upstream, slope, w_in, w_back)


def store_halves(meta, block, keep, send, scratch):
    groups, _, part, lanes = scratch.shape
    scratch[...] = block.astype(BF16).reshape(groups, 2, part, lanes)
    core = meta[1]
    keep[...] = scratch[:, pl.ds(core, 1)].reshape(keep.shape)
    send[...] = scratch[:, pl.ds(1 - core, 1)].reshape(send.shape)


def late_feed_body(shards, block, meta, active_c, active_d, up, back, up_d, slope, *rest, push):
    w_in_h, w_back_h, keep, send, d_upper, d_second, up_c, w_in, w_back, scratch, sems = rest
    up_c[...] = pick(meta, back, up)
    push(up_c)
    inner = w_in.shape[1]
    operands = []
    for start in range(0, inner, block):
        lanes = pl.ds(start, block)
        operands.append((w_back_h.at[0, lanes, :], w_back.at[lanes, :]))
        operands.append((w_in_h.at[0, :, lanes], w_in.at[:, lanes]))
    copies = fetch(sems, *operands)
    part = inner // shards
    both = jnp.concatenate([up_c[...], up_d[...]], axis=0)
    for group in range(shards // 2):
        lanes = slice(group * 2 * part, (group + 1) * 2 * part)
        left = jnp.concatenate([active_c[:, lanes], active_d[:, lanes]], axis=0)
        scratch[group] = dot_tn(left, both).astype(BF16).reshape(2, part, both.shape[1])
    core = meta[1]
    keep[...] = scratch[:, pl.ds(core, 1)].reshape(keep.shape)
    send[...] = scratch[:, pl.ds(1 - core, 1)].reshape(send.shape)
    push(send, keep)

    def waits(step):
        copies[2 * step].wait()
        copies[2 * step + 1].wait()

    d_second[...] = feed_back_part(up_c[...], slope, w_in, w_back, d_upper, block, waits)
    push(d_upper, d_second)


def late_feed(meta, shards, active_c, active_d, up, back, up_d, slope, w_in, w_back, behind=()):
    rows, width = up.shape
    inner = w_in.shape[2]
    part = inner // shards
    if part % 64:
        up_c = jnp.where(meta[2] == 0, back, up)
        halves = weights_full(meta, shards, active_c, active_d, up_c, up_d)
        return (*halves, *feed_back(meta, up_c, slope, w_in, w_back), up_c)
    block = 768 if inner % 768 == 0 else inner
    half = (shards // 2, part, width)
    return call(
        partial(late_feed_body, shards, block),
        (1,),
        [whole((rows, inner))] * 2 + [whole((rows, width))] * 3 + [whole((rows, inner))] + [IN_HBM] * 2,
        [whole(half), whole(half), whole((rows, inner)), whole((rows, width)), whole((rows, width))],
        [jax.ShapeDtypeStruct(half, BF16)] * 2 + [shape_of(rows, inner, BF16), shape_of(rows, width, F32), shape_of(rows, width, BF16)],
        [
            pltpu.VMEM((width, inner), BF16),
            pltpu.VMEM((inner, width), BF16),
            pltpu.VMEM((shards // 2, 2, part, width), BF16),
            pltpu.SemaphoreType.DMA((2 * (inner // block),)),
        ],
        behind=behind,
        pushed=(0, 1, 2, 3, 4),
    )(meta, active_c, active_d, up, back, up_d, slope, w_in, w_back)


def weights_full_body(meta, left_c, left_d, right_c, right_d, full, turned_c, turned_d):
    @pl.when(pl.program_id(0) == 0)
    def _():
        turned_c[...] = left_c[...].T
        turned_d[...] = left_d[...].T

    block = dot(turned_c[...], right_c[...]) + dot(turned_d[...], right_d[...])
    full[...] = block.astype(BF16)


def weights_full(meta, shards, left_c, left_d, right_c, right_d):
    rows, tall = left_c.shape
    wide = right_c.shape[1]
    block = 256
    full = call(
        weights_full_body,
        (wide // block,),
        [whole((rows, tall))] * 2 + [pl.BlockSpec((rows, block), lambda j, meta: (0, j))] * 2,
        pl.BlockSpec((tall, block), lambda j, meta: (0, j)),
        jax.ShapeDtypeStruct((tall, wide), BF16),
        [pltpu.VMEM((tall, rows), BF16), pltpu.VMEM((tall, rows), BF16)],
    )(meta, left_c, left_d, right_c, right_d)
    return split_cores(full.reshape(shards, tall // shards, wide))


def weights_wide_body(meta, left_c, left_d, right_c, right_d, keep, send, scratch, turned_c, turned_d):
    @pl.when(pl.program_id(0) == 0)
    def _():
        turned_c[...] = left_c[...].T
        turned_d[...] = left_d[...].T

    block = dot(turned_c[...], right_c[...]) + dot(turned_d[...], right_d[...])
    store_halves(meta, block, keep, send, scratch)


def weights_wide(meta, shards, left_c, left_d, right_c, right_d):
    rows, tall = left_c.shape
    wide = right_c.shape[1]
    block = wide // 2
    part = tall // shards
    if part % 16:
        return weights_full(meta, shards, left_c, left_d, right_c, right_d)
    spec = pl.BlockSpec((shards // 2, part, block), lambda j, meta: (0, 0, j))
    shape = jax.ShapeDtypeStruct((shards // 2, part, wide), BF16)
    return call(
        weights_wide_body,
        (wide // block,),
        [whole((rows, tall))] * 2 + [pl.BlockSpec((rows, block), lambda j, meta: (0, j))] * 2,
        [spec, spec],
        [shape, shape],
        [
            pltpu.VMEM((shards // 2, 2, part, block), BF16),
            pltpu.VMEM((tall, rows), BF16),
            pltpu.VMEM((tall, rows), BF16),
        ],
    )(meta, left_c, left_d, right_c, right_d)


def tail_body(
    meta, keys, hid_d, hid_c, nrm_d, nrm_c, dh_d, sums_d, up_c, one_c, two_c,
    gains_h, w_keys_h, table_h, grads, *rest
):
    small, (gains, w_keys, table, sems) = rest[:2], rest[2:6]
    section = meta[2]
    first = (section == 0).astype(F32)
    span = table.shape[0]
    seqs = keys.shape[1]
    rows = pl.ds(pl.multiple_of(meta[0] * span, span), span)
    copies = fetch(sems, (gains_h, gains), (w_keys_h, w_keys), (table_h.at[rows], table))
    for copy in copies:
        copy.wait()
    keys_sum = None
    norm_sum = sums_d[...]
    for slot, (hidden, normed) in enumerate(((hid_d, nrm_d), (hid_c, nrm_c))):
        raw = []
        for seq in range(seqs):
            both = keys[slot, seq] * first
            raw.append(rotate_keys(both, table[...], -1.0).astype(BF16))
        raw = jnp.concatenate(raw, axis=0)
        part = dot_tn(normed[...], raw)
        keys_sum = part if keys_sum is None else keys_sum + part
        one = dot_nt(raw, w_keys[...])
        unit, scale = standardize(hidden[...].astype(F32))
        if slot == 0:
            total = dh_d[...] + norm_back(one, gains[0, 0:1], unit, scale)
            norm_sum += sum_rows(one * unit, one)
        else:
            one, two = one + one_c[...], two_c[...]
            total = up_c[...].astype(F32) + norm_back(one * gains[0, 0:1] + two * gains[0, 1:2], 1.0, unit, scale)
            norm_sum += sum_rows(one * unit, one, two * unit, two)
        batch = section if slot == 0 else 1 - section
        grads[pl.ds(batch, 1)] = total[None]
    if len(rest) == 6:
        small[0][...] = keys_sum.astype(BF16)
        small[1][...] = norm_sum
        return
    gather = rest[6]
    groups, _, part, _ = gather.shape
    share = part // 2
    width = keys_sum.shape[0]
    turned = jnp.concatenate([norm_sum, jnp.zeros((PAIR - 8, width), F32)], axis=0).T
    for shard in range(2 * groups):
        place = gather.at[shard // 2, shard % 2]
        for half in range(2):
            start = half * width // 2 + shard * share
            place[half * share : (half + 1) * share, :PAIR] = keys_sum[start : start + share]
        place[:, PAIR:] = turned[shard * part : (shard + 1) * part]
    small[0][...] = gather[:, pl.ds(meta[1], 1)].reshape(small[0].shape).astype(BF16)
    small[1][...] = gather[:, pl.ds(1 - meta[1], 1)].reshape(small[1].shape).astype(BF16)


def small_parts(shards, sections, d_keys, d_norms):
    width = d_keys.shape[0]
    share = width // (sections * shards)
    d_keys = d_keys.reshape(sections, shards, share, PAIR).transpose(1, 0, 2, 3).reshape(shards, sections * share, PAIR)
    d_norms = d_norms.T.reshape(shards, width // shards, 8)
    d_norms = jnp.pad(d_norms, ((0, 0), (0, 0), (0, PAIR - 8))).astype(BF16)
    return split_cores(jnp.concatenate([d_keys, d_norms], axis=-1))


def tail(shards, sections, meta, *arrays, behind=()):
    rows, width = arrays[1].shape
    span = arrays[0].shape[2]
    gains, w_keys, table = arrays[-3:]
    part = width // shards
    split = part % 16 == 0 and sections == 2
    if split:
        outs = [jax.ShapeDtypeStruct((shards // 2, part, 2 * PAIR), BF16)] * 2
    else:
        outs = [shape_of(width, PAIR, BF16), shape_of(8, width, F32)]
    grads, *small = call(
        tail_body,
        (1,),
        [whole(array.shape) for array in arrays[:-3]] + [IN_HBM] * 3,
        [whole((2, rows, width))] + [whole(out.shape) for out in outs],
        [jax.ShapeDtypeStruct((2, rows, width), F32)] + outs,
        [
            pltpu.VMEM(gains.shape, F32),
            pltpu.VMEM(w_keys.shape, BF16),
            pltpu.VMEM((span, table.shape[1]), F32),
            pltpu.SemaphoreType.DMA((3,)),
        ]
        + ([pltpu.VMEM((shards // 2, 2, part, 2 * PAIR), F32)] if split else []),
        behind=behind,
    )(meta, *arrays)
    return (grads, *small) if split else (grads, *small_parts(shards, sections, *small))


def swap(value, axis, bit):
    count = lax.axis_size(axis)
    return lax.ppermute(value, axis, [(source, source ^ bit) for source in range(count)])


def across(value, steps):
    pairs = [(0, 1)] if steps > 0 else [(1, 0)]
    return lax.ppermute(value, "section", pairs)


def after(value, *others):
    return lax.optimization_barrier((value, *others))[0]


def wide_sum(values):
    total = values[0].astype(F32)
    for value in values[1:]:
        total = total + value.astype(F32)
    return total


class Halving:
    def __init__(self, *parts):
        self.parts = list(parts)

    def prepare(self, axis, bit, low, *hold):
        cut = []
        for value in self.parts:
            places = value.shape[0]
            cut.append(value.reshape(((places // 2, 2) if low else (2, places // 2)) + value.shape[1:]))
        if hold:
            cut[0] = after(cut[0], *hold)
        place = 1 if low else 0
        mine = (lax.axis_index(axis) // bit) % 2
        other = wide_sum([lax.dynamic_index_in_dim(value, 1 - mine, place, keepdims=False) for value in cut])
        self.sent = other.astype(BF16)
        kept = wide_sum([lax.dynamic_index_in_dim(value, mine, place, keepdims=False) for value in cut])
        self.parts = [kept.astype(BF16)]
        self.way = (axis, bit)

    def launch(self, *hold):
        if hold:
            self.sent = after(self.sent, *hold)
        self.parts.append(swap(self.sent, *self.way))

    @property
    def received(self):
        return self.parts[-1]

    def bits(self, axis):
        count = lax.axis_size(axis)
        found = [1 << n for n in range(1 if axis == "ctx" else 0, count.bit_length() - 1)]
        return [(axis, bit, axis == "ctx") for bit in (found if axis == "ctx" else found[::-1])]

    def along(self, steps, hold=(), held=()):
        for step in steps:
            self.prepare(*step, *hold)
            self.launch(*held)
            hold, held = (), ()

    def result(self):
        return wide_sum([value.reshape(value.shape[1:]) for value in self.parts])


def split_cores(value):
    shards, part, lanes = value.shape
    cut = value.reshape(shards // 2, 2, part, lanes)
    core = lax.axis_index("ctx") % 2
    return (
        lax.dynamic_index_in_dim(cut, core, 1, keepdims=False),
        lax.dynamic_index_in_dim(cut, 1 - core, 1, keepdims=False),
    )


def per_device(
    length, tokens, lengths, norm_gains, norm_offsets, w_query, w_keys, w_out, w_in, w_back, cotangent
):
    batches, seqs, span, width = tokens.shape
    rows = seqs * span
    shards = lax.axis_size("dp") * lax.axis_size("ctx")
    section = lax.axis_index("section")
    place = lax.axis_index("ctx")
    first = section == 0
    table = jnp.asarray(rotary_table(length))

    own = make_keys(tokens, norm_gains, norm_offsets, w_keys, table)
    gathered = lax.all_gather(own, "ctx")
    meta = jnp.concatenate(
        [jnp.stack([place, place % 2, section, section]).astype(jnp.int32), lengths.reshape(-1)]
    )
    queries, base = front(meta, tokens, norm_gains, norm_offsets, table, w_query, w_in, w_back)
    chosen = choose(meta, own, across(own, 1), behind=(base,))
    came_a = across(attend(0, meta, queries, gathered, w_out, base), 1)
    came_b = across(attend(1, meta, queries, gathered, w_out, base), 1)
    gathered = lax.all_gather(chosen, "ctx")

    flat = tokens.reshape(batches, rows, width)
    cot = cotangent.reshape(batches, rows, width)

    def chain_of(which, upstream, hidden, *more):
        return chain(
            which, meta, upstream, hidden, more, gathered, norm_gains, norm_offsets, table, w_query, w_out, w_in, w_back
        )

    hid_c, queries_c, normed_c, second_c, active_c, slope_c, mixed_c, norms_c, ds_one, low_one = chain_of(
        PASS_C, cot[0], flat[1], came_a
    )
    back_d = across(low_one, -1)
    hid_d, queries_d, normed_d, second_d, active_d, slope_d = front(
        meta, flat[0], norm_gains, norm_offsets, table, w_query, w_in, came=came_b
    )
    up_d, mixed_d, _, ds_d, low_d, raw_d, upper_d, dh_d, sums_d, keys_keep, keys_send = chain_of(
        PASS_D, cot[1], hid_d, back_d, queries_d, slope_d, ds_one
    )
    back_c = across(low_d, -1)
    sent_keys = wide_sum([keys_keep, swap(keys_send, "ctx", 1)]).astype(BF16)
    came_keys = across(sent_keys, -1)
    keep, send, upper_c, two_c, up_c = late_feed(
        meta, shards, active_c, active_d, cot[0], back_c, up_d, slope_c, w_in, w_back, behind=(sent_keys,)
    )
    back = Halving(keep, swap(send, "ctx", 1))
    groups, depth = back.bits("dp"), back.bits("ctx")
    keep, send = weights_wide(meta, shards, second_c, second_d, upper_c, upper_d)
    inner = Halving(keep, swap(send, "ctx", 1))
    back.prepare(*groups[0], keep)
    back.launch()
    inner.prepare(*depth[0], back.sent)
    inner.launch()
    key_keep, key_send, one_c, keep, send = attend_back(
        PASS_C, shards, meta, up_c, queries_c, norms_c, gathered, ds_d, up_d, raw_d,
        mixed_c, mixed_d, normed_c, normed_d, w_out, w_query, table, behind=(back.sent, inner.sent)
    )
    late = Halving(key_keep, swap(key_send, "ctx", 1), came_keys)
    pair = Halving(keep, swap(send, "ctx", 1))
    back.along(groups[1:])
    back.prepare(*depth[0], one_c)
    inner.prepare(*depth[1], one_c)
    late.prepare(*depth[0], back.sent, inner.sent)
    late.launch()
    pair.prepare(*groups[0], late.sent)
    pair.launch()
    late.along(depth[1:], hold=(pair.sent,))
    back.launch(late.sent)
    inner.launch(late.sent)
    sections = lax.axis_size("section")
    input_grads, keep, send = tail(
        shards, sections, meta, late.result(), hid_d, hid_c, normed_d, normed_c, dh_d, sums_d, up_c, one_c, two_c,
        norm_gains, w_keys, table, behind=(back.sent, inner.sent, pair.sent)
    )
    small = Halving(keep, swap(send, "ctx", 1))
    outs = finish(
        meta, (hid_c, hid_d), (mixed_c, mixed_d), (active_c, active_d), w_out, w_back, behind=(keep,)
    )
    pair.along(groups[1:])
    back.prepare(*depth[1], outs)
    inner.prepare(*(depth[2:] + groups)[0], outs)
    pair.prepare(*depth[0], outs)
    back.launch()
    inner.launch(back.sent)
    pair.launch(inner.sent)
    small.along(groups, hold=(back.sent, inner.sent, pair.sent))
    pair.along(depth[1:], hold=(small.sent,))
    back.along(depth[2:])
    inner.along((depth[2:] + groups)[1:])
    small.along(depth[:1], hold=(pair.sent,))
    grad_back = after(back.result(), small.sent)
    grad_in = after(inner.result(), grad_back)
    small.along(depth[1:], hold=(grad_in,))
    small = small.result()
    pair_last, pair = pair.received, pair.result()
    share = width // (sections * shards)
    grad_norms = small[:, PAIR : PAIR + 4]
    keys_both = small[:, :PAIR].reshape(sections, share, PAIR)
    other_half = jnp.where(lengths[0, 0] > 0, keys_both[1], pair_last[0, :share, :PAIR].astype(F32))
    grad_keys = jnp.where(first, keys_both[0], across(other_half, 1))
    return (
        outs.reshape((1,) + tokens.shape),
        input_grads.reshape((1,) + tokens.shape),
        grad_norms[None],
        pair[None, :, width:],
        grad_keys,
        pair[None, :, :width],
        grad_in[None],
        grad_back[None],
    )


def solution(mesh):
    def run(*arrays):
        length = arrays[0].shape[2]
        return jax.shard_map(
            partial(per_device, length),
            mesh=mesh,
            in_specs=(
                P(None, "dp", "ctx", None),
                P(None, "dp"),
                P("section", None, None),
                P("section", None, None),
                P("section", None, None),
                P(),
                P("section", None, None),
                P("section", None, None),
                P("section", None, None),
                P(None, "dp", "ctx", None),
            ),
            out_specs=(
                P("section", None, "dp", "ctx", None),
                P("section", None, "dp", "ctx", None),
                P("section", ("dp", "ctx"), None),
                P("section", ("dp", "ctx"), None),
                P(("section", "dp", "ctx"), None),
                P("section", ("dp", "ctx"), None),
                P("section", ("dp", "ctx"), None),
                P("section", ("dp", "ctx"), None),
            ),
            check_vma=False,
        )(*arrays)

    return run
```

```python
from functools import partial

import jax
import jax.numpy as jnp
import numpy as np
from jax import lax
from jax.experimental import pallas as pl
from jax.experimental.pallas import tpu as pltpu
from jax.sharding import PartitionSpec as P

HEADS = 12
HEAD_DIM = 64
ROT = 16
PAIR = 2 * HEAD_DIM
PAIRS = HEADS // 2
LOG2E = 1.4426950408889634
SCALE = HEAD_DIM**-0.5
MASKED = -1e30
F32 = jnp.float32
BF16 = jnp.bfloat16
VMEM_LIMIT = 60 * 1024 * 1024
VMEM_MOST = 65280 * 1024
FLOPS = 1_000_000

PASS_C = (1, -1)
PASS_D = (0, 1)


def dot(left, right):
    return jnp.dot(left, right, preferred_element_type=F32)


def dot_nt(left, right, **kwargs):
    return lax.dot_general(left, right, (((1,), (1,)), ((), ())), preferred_element_type=F32, **kwargs)


def dot_tn(left, right):
    return lax.dot_general(left, right, (((0,), (0,)), ((), ())), preferred_element_type=F32)


def whole(shape):
    zeros = (0,) * len(shape)
    return pl.BlockSpec(shape, lambda *_: zeros)


def call(body, grid, in_specs, out_specs, out_shape, scratch=(), behind=(), pushed=(), limit=VMEM_LIMIT):
    count, hidden = len(in_specs), len(behind)
    in_specs = list(in_specs) + [IN_HBM] * hidden
    scratch = list(scratch)
    if pushed:
        out_specs = [IN_HBM if n in pushed else spec for n, spec in enumerate(out_specs)]
        scratch += [pltpu.VMEM(out_shape[n].shape, out_shape[n].dtype) for n in pushed]
        scratch.append(pltpu.SemaphoreType.DMA((len(pushed),)))

    def run(meta, *refs):
        ins, refs = refs[:count], refs[count + hidden :]
        if not pushed:
            body(meta, *ins, *refs)
            return
        outs, own = list(refs[: len(out_shape)]), refs[len(out_shape) :]
        own, places, sems = own[: -1 - len(pushed)], own[-1 - len(pushed) : -1], own[-1]
        copies = {}
        for place, (number, local) in enumerate(zip(pushed, places)):
            copies[id(local)] = pltpu.make_async_copy(local, outs[number], sems.at[place])
            outs[number] = local
        waiting = []

        def push(*locals_):
            for local in locals_:
                copies[id(local)].start()
                waiting.append(copies[id(local)])

        body(meta, *ins, *outs, *own, push=push)
        for copy in waiting:
            copy.wait()

    made = pl.pallas_call(
        run,
        grid_spec=pltpu.PrefetchScalarGridSpec(
            num_scalar_prefetch=1,
            grid=grid,
            in_specs=in_specs,
            out_specs=out_specs,
            scratch_shapes=scratch,
        ),
        out_shape=out_shape,
        compiler_params=pltpu.CompilerParams(vmem_limit_bytes=limit),
        cost_estimate=pl.CostEstimate(flops=FLOPS, bytes_accessed=0, transcendentals=0),
    )
    return lambda *operands: made(*operands, *behind)


IN_HBM = pl.BlockSpec(memory_space=pltpu.HBM)


def fetch(sems, *pairs):
    copies = [pltpu.make_async_copy(source, target, sems.at[n]) for n, (source, target) in enumerate(pairs)]
    for copy in copies:
        copy.start()
    return copies


def shape_of(rows, columns, dtype):
    return jax.ShapeDtypeStruct((rows, columns), dtype)


def rotary_table(length):
    half = ROT // 2
    inverse = 10000.0 ** (-np.arange(half) * (2.0 / ROT))
    angles = np.arange(length)[:, None] * inverse[None, :]
    cosine, sine = np.cos(angles), np.sin(angles)
    table = np.zeros((length, 3, 2, HEAD_DIM), np.float32)
    table[:, 0] = 1.0
    table[:, 0, :, :half] = cosine[:, None]
    table[:, 0, :, half:ROT] = cosine[:, None]
    table[:, 1, :, :half] = -sine[:, None]
    table[:, 2, :, half:ROT] = sine[:, None]
    return table.reshape(length, 3 * PAIR)


def rotate(values, table, sign=1.0):
    around = pltpu.roll(values, PAIR - ROT // 2, 1) * table[:, PAIR : 2 * PAIR]
    around = around + pltpu.roll(values, ROT // 2, 1) * table[:, 2 * PAIR :]
    return values * table[:, :PAIR] + (around if sign > 0 else -around)


def rotate_keys(values, table, sign=1.0):
    lane = lax.broadcasted_iota(jnp.int32, values.shape, 1)
    return jnp.where(lane < HEAD_DIM, rotate(values, table, sign), values)


def standardize(values):
    center = values - jnp.mean(values, axis=-1, keepdims=True)
    scale = lax.rsqrt(jnp.mean(center * center, axis=-1, keepdims=True) + 1e-05)
    return center * scale, scale


def norm_back(grads, gain, normed, scale):
    inner = grads * gain
    lean = jnp.mean(inner, axis=-1, keepdims=True)
    along = jnp.mean(inner * normed, axis=-1, keepdims=True)
    return scale * (inner - lean - normed * along)


def gelu_parts(values):
    size = jnp.abs(values) * 0.7071067811865476
    base = 1.0 + 0.3275911 * size
    turn = pl.reciprocal(base, approx=True)
    turn = turn * (2.0 - base * turn)
    bell = jnp.exp2(values * values * (-0.5 * LOG2E))
    tail = turn * (
        0.127414796 + turn * (-0.142248368 + turn * (0.7107068705 + turn * (-0.7265760135 + turn * 0.5307027145)))
    )
    tail = tail * bell
    share = jnp.where(values >= 0.0, 1.0 - tail, tail)
    return values * share, share + values * (bell * 0.3989422804014327)


def keys_body(tokens_h, gains_h, offsets_h, w_keys_h, table_h, shared, tokens, gains, offsets, w_keys, table, sems):
    span = table.shape[0]
    rows = pl.ds(pl.multiple_of(lax.axis_index("ctx") * span, span), span)
    copies = fetch(
        sems,
        (tokens_h, tokens),
        (gains_h, gains),
        (offsets_h, offsets),
        (w_keys_h, w_keys),
        (table_h.at[rows], table),
    )
    for copy in copies:
        copy.wait()
    batches, seqs, _, width = tokens.shape
    normed, _ = standardize(tokens[...].reshape(-1, width).astype(F32))
    normed = (normed * gains[0, 0:1] + offsets[0, 0:1]).astype(BF16)
    raw = dot(normed, w_keys[...])
    for batch in range(batches):
        for seq in range(seqs):
            start = (batch * seqs + seq) * span
            shared[batch, seq] = rotate_keys(raw[start : start + span], table[...]).astype(BF16)


def make_keys(tokens, gains, offsets, w_keys, table):
    batches, seqs, span, width = tokens.shape
    return pl.pallas_call(
        keys_body,
        in_specs=[IN_HBM] * 5,
        out_specs=pl.BlockSpec(memory_space=pltpu.VMEM),
        out_shape=jax.ShapeDtypeStruct((batches, seqs, span, PAIR), BF16),
        scratch_shapes=[
            pltpu.VMEM(tokens.shape, BF16),
            pltpu.VMEM(gains.shape, F32),
            pltpu.VMEM(offsets.shape, F32),
            pltpu.VMEM(w_keys.shape, BF16),
            pltpu.VMEM((span, table.shape[1]), F32),
            pltpu.SemaphoreType.DMA((5,)),
        ],
        compiler_params=pltpu.CompilerParams(vmem_limit_bytes=VMEM_LIMIT),
    )(tokens, gains, offsets, w_keys, table)


def choose_body(meta, mine, other, out):
    out[...] = pick(meta, mine, other)


def choose(meta, mine, other, behind):
    return call(
        choose_body, (1,), [whole(mine.shape)] * 2, whole(mine.shape), jax.ShapeDtypeStruct(mine.shape, mine.dtype), behind=behind
    )(meta, mine, other)


def make_queries(first, w_query, table, queries):
    raw = dot(first, w_query)
    span = table.shape[0]
    for start in range(0, raw.shape[0], span):
        for pair in range(PAIRS):
            lanes = slice(pair * PAIR, (pair + 1) * PAIR)
            queries[start : start + span, lanes] = rotate(raw[start : start + span, lanes], table[...]).astype(BF16)


def front_part(hidden, gains, offsets, table, w_query, w_in, queries, normed, second, waits):
    values = hidden.astype(F32)
    waits(0)
    unit, _ = standardize(values)
    first = (unit * gains[0, 0:1] + offsets[0, 0:1]).astype(BF16)
    feed = (unit * gains[0, 1:2] + offsets[0, 1:2]).astype(BF16)
    if normed is not None:
        normed[...] = first
        second[...] = feed
    waits(1)
    make_queries(first, w_query[...], table, queries)
    return values, feed


def pick(meta, mine, other):
    return jnp.where(meta[2] == 0, mine[...], other[...])


def front_body(save, block, meta, hidden_h, gains_h, offsets_h, table_h, w_query_h, w_in_h, *rest):
    if save:
        came_h, chosen, queries, normed, second, active, slope, *rest = rest
        hidden, gains, offsets, table, w_query, w_in, sems, came = rest
    else:
        w_back_h, queries, result, hidden, gains, offsets, table, w_query, w_in, w_back, sems = rest
        normed = second = None
    span = table.shape[0]
    inner = w_in.shape[1]

    def run():
        rows = pl.ds(pl.multiple_of(meta[0] * span, span), span)
        pairs = [
            (hidden_h, hidden),
            (gains_h, gains),
            (offsets_h, offsets),
            (w_query_h.at[0], w_query),
            (table_h.at[rows], table),
        ]
        for start in range(0, inner, block):
            lanes = pl.ds(start, block)
            pairs.append((w_in_h.at[0, :, lanes], w_in.at[:, lanes]))
            if not save:
                pairs.append((w_back_h.at[0, lanes, :], w_back.at[lanes, :]))
        if save:
            pairs.append((came_h, came))
        copies = fetch(sems, *pairs)

        def waits(stage):
            for copy in copies[1:3] if stage == 0 else copies[3:5]:
                copy.wait()

        copies[0].wait()
        flat = hidden[...].reshape(-1, hidden.shape[-1])
        if save:
            copies[-1].wait()
            flat = jnp.where(meta[2] == 0, flat, came[...])
            chosen[...] = flat
        values, feed = front_part(flat, gains, offsets, table, w_query, w_in, queries, normed, second, waits)
        if not save:
            result[...] = values
        each = 1 if save else 2
        for step in range(inner // block):
            lanes = slice(step * block, (step + 1) * block)
            copies[5 + each * step].wait()
            value, rate = gelu_parts(dot(feed, w_in[:, lanes]))
            value = value.astype(BF16)
            if save:
                active[:, lanes] = value
                slope[:, lanes] = rate.astype(BF16)
            else:
                copies[6 + each * step].wait()
                result[...] += dot(value, w_back[lanes, :])

    if save:
        run()
    else:
        pl.when(meta[2] == 0)(run)


def front(meta, hidden, gains, offsets, table, w_query, w_in, w_back=None, came=None):
    save = came is not None
    shape = hidden.shape
    width = shape[-1]
    rows = int(np.prod(shape[:-1]))
    span = rows // 2 if save else shape[-2]
    inner = w_in.shape[2]
    block = 768 if inner % 768 == 0 else inner
    operands = [hidden, gains, offsets, table, w_query, w_in, came if save else w_back]
    if save:
        outs = [(rows, width, BF16)] * 4 + [(rows, inner, BF16)] * 2
    else:
        outs = [(rows, width, BF16), (rows, width, F32)]
    scratch = [
        pltpu.VMEM(shape, BF16),
        pltpu.VMEM(gains.shape, F32),
        pltpu.VMEM(offsets.shape, F32),
        pltpu.VMEM((span, table.shape[1]), F32),
        pltpu.VMEM((width, width), BF16),
        pltpu.VMEM((width, inner), BF16),
    ]
    if not save:
        scratch.append(pltpu.VMEM((inner, width), BF16))
    scratch.append(pltpu.SemaphoreType.DMA((6 + (1 if save else 2) * (inner // block),)))
    if save:
        scratch.append(pltpu.VMEM(shape, BF16))
    return call(
        partial(front_body, save, block),
        (1,),
        [IN_HBM] * len(operands),
        [whole(out[:2]) for out in outs],
        [shape_of(*out) for out in outs],
        scratch,
        limit=VMEM_MOST,
    )(meta, *operands)


def spread_pair(values, low):
    lane = lax.broadcasted_iota(jnp.int32, values.shape, 1)
    here = lane < HEAD_DIM if low else lane >= HEAD_DIM
    turned = pltpu.roll(values.astype(F32), HEAD_DIM, 1).astype(BF16)
    one, two = (values, turned) if low else (turned, values)
    zero = jnp.zeros_like(values)
    return jnp.where(here, one, zero), jnp.where(here, two, zero)


def mask_rows(meta, span, length, seq_length, first_key=0):
    key = lax.broadcasted_iota(jnp.int32, (span, length), 1) + first_key
    query = lax.broadcasted_iota(jnp.int32, (span, length), 0) + meta[0] * span
    return jnp.where(key <= jnp.minimum(query, seq_length - 1), 0.0, MASKED)


GROUP = 4
QUARTERS = 4


def by_quarters(meta, span, length, seq_length, run):
    quarter = length // QUARTERS
    needed = jnp.minimum((meta[0] + 1) * span, seq_length)
    count = lax.div(needed + quarter - 1, quarter)
    for number in range(1, QUARTERS + 1):
        pl.when(count == number)(partial(run, number * quarter))


def value_sides(pairs):
    lane = lax.broadcasted_iota(jnp.int32, pairs.shape, 1)
    high = jnp.where(lane < HEAD_DIM, jnp.ones_like(pairs), pairs)
    return pltpu.roll(high.astype(F32), HEAD_DIM, 1).astype(BF16), high


def attend_rows(pairs, mask, stacked, mixed):
    span = mixed.shape[0]
    side = value_sides(pairs)[0]
    lane = lax.broadcasted_iota(jnp.int32, (span, PAIR), 1)
    for start in range(0, HEADS, GROUP):
        all_scores = dot_nt(stacked[start * span : (start + GROUP) * span], pairs)
        weights = []
        for head in range(start, start + GROUP):
            place = (head - start) * span
            scores = all_scores[place : place + span] + mask
            top = jnp.max(scores, axis=1, keepdims=True)
            weights.append(jnp.exp2((scores - top) * (SCALE * LOG2E)).astype(BF16))
        summed = dot(jnp.concatenate(weights, axis=0), side)
        summed = summed * pltpu.roll(1.0 / summed, HEAD_DIM, 1)
        for head in range(0, GROUP, 2):
            one = summed[head * span : (head + 1) * span]
            two = pltpu.roll(summed[(head + 1) * span : (head + 2) * span], HEAD_DIM, 1)
            lanes = slice((start + head) // 2 * PAIR, ((start + head) // 2 + 1) * PAIR)
            mixed[:, lanes] = jnp.where(lane < HEAD_DIM, one, two).astype(BF16)


def attend_body(batch, meta, queries, shared, w_out_h, base, result, mixed, stacked, mask, w_out, sems):
    seq = pl.program_id(0)
    span = queries.shape[0]
    length = mask.shape[1]
    seq_length = meta[4 + 2 * batch + seq]

    def run():
        @pl.when(seq == 0)
        def _():
            fetch(sems, (w_out_h.at[0], w_out))

        for pair in range(PAIRS):
            for side, value in enumerate(spread_pair(queries[:, pair * PAIR : (pair + 1) * PAIR], True)):
                stacked[(2 * pair + side) * span : (2 * pair + side + 1) * span] = value
        def some(keys):
            mask[:, :keys] = mask_rows(meta, span, keys, seq_length)
            pairs = shared[: keys // span, 0, 0].reshape(keys, PAIR)
            attend_rows(pairs, mask[:, :keys], stacked, mixed)

        by_quarters(meta, span, length, seq_length, some)

        @pl.when(seq == 0)
        def _():
            pltpu.make_async_copy(w_out_h.at[0], w_out, sems.at[0]).wait()

        result[...] = (base[...] + dot(mixed[...], w_out[...])).astype(BF16)

    pl.when(meta[2] == 0)(run)


def attend(batch, meta, queries, gathered, w_out, base):
    width = queries.shape[1]
    count, _, seqs, span, _ = gathered.shape
    rows = seqs * span
    length = count * span
    return call(
        partial(attend_body, batch),
        (seqs,),
        [
            pl.BlockSpec((span, width), lambda s, meta: (batch * seqs + s, 0)),
            pl.BlockSpec((count, 1, 1, span, PAIR), lambda s, meta: (0, batch, s, 0, 0)),
            IN_HBM,
            pl.BlockSpec((span, width), lambda s, meta: (batch * seqs + s, 0)),
        ],
        pl.BlockSpec((span, width), lambda s, meta: (s, 0)),
        jax.ShapeDtypeStruct((rows, width), BF16),
        [
            pltpu.VMEM((span, width), BF16),
            pltpu.VMEM((HEADS * span, PAIR), BF16),
            pltpu.VMEM((span, length), F32),
            pltpu.VMEM((width, width), BF16),
            pltpu.SemaphoreType.DMA((1,)),
        ],
    )(meta, queries, gathered, w_out, base)


def softmax_back(fresh, pairs, sides, mask, q_sides, d_sides, saved, first_head, weights_sc, d_scores_sc):
    span = q_sides[0].shape[0]
    count = len(q_sides)
    lane = lax.broadcasted_iota(jnp.int32, (span, PAIR), 1)
    products = dot_nt(jnp.concatenate(q_sides + d_sides, axis=0), pairs)
    for n in range(count):
        rows = slice(n * span, (n + 1) * span)
        here = lane == first_head + n
        scores = products[rows]
        d_weights = products[(count + n) * span : (count + n + 1) * span]
        if fresh:
            scores = scores + mask
            top = jnp.max(scores, axis=1, keepdims=True)
            weights = jnp.exp2((scores - top) * (SCALE * LOG2E))
            sums = jnp.sum(weights, axis=1, keepdims=True)
            weights = weights * (1.0 / sums)
            saved = jnp.where(here, top * (SCALE * LOG2E) + jnp.log2(sums), saved)
        else:
            norm = jnp.sum(jnp.where(here, saved, 0.0), axis=1, keepdims=True)
            weights = jnp.exp2(scores * (SCALE * LOG2E) + mask - norm)
        lean = jnp.sum(weights * d_weights, axis=1, keepdims=True)
        weights_sc[rows] = weights.astype(BF16)
        d_scores_sc[rows] = (weights * (d_weights - lean)).astype(BF16)
    return saved


def attend_back_part(fresh, seq_length, meta, rows, pairs, queries, d_mixed, table, norms, mixed, d_raw, mask_sc, weights_sc, d_scores_sc, total):
    span = table.shape[0]
    length = pairs.shape[0]
    lane = lax.broadcasted_iota(jnp.int32, (span, PAIR), 1)
    mask_sc[:, :length] = mask_rows(meta, span, length, seq_length)
    mask = mask_sc[:, :length]
    side = value_sides(pairs)[0] if fresh else None
    saved = jnp.zeros((span, PAIR), F32) if fresh else norms[rows]
    for number, first_head in enumerate(range(0, HEADS, GROUP)):
        q_sides, d_sides = [], []
        for pair in range(first_head // 2, (first_head + GROUP) // 2):
            lanes = slice(pair * PAIR, (pair + 1) * PAIR)
            q_sides += spread_pair(queries[rows, lanes], True)
            d_sides += spread_pair(d_mixed[rows, lanes], False)
        slot = number % 2
        weights = weights_sc.at[slot, :, :length]
        d_scores = d_scores_sc.at[slot, :, :length]
        saved = softmax_back(fresh, pairs, side, mask, q_sides, d_sides, saved, first_head, weights, d_scores)
        weights, d_scores = weights[...], d_scores[...]
        d_query = dot(d_scores, pairs)
        out = dot(weights, side) if fresh else None
        scaled = [(value.astype(F32) * SCALE).astype(BF16) for value in q_sides]
        part = dot_tn(
            jnp.concatenate([d_scores, weights], axis=0), jnp.concatenate(scaled + d_sides, axis=0)
        )
        if number == 0:
            total[:length] = part
        else:
            total[:length] += part
        for n in range(0, GROUP, 2):
            pair = (first_head + n) // 2
            lanes = slice(pair * PAIR, (pair + 1) * PAIR)

            def join(values):
                one = values[n * span : (n + 1) * span]
                two = values[(n + 1) * span : (n + 2) * span]
                return jnp.where(lane < HEAD_DIM, one, pltpu.roll(two, HEAD_DIM, 1))

            if fresh:
                mixed[rows, lanes] = join(out).astype(BF16)
            d_raw[rows, lanes] = rotate(join(d_query) * SCALE, table[...], -1.0).astype(BF16)
    if fresh:
        norms[rows] = saved


def attend_back_all(fresh, batch, meta, shared, d_shared, span, total, run):
    count, seqs = d_shared.shape[:2]
    length = count * span

    @pl.loop(0, seqs)
    def _(seq):
        rows = pl.ds(pl.multiple_of(seq * span, span), span)
        seq_length = meta[4 + 2 * batch + seq]

        def some(keys):
            pairs = shared[: keys // span, 0, pl.ds(seq, 1)].reshape(keys, PAIR)
            run(seq_length, rows, pairs)
            if keys < length:
                total[keys:] = jnp.zeros((length - keys, PAIR), F32)

        by_quarters(meta, span, length, seq_length, some)
        d_shared[:, pl.ds(seq, 1)] = total[...].astype(BF16).reshape(count, 1, span, PAIR)


def feed_back_part(upstream, slope, w_in, w_back, d_upper, block, waits):
    inner = slope.shape[1]
    two = None
    for step in range(inner // block):
        lanes = slice(step * block, (step + 1) * block)
        waits(step)
        rate = (dot_nt(upstream, w_back[lanes, :]) * slope[:, lanes].astype(F32)).astype(BF16)
        d_upper[:, lanes] = rate
        part = dot_nt(rate, w_in[:, lanes])
        two = part if two is None else two + part
    return two


def chain_body(front, which, block, meta, up, hid, *rest, push):
    if front:
        came, shared, offsets_h, *rest = rest
    else:
        back, queries, slope, first_keys, shared, *rest = rest
    gains_h, table_h, w_query_h, w_out_h, w_in_h, w_back_h, *rest = rest
    if front:
        hidden, queries, normed, second, active, slope, *rest = rest
        hidden[...] = pick(meta, hid, came)
        push(hidden)
        upstream = up
    else:
        upstream, *rest = rest
        upstream[...] = pick(meta, back, up)
        push(upstream)
        hidden = hid
    mixed, norms, d_shared, d_low, *rest = rest
    if not front:
        d_raw, d_upper, d_hidden, d_norms, keys_keep, keys_send, *rest = rest
    gains, table, w_query, w_out, w_in, w_back, d_mixed, mask_sc, weights_sc, d_scores_sc, total_sc, sems, *rest = rest
    if front:
        offsets, d_raw, d_upper = rest
    span = table.shape[0]
    inner = slope.shape[1]
    steps = inner // block
    batch = which[0] + which[1] * meta[2]
    place = pl.ds(pl.multiple_of(meta[0] * span, span), span)
    operands = [(gains_h, gains), (w_query_h.at[0], w_query), (table_h.at[place], table), (w_out_h.at[0], w_out)]
    for start in range(0, inner, block):
        lanes = pl.ds(start, block)
        operands.append((w_in_h.at[0, :, lanes], w_in.at[:, lanes]))
    for start in range(0, inner, block):
        lanes = pl.ds(start, block)
        operands.append((w_back_h.at[0, lanes, :], w_back.at[lanes, :]))
    if front:
        operands.append((offsets_h, offsets))
    copies = fetch(sems, *operands)
    if front:

        def waits(stage):
            for copy in (copies[0], copies[-1]) if stage == 0 else copies[1:3]:
                copy.wait()

        _, feed = front_part(hidden[...], gains, offsets, table, w_query, w_in, queries, normed, second, waits)
        for step in range(steps):
            lanes = slice(step * block, (step + 1) * block)
            copies[4 + step].wait()
            value, rate = gelu_parts(dot(feed, w_in[:, lanes]))
            active[:, lanes] = value.astype(BF16)
            slope[:, lanes] = rate.astype(BF16)
        push(queries, normed, second, active, slope)
    else:
        copies[2].wait()
    copies[3].wait()
    d_mixed[...] = dot_nt(upstream[...], w_out[...]).astype(BF16)

    def run(seq_length, rows, pairs):
        attend_back_part(
            True, seq_length, meta, rows, pairs, queries, d_mixed, table, norms, mixed, d_raw,
            mask_sc, weights_sc, d_scores_sc, total_sc
        )

    attend_back_all(True, batch, meta, shared, d_shared, span, total_sc, run)
    push(mixed, norms, d_shared)
    if not front:
        push(d_raw)
        for out, core in ((keys_keep, meta[1]), (keys_send, 1 - meta[1])):
            for pair in range(out.shape[0]):
                for slot, keys in enumerate((first_keys, d_shared)):
                    out[pair, slot] = keys[pl.ds(2 * pair + core, 1)].reshape(out.shape[2:])
        push(keys_keep, keys_send)

    def more_waits(step):
        if not front:
            copies[4 + step].wait()
        copies[4 + steps + step].wait()

    two = feed_back_part(upstream[...], slope, w_in, w_back, d_upper, block, more_waits)
    if not front:
        push(d_upper)
        for copy in copies[:2]:
            copy.wait()
    one = dot_nt(d_raw[...], w_query[...])
    unit, scale = standardize(hidden[...].astype(F32))
    total = upstream[...].astype(F32) + norm_back(one * gains[0, 0:1] + two * gains[0, 1:2], 1.0, unit, scale)
    d_low[...] = total.astype(BF16)
    push(d_low)
    if not front:
        d_hidden[...] = total
        push(d_hidden)
        d_norms[...] = sum_rows(one * unit, one, two * unit, two)
        push(d_norms)


def chain(which, meta, upstream, hidden, more, gathered, gains, offsets, table, w_query, w_out, w_in, w_back):
    rows, width = hidden.shape
    count, _, seqs, span, _ = gathered.shape
    inner = w_in.shape[2]
    length = count * span
    block = inner // 2
    front = len(more) == 1
    flat = whole((rows, width))
    shared_shape = (count, seqs, span, PAIR)
    shared_spec = pl.BlockSpec((count, 1, seqs, span, PAIR), lambda j, meta: (0, which[0] + which[1] * meta[2], 0, 0, 0))
    outs = [(rows, width, BF16)] * 4 + [(rows, inner, BF16)] * 2 if front else [(rows, width, BF16)]
    outs += [(rows, width, BF16), (rows, PAIR, F32), None, (rows, width, BF16)]
    if not front:
        outs += [(rows, width, BF16), (rows, inner, BF16), (rows, width, F32), (8, width, F32)]
        outs += [(count // 2, 2, seqs, span, PAIR, BF16)] * 2
    if front:
        operands, specs = [upstream, hidden, *more, gathered, offsets], [flat, flat, flat, shared_spec, IN_HBM]
    else:
        operands = [upstream, hidden, *more, gathered]
        specs = [flat, flat, flat, flat, whole((rows, inner)), whole(shared_shape), shared_spec]
    return call(
        partial(chain_body, front, which, block),
        (1,),
        specs + [IN_HBM] * 6,
        [whole(shared_shape) if out is None else whole(out[:-1]) for out in outs],
        [jax.ShapeDtypeStruct(shared_shape, BF16) if out is None else jax.ShapeDtypeStruct(out[:-1], out[-1]) for out in outs],
        [
            pltpu.VMEM(gains.shape, F32),
            pltpu.VMEM((span, table.shape[1]), F32),
            pltpu.VMEM((width, width), BF16),
            pltpu.VMEM((width, width), BF16),
            pltpu.VMEM((width, inner), BF16),
            pltpu.VMEM((inner, width), BF16),
            pltpu.VMEM((rows, width), BF16),
            pltpu.VMEM((span, length), F32),
            pltpu.VMEM((2, GROUP * span, length), BF16),
            pltpu.VMEM((2, GROUP * span, length), BF16),
            pltpu.VMEM((length, PAIR), F32),
            pltpu.SemaphoreType.DMA((5 + 2 * (inner // block),)),
        ]
        + ([pltpu.VMEM(offsets.shape, F32), pltpu.VMEM((rows, width), BF16), pltpu.VMEM((rows, inner), BF16)] if front else []),
        pushed=tuple(range(len(outs))),
        limit=VMEM_MOST,
    )(meta, *operands, gains, table, w_query, w_out, w_in, w_back)


def attend_back_body(which, split, meta, upstream, queries, norms, shared, *rest, push):
    (first_own, *rest) = rest
    (up_d, raw_d, mixed_c, mixed_d, normed_c, normed_d, w_out_h, w_query_h, table_h) = rest[:9]
    (key_keep, key_send, d_normed) = rest[9:12]
    halves = rest[12:14] if split else rest[12:13]
    (d_raw, d_mixed, mask_sc, weights_sc, d_scores_sc, total_sc, d_shared, table, w_out, w_query, sems) = rest[12 + len(halves) :][:11]
    span = table.shape[0]
    batch = which[0] + which[1] * meta[2]
    place = pl.ds(pl.multiple_of(meta[0] * span, span), span)
    copies = fetch(sems, (w_out_h.at[0], w_out), (table_h.at[place], table), (w_query_h.at[0], w_query))
    copies[0].wait()
    d_mixed[...] = dot_nt(upstream[...], w_out[...]).astype(BF16)
    copies[1].wait()

    def run(seq_length, rows, pairs):
        attend_back_part(
            False, seq_length, meta, rows, pairs, queries, d_mixed, table, norms, None, d_raw,
            mask_sc, weights_sc, d_scores_sc, total_sc
        )

    attend_back_all(False, batch, meta, shared, d_shared, span, total_sc, run)
    for out, core in ((key_keep, meta[1]), (key_send, 1 - meta[1])):
        for pair in range(out.shape[0]):
            for slot, keys in enumerate((first_own, d_shared)):
                part = keys[pl.ds(2 * pair + core, 1)].reshape(out.shape[2:])
                out[pair, slot] = part
    push(key_keep, key_send)
    copies[2].wait()
    d_normed[...] = dot_nt(d_raw[...], w_query[...])
    push(d_normed)
    both = jnp.concatenate([upstream[...], up_d[...]], axis=0)
    left = jnp.concatenate([mixed_c[...], mixed_d[...]], axis=0)
    outer = dot_tn(left, both).astype(BF16)
    both = jnp.concatenate([d_raw[...], raw_d[...]], axis=0)
    left = jnp.concatenate([normed_c[...], normed_d[...]], axis=0)
    query = dot_tn(left, both).astype(BF16)
    width = both.shape[1]
    if len(halves) == 1:
        halves[0][:, :width] = outer
        halves[0][:, width:] = query
        push(halves[0])
        return
    keep, send, pair_sc = halves[0], halves[1], rest[-1]
    pair_sc[..., :width] = outer.reshape(pair_sc.shape[:3] + (width,))
    pair_sc[..., width:] = query.reshape(pair_sc.shape[:3] + (width,))
    keep[...] = pair_sc[:, pl.ds(meta[1], 1)].reshape(keep.shape)
    send[...] = pair_sc[:, pl.ds(1 - meta[1], 1)].reshape(send.shape)
    push(keep, send)


def attend_back(
    which, shards, meta, upstream, queries, norms, gathered, first_own, up_d, raw_d, mixed_c, mixed_d, normed_c, normed_d, w_out, w_query, table,
    behind=()
):
    rows, width = queries.shape
    count, _, seqs, span, _ = gathered.shape
    length = count * span
    shared_shape = (count, seqs, span, PAIR)
    key_half = (count // 2, 2, seqs, span, PAIR)
    part = width // shards
    split = part % 16 == 0
    if split:
        pairs = [(shards // 2, part, 2 * width)] * 2
    else:
        pairs = [(width, 2 * width)]
    outs = call(
        partial(attend_back_body, which, split),
        (1,),
        [whole((rows, width))] * 2
        + [whole(norms.shape)]
        + [pl.BlockSpec((count, 1, seqs, span, PAIR), lambda j, meta: (0, which[0] + which[1] * meta[2], 0, 0, 0))]
        + [whole(shared_shape)]
        + [whole((rows, width))] * 6
        + [IN_HBM] * 3,
        [whole(key_half)] * 2 + [whole((rows, width))] + [whole(shape) for shape in pairs],
        [
            jax.ShapeDtypeStruct(key_half, BF16),
            jax.ShapeDtypeStruct(key_half, BF16),
            shape_of(rows, width, F32),
        ]
        + [jax.ShapeDtypeStruct(shape, BF16) for shape in pairs],
        [
            pltpu.VMEM((rows, width), BF16),
            pltpu.VMEM((rows, width), BF16),
            pltpu.VMEM((span, length), F32),
            pltpu.VMEM((2, GROUP * span, length), BF16),
            pltpu.VMEM((2, GROUP * span, length), BF16),
            pltpu.VMEM((length, PAIR), F32),
            pltpu.VMEM(shared_shape, BF16),
            pltpu.VMEM((span, table.shape[1]), F32),
            pltpu.VMEM((width, width), BF16),
            pltpu.VMEM((width, width), BF16),
            pltpu.SemaphoreType.DMA((3,)),
        ]
        + ([pltpu.VMEM((shards // 2, 2, part, 2 * width), BF16)] if split else []),
        behind=behind,
        pushed=tuple(range(3 + len(pairs))),
    )(meta, upstream, queries, norms, gathered, first_own, up_d, raw_d, mixed_c, mixed_d, normed_c, normed_d, w_out, w_query, table)
    if split:
        return outs
    return (*outs[:3], *split_cores(outs[3].reshape(shards, part, 2 * width)))


def finish_body(block, meta, *rest):
    hidden, mixed, active = rest[0:2], rest[2:4], rest[4:6]
    w_out_h, w_back_h, outs, w_out, w_back, sems = rest[6:]
    inner = w_back.shape[0]
    pairs = [(w_out_h.at[0], w_out)]
    for start in range(0, inner, block):
        pairs.append((w_back_h.at[0, pl.ds(start, block), :], w_back.at[pl.ds(start, block), :]))
    copies = fetch(sems, *pairs)
    rows = hidden[0].shape[0]

    def both(refs, lanes=slice(None)):
        return jnp.concatenate([refs[0][:, lanes], refs[1][:, lanes]], axis=0)

    copies[0].wait()
    total = both(hidden).astype(F32) + dot(both(mixed), w_out[...])
    for step in range(inner // block):
        lanes = slice(step * block, (step + 1) * block)
        copies[1 + step].wait()
        total += dot(both(active, lanes), w_back[lanes, :])
    section = meta[2]
    outs[pl.ds(1 - section, 1)] = total[:rows].astype(BF16)[None]
    outs[pl.ds(section, 1)] = total[rows:].astype(BF16)[None]


def finish(meta, hidden, mixed, active, w_out, w_back, behind=()):
    rows, width = hidden[0].shape
    inner = active[0].shape[1]
    block = 768 if inner % 768 == 0 else inner
    return call(
        partial(finish_body, block),
        (1,),
        [whole((rows, width))] * 4 + [whole((rows, inner))] * 2 + [IN_HBM] * 2,
        whole((2, rows, width)),
        jax.ShapeDtypeStruct((2, rows, width), BF16),
        [
            pltpu.VMEM((width, width), BF16),
            pltpu.VMEM((inner, width), BF16),
            pltpu.SemaphoreType.DMA((1 + inner // block,)),
        ],
        behind=behind,
    )(meta, *hidden, *mixed, *active, w_out, w_back)


def sum_rows(*values):
    sums = [jnp.sum(value, axis=0, keepdims=True) for value in values]
    return jnp.concatenate(sums + [jnp.zeros_like(sums[0])] * (8 - len(sums)), axis=0)


def feed_back_body(block, meta, upstream, slope, w_in_h, w_back_h, d_upper, d_second, w_in, w_back, sems):
    inner = slope.shape[1]
    operands = []
    for start in range(0, inner, block):
        lanes = pl.ds(start, block)
        operands.append((w_back_h.at[0, lanes, :], w_back.at[lanes, :]))
        operands.append((w_in_h.at[0, :, lanes], w_in.at[:, lanes]))
    copies = fetch(sems, *operands)

    def waits(step):
        copies[2 * step].wait()
        copies[2 * step + 1].wait()

    d_second[...] = feed_back_part(upstream[...], slope, w_in, w_back, d_upper, block, waits)


def feed_back(meta, upstream, slope, w_in, w_back):
    rows, width = upstream.shape
    inner = w_in.shape[2]
    block = 768 if inner % 768 == 0 else inner
    return call(
        partial(feed_back_body, block),
        (1,),
        [whole((rows, width)), whole((rows, inner))] + [IN_HBM] * 2,
        [whole((rows, inner)), whole((rows, width))],
        [shape_of(rows, inner, BF16), shape_of(rows, width, F32)],
        [
            pltpu.VMEM((width, inner), BF16),
            pltpu.VMEM((inner, width), BF16),
            pltpu.SemaphoreType.DMA((2 * (inner // block),)),
        ],
    )(meta, upstream, slope, w_in, w_back)


def store_halves(meta, block, keep, send, scratch):
    groups, _, part, lanes = scratch.shape
    scratch[...] = block.astype(BF16).reshape(groups, 2, part, lanes)
    core = meta[1]
    keep[...] = scratch[:, pl.ds(core, 1)].reshape(keep.shape)
    send[...] = scratch[:, pl.ds(1 - core, 1)].reshape(send.shape)


def late_feed_body(shards, block, meta, active_c, active_d, up, back, up_d, slope, *rest, push):
    w_in_h, w_back_h, keep, send, d_upper, d_second, up_c, w_in, w_back, scratch, sems = rest
    up_c[...] = pick(meta, back, up)
    push(up_c)
    inner = w_in.shape[1]
    operands = []
    for start in range(0, inner, block):
        lanes = pl.ds(start, block)
        operands.append((w_back_h.at[0, lanes, :], w_back.at[lanes, :]))
        operands.append((w_in_h.at[0, :, lanes], w_in.at[:, lanes]))
    copies = fetch(sems, *operands)
    part = inner // shards
    both = jnp.concatenate([up_c[...], up_d[...]], axis=0)
    for group in range(shards // 2):
        lanes = slice(group * 2 * part, (group + 1) * 2 * part)
        left = jnp.concatenate([active_c[:, lanes], active_d[:, lanes]], axis=0)
        scratch[group] = dot_tn(left, both).astype(BF16).reshape(2, part, both.shape[1])
    core = meta[1]
    keep[...] = scratch[:, pl.ds(core, 1)].reshape(keep.shape)
    send[...] = scratch[:, pl.ds(1 - core, 1)].reshape(send.shape)
    push(send, keep)

    def waits(step):
        copies[2 * step].wait()
        copies[2 * step + 1].wait()

    d_second[...] = feed_back_part(up_c[...], slope, w_in, w_back, d_upper, block, waits)
    push(d_upper, d_second)


def late_feed(meta, shards, active_c, active_d, up, back, up_d, slope, w_in, w_back, behind=()):
    rows, width = up.shape
    inner = w_in.shape[2]
    part = inner // shards
    if part % 64:
        up_c = jnp.where(meta[2] == 0, back, up)
        halves = weights_full(meta, shards, active_c, active_d, up_c, up_d)
        return (*halves, *feed_back(meta, up_c, slope, w_in, w_back), up_c)
    block = 768 if inner % 768 == 0 else inner
    half = (shards // 2, part, width)
    return call(
        partial(late_feed_body, shards, block),
        (1,),
        [whole((rows, inner))] * 2 + [whole((rows, width))] * 3 + [whole((rows, inner))] + [IN_HBM] * 2,
        [whole(half), whole(half), whole((rows, inner)), whole((rows, width)), whole((rows, width))],
        [jax.ShapeDtypeStruct(half, BF16)] * 2 + [shape_of(rows, inner, BF16), shape_of(rows, width, F32), shape_of(rows, width, BF16)],
        [
            pltpu.VMEM((width, inner), BF16),
            pltpu.VMEM((inner, width), BF16),
            pltpu.VMEM((shards // 2, 2, part, width), BF16),
            pltpu.SemaphoreType.DMA((2 * (inner // block),)),
        ],
        behind=behind,
        pushed=(0, 1, 2, 3, 4),
        limit=VMEM_MOST,
    )(meta, active_c, active_d, up, back, up_d, slope, w_in, w_back)


def weights_full_body(meta, left_c, left_d, right_c, right_d, full, turned_c, turned_d):
    @pl.when(pl.program_id(0) == 0)
    def _():
        turned_c[...] = left_c[...].T
        turned_d[...] = left_d[...].T

    block = dot(turned_c[...], right_c[...]) + dot(turned_d[...], right_d[...])
    full[...] = block.astype(BF16)


def weights_full(meta, shards, left_c, left_d, right_c, right_d):
    rows, tall = left_c.shape
    wide = right_c.shape[1]
    block = 256
    full = call(
        weights_full_body,
        (wide // block,),
        [whole((rows, tall))] * 2 + [pl.BlockSpec((rows, block), lambda j, meta: (0, j))] * 2,
        pl.BlockSpec((tall, block), lambda j, meta: (0, j)),
        jax.ShapeDtypeStruct((tall, wide), BF16),
        [pltpu.VMEM((tall, rows), BF16), pltpu.VMEM((tall, rows), BF16)],
    )(meta, left_c, left_d, right_c, right_d)
    return split_cores(full.reshape(shards, tall // shards, wide))


def weights_wide_body(meta, left_c, left_d, right_c, right_d, keep, send, scratch, turned_c, turned_d):
    @pl.when(pl.program_id(0) == 0)
    def _():
        turned_c[...] = left_c[...].T
        turned_d[...] = left_d[...].T

    block = dot(turned_c[...], right_c[...]) + dot(turned_d[...], right_d[...])
    store_halves(meta, block, keep, send, scratch)


def weights_wide(meta, shards, left_c, left_d, right_c, right_d):
    rows, tall = left_c.shape
    wide = right_c.shape[1]
    block = wide // 2
    part = tall // shards
    if part % 16:
        return weights_full(meta, shards, left_c, left_d, right_c, right_d)
    spec = pl.BlockSpec((shards // 2, part, block), lambda j, meta: (0, 0, j))
    shape = jax.ShapeDtypeStruct((shards // 2, part, wide), BF16)
    return call(
        weights_wide_body,
        (wide // block,),
        [whole((rows, tall))] * 2 + [pl.BlockSpec((rows, block), lambda j, meta: (0, j))] * 2,
        [spec, spec],
        [shape, shape],
        [
            pltpu.VMEM((shards // 2, 2, part, block), BF16),
            pltpu.VMEM((tall, rows), BF16),
            pltpu.VMEM((tall, rows), BF16),
        ],
    )(meta, left_c, left_d, right_c, right_d)


def tail_body(
    meta, keys, hid_d, hid_c, nrm_d, nrm_c, dh_d, sums_d, up_c, one_c, two_c,
    gains_h, w_keys_h, table_h, grads, *rest
):
    small, (gains, w_keys, table, sems) = rest[:2], rest[2:6]
    section = meta[2]
    first = (section == 0).astype(F32)
    span = table.shape[0]
    seqs = keys.shape[1]
    rows = pl.ds(pl.multiple_of(meta[0] * span, span), span)
    copies = fetch(sems, (gains_h, gains), (w_keys_h, w_keys), (table_h.at[rows], table))
    for copy in copies:
        copy.wait()
    keys_sum = None
    norm_sum = sums_d[...]
    for slot, (hidden, normed) in enumerate(((hid_d, nrm_d), (hid_c, nrm_c))):
        raw = []
        for seq in range(seqs):
            both = keys[slot, seq] * first
            raw.append(rotate_keys(both, table[...], -1.0).astype(BF16))
        raw = jnp.concatenate(raw, axis=0)
        part = dot_tn(normed[...], raw)
        keys_sum = part if keys_sum is None else keys_sum + part
        one = dot_nt(raw, w_keys[...])
        unit, scale = standardize(hidden[...].astype(F32))
        if slot == 0:
            total = dh_d[...] + norm_back(one, gains[0, 0:1], unit, scale)
            norm_sum += sum_rows(one * unit, one)
        else:
            one, two = one + one_c[...], two_c[...]
            total = up_c[...].astype(F32) + norm_back(one * gains[0, 0:1] + two * gains[0, 1:2], 1.0, unit, scale)
            norm_sum += sum_rows(one * unit, one, two * unit, two)
        batch = section if slot == 0 else 1 - section
        grads[pl.ds(batch, 1)] = total[None]
    if len(rest) == 6:
        small[0][...] = keys_sum.astype(BF16)
        small[1][...] = norm_sum
        return
    gather = rest[6]
    groups, _, part, _ = gather.shape
    share = part // 2
    width = keys_sum.shape[0]
    turned = jnp.concatenate([norm_sum, jnp.zeros((PAIR - 8, width), F32)], axis=0).T
    for shard in range(2 * groups):
        place = gather.at[shard // 2, shard % 2]
        for half in range(2):
            start = half * width // 2 + shard * share
            place[half * share : (half + 1) * share, :PAIR] = keys_sum[start : start + share]
        place[:, PAIR:] = turned[shard * part : (shard + 1) * part]
    small[0][...] = gather[:, pl.ds(meta[1], 1)].reshape(small[0].shape).astype(BF16)
    small[1][...] = gather[:, pl.ds(1 - meta[1], 1)].reshape(small[1].shape).astype(BF16)


def small_parts(shards, sections, d_keys, d_norms):
    width = d_keys.shape[0]
    share = width // (sections * shards)
    d_keys = d_keys.reshape(sections, shards, share, PAIR).transpose(1, 0, 2, 3).reshape(shards, sections * share, PAIR)
    d_norms = d_norms.T.reshape(shards, width // shards, 8)
    d_norms = jnp.pad(d_norms, ((0, 0), (0, 0), (0, PAIR - 8))).astype(BF16)
    return split_cores(jnp.concatenate([d_keys, d_norms], axis=-1))


def tail(shards, sections, meta, *arrays, behind=()):
    rows, width = arrays[1].shape
    span = arrays[0].shape[2]
    gains, w_keys, table = arrays[-3:]
    part = width // shards
    split = part % 16 == 0 and sections == 2
    if split:
        outs = [jax.ShapeDtypeStruct((shards // 2, part, 2 * PAIR), BF16)] * 2
    else:
        outs = [shape_of(width, PAIR, BF16), shape_of(8, width, F32)]
    grads, *small = call(
        tail_body,
        (1,),
        [whole(array.shape) for array in arrays[:-3]] + [IN_HBM] * 3,
        [whole((2, rows, width))] + [whole(out.shape) for out in outs],
        [jax.ShapeDtypeStruct((2, rows, width), F32)] + outs,
        [
            pltpu.VMEM(gains.shape, F32),
            pltpu.VMEM(w_keys.shape, BF16),
            pltpu.VMEM((span, table.shape[1]), F32),
            pltpu.SemaphoreType.DMA((3,)),
        ]
        + ([pltpu.VMEM((shards // 2, 2, part, 2 * PAIR), F32)] if split else []),
        behind=behind,
    )(meta, *arrays)
    return (grads, *small) if split else (grads, *small_parts(shards, sections, *small))


def swap(value, axis, bit):
    count = lax.axis_size(axis)
    return lax.ppermute(value, axis, [(source, source ^ bit) for source in range(count)])


def across(value, steps):
    pairs = [(0, 1)] if steps > 0 else [(1, 0)]
    return lax.ppermute(value, "section", pairs)


def after(value, *others):
    return lax.optimization_barrier((value, *others))[0]


def wide_sum(values):
    total = values[0].astype(F32)
    for value in values[1:]:
        total = total + value.astype(F32)
    return total


class Halving:
    def __init__(self, *parts):
        self.parts = list(parts)

    def prepare(self, axis, bit, low, *hold):
        cut = []
        for value in self.parts:
            places = value.shape[0]
            cut.append(value.reshape(((places // 2, 2) if low else (2, places // 2)) + value.shape[1:]))
        if hold:
            cut[0] = after(cut[0], *hold)
        place = 1 if low else 0
        mine = (lax.axis_index(axis) // bit) % 2
        other = wide_sum([lax.dynamic_index_in_dim(value, 1 - mine, place, keepdims=False) for value in cut])
        self.sent = other.astype(BF16)
        kept = wide_sum([lax.dynamic_index_in_dim(value, mine, place, keepdims=False) for value in cut])
        self.parts = [kept.astype(BF16)]
        self.way = (axis, bit)

    def launch(self, *hold):
        if hold:
            self.sent = after(self.sent, *hold)
        self.parts.append(swap(self.sent, *self.way))

    @property
    def received(self):
        return self.parts[-1]

    def bits(self, axis):
        count = lax.axis_size(axis)
        found = [1 << n for n in range(1 if axis == "ctx" else 0, count.bit_length() - 1)]
        return [(axis, bit, axis == "ctx") for bit in (found if axis == "ctx" else found[::-1])]

    def along(self, steps, hold=(), held=()):
        for step in steps:
            self.prepare(*step, *hold)
            self.launch(*held)
            hold, held = (), ()

    def result(self):
        return wide_sum([value.reshape(value.shape[1:]) for value in self.parts])


def split_cores(value):
    shards, part, lanes = value.shape
    cut = value.reshape(shards // 2, 2, part, lanes)
    core = lax.axis_index("ctx") % 2
    return (
        lax.dynamic_index_in_dim(cut, core, 1, keepdims=False),
        lax.dynamic_index_in_dim(cut, 1 - core, 1, keepdims=False),
    )


def per_device(
    length, tokens, lengths, norm_gains, norm_offsets, w_query, w_keys, w_out, w_in, w_back, cotangent
):
    batches, seqs, span, width = tokens.shape
    rows = seqs * span
    shards = lax.axis_size("dp") * lax.axis_size("ctx")
    section = lax.axis_index("section")
    place = lax.axis_index("ctx")
    first = section == 0
    table = jnp.asarray(rotary_table(length))

    own = make_keys(tokens, norm_gains, norm_offsets, w_keys, table)
    gathered = lax.all_gather(own, "ctx")
    meta = jnp.concatenate(
        [jnp.stack([place, place % 2, section, section]).astype(jnp.int32), lengths.reshape(-1)]
    )
    queries, base = front(meta, tokens, norm_gains, norm_offsets, table, w_query, w_in, w_back)
    chosen = choose(meta, own, across(own, 1), behind=(base,))
    came_a = across(attend(0, meta, queries, gathered, w_out, base), 1)
    came_b = across(attend(1, meta, queries, gathered, w_out, base), 1)
    gathered = lax.all_gather(chosen, "ctx")

    flat = tokens.reshape(batches, rows, width)
    cot = cotangent.reshape(batches, rows, width)

    def chain_of(which, upstream, hidden, *more):
        return chain(
            which, meta, upstream, hidden, more, gathered, norm_gains, norm_offsets, table, w_query, w_out, w_in, w_back
        )

    hid_c, queries_c, normed_c, second_c, active_c, slope_c, mixed_c, norms_c, ds_one, low_one = chain_of(
        PASS_C, cot[0], flat[1], came_a
    )
    back_d = across(low_one, -1)
    hid_d, queries_d, normed_d, second_d, active_d, slope_d = front(
        meta, flat[0], norm_gains, norm_offsets, table, w_query, w_in, came=came_b
    )
    up_d, mixed_d, _, ds_d, low_d, raw_d, upper_d, dh_d, sums_d, keys_keep, keys_send = chain_of(
        PASS_D, cot[1], hid_d, back_d, queries_d, slope_d, ds_one
    )
    back_c = across(low_d, -1)
    sent_keys = wide_sum([keys_keep, swap(keys_send, "ctx", 1)]).astype(BF16)
    came_keys = across(sent_keys, -1)
    keep, send, upper_c, two_c, up_c = late_feed(
        meta, shards, active_c, active_d, cot[0], back_c, up_d, slope_c, w_in, w_back, behind=(sent_keys,)
    )
    back = Halving(keep, swap(send, "ctx", 1))
    groups, depth = back.bits("dp"), back.bits("ctx")
    keep, send = weights_wide(meta, shards, second_c, second_d, upper_c, upper_d)
    inner = Halving(keep, swap(send, "ctx", 1))
    back.prepare(*groups[0], keep)
    back.launch()
    inner.prepare(*depth[0], back.sent)
    inner.launch()
    key_keep, key_send, one_c, keep, send = attend_back(
        PASS_C, shards, meta, up_c, queries_c, norms_c, gathered, ds_d, up_d, raw_d,
        mixed_c, mixed_d, normed_c, normed_d, w_out, w_query, table, behind=(back.sent, inner.sent)
    )
    late = Halving(key_keep, swap(key_send, "ctx", 1), came_keys)
    pair = Halving(keep, swap(send, "ctx", 1))
    back.along(groups[1:])
    back.prepare(*depth[0], one_c)
    inner.prepare(*depth[1], one_c)
    late.prepare(*depth[0], back.sent, inner.sent)
    late.launch()
    pair.prepare(*groups[0], late.sent)
    pair.launch()
    late.along(depth[1:], hold=(pair.sent,))
    back.launch(late.sent)
    inner.launch(back.sent)
    sections = lax.axis_size("section")
    input_grads, keep, send = tail(
        shards, sections, meta, late.result(), hid_d, hid_c, normed_d, normed_c, dh_d, sums_d, up_c, one_c, two_c,
        norm_gains, w_keys, table, behind=(back.sent, inner.sent, pair.sent)
    )
    small = Halving(keep, swap(send, "ctx", 1))
    outs = finish(
        meta, (hid_c, hid_d), (mixed_c, mixed_d), (active_c, active_d), w_out, w_back, behind=(keep,)
    )
    pair.along(groups[1:])
    back.prepare(*depth[1], outs)
    inner.prepare(*(depth[2:] + groups)[0], outs)
    pair.prepare(*depth[0], outs)
    back.launch()
    inner.launch(back.sent)
    pair.launch(inner.sent)
    small.along(groups, hold=(back.sent, inner.sent, pair.sent))
    pair.along(depth[1:], hold=(small.sent,))
    back.along(depth[2:])
    inner.along((depth[2:] + groups)[1:])
    small.along(depth[:1], hold=(pair.sent,))
    grad_back = after(back.result(), small.sent)
    grad_in = after(inner.result(), grad_back)
    small.along(depth[1:], hold=(grad_in,))
    small = small.result()
    pair = pair.result()
    share = width // (sections * shards)
    grad_norms = small[:, PAIR : PAIR + 4]
    keys_both = small[:, :PAIR].reshape(sections, share, PAIR)
    grad_keys = jnp.where(first, keys_both[0], across(keys_both[1], 1))
    grad_keys = jnp.where(lengths[0, 0] > 0, grad_keys, pair[:share, :PAIR])
    return (
        outs.reshape((1,) + tokens.shape),
        input_grads.reshape((1,) + tokens.shape),
        grad_norms[None],
        pair[None, :, width:],
        grad_keys,
        pair[None, :, :width],
        grad_in[None],
        grad_back[None],
    )


def solution(mesh):
    def run(*arrays):
        length = arrays[0].shape[2]
        return jax.shard_map(
            partial(per_device, length),
            mesh=mesh,
            in_specs=(
                P(None, "dp", "ctx", None),
                P(None, "dp"),
                P("section", None, None),
                P("section", None, None),
                P("section", None, None),
                P(),
                P("section", None, None),
                P("section", None, None),
                P("section", None, None),
                P(None, "dp", "ctx", None),
            ),
            out_specs=(
                P("section", None, "dp", "ctx", None),
                P("section", None, "dp", "ctx", None),
                P("section", ("dp", "ctx"), None),
                P("section", ("dp", "ctx"), None),
                P(("section", "dp", "ctx"), None),
                P("section", ("dp", "ctx"), None),
                P("section", ("dp", "ctx"), None),
                P("section", ("dp", "ctx"), None),
            ),
            check_vma=False,
        )(*arrays)

    return run
```
